32 devices in a mesh: ctx: 16 (over z, y, core), tp: 2 (over x).
Axes of the slice: x: 2, y: 2, z: 4, core: 2. Of those that a mesh axis runs over, the one named last changes fastest.
Arguments:
- queries: bfloat16 [8192, 4096], P('ctx', 'tp'), may hold values from -0.19921875 to 0.19921875
- keys: bfloat16 [8192, 4096], P('ctx', 'tp'), may hold values from -0.19921875 to 0.19921875
- values: bfloat16 [8192, 4096], P('ctx', 'tp'), may hold values from -0.19921875 to 0.19921875
- cotangent: bfloat16 [8192, 2048], P('ctx', 'tp'), may hold values from -6 to 6
- out_weight: bfloat16 [4096, 2048], P('tp'), may hold values from -0.125 to 0.125
- memory: float32 [32, 128, 128], P('tp'), may hold values from -0.6 to 0.6
Outputs:
- query_grad: bfloat16 [8192, 4096], P('ctx', 'tp')
- key_grad: bfloat16 [8192, 4096], P('ctx', 'tp')
- value_grad: bfloat16 [8192, 4096], P('ctx', 'tp')
- weight_grad: float32 [4096, 2048], P(('tp', 'ctx'))
The draws below stay inside these ranges and needn't reach their ends.
All inputs are finite; a program needn't handle non-finite values.
Results may differ from the reference program's by a relative error of at most 0.0058.
Values may be sent and summed in bfloat16 or wider, within the bound.
No kernel may reach another device: no remote copies, remote signals or barrier semaphores. Data moves between devices by JAX's collectives and lax.ppermute only.
A program may use at most 320 MiB of HBM per device.

```python
import jax
import jax.numpy as jnp
from jax import lax

D = 2048
H = 32
E = 128
HD = 4096
TOK_DEV = 512
TOKENS = 8192


def levels(own_key, shape, pieces, least, top_value):
    loudness = 1.0
    for dim, shards_of in pieces:
        draws = jax.random.uniform(jax.random.fold_in(jax.random.fold_in(own_key, 6), dim), (shards_of,), jnp.float32, least / len(pieces), top_value / len(pieces))
        loudness = loudness * jnp.repeat(jnp.exp(draws), shape[dim] // shards_of).reshape((-1,) + (1,) * (len(shape) - 1 - dim))
    return loudness


def bell_draw(rng, dims, width, most, shards=(), kind=jnp.bfloat16):
    loudness = levels(rng, dims, shards, -0.22, 0.18) if shards else 1.0
    values = jax.random.normal(rng, dims, jnp.float32) * width * loudness
    return jnp.minimum(jnp.maximum(values, -most), most).astype(kind)


def setup_inputs(seed: int = 0) -> dict:
    splits = jax.random.split(jax.random.key(seed), 7)
    return {
        "queries": bell_draw(splits[0], (TOKENS, HD), 0.03, 0.19921875, ((0, 16), (1, 2))),
        "keys": bell_draw(splits[1], (TOKENS, HD), 0.03, 0.19921875, ((0, 16), (1, 2))),
        "values": bell_draw(splits[2], (TOKENS, HD), 0.03, 0.19921875, ((0, 16), (1, 2))),
        "cotangent": bell_draw(splits[3], (TOKENS, D), 1.0, 6.0, ((0, 16), (1, 2))),
        "out_weight": bell_draw(splits[4], (HD, D), D ** -0.5, 0.125, ((0, 2),)),
        "memory": bell_draw(splits[5], (H, E, E), 0.1, 0.6, ((0, 2),), jnp.float32),
    }


def reference(queries, keys, values, cotangent, out_weight, memory):
    tok_all, col_width = queries.shape
    heads = memory.shape[0]
    head_size = memory.shape[1]
    blocks = tok_all // TOK_DEV
    out_grad = jnp.dot(cotangent, out_weight.T, preferred_element_type=jnp.float32).astype(jnp.bfloat16)

    def split(array):
        return array.reshape(blocks, TOK_DEV, heads, head_size)

    query_b, key_b, value_b, grad_b = split(queries), split(keys), split(values), split(out_grad)
    kv_sum = jnp.einsum('cthe,cthf->chef', key_b.astype(jnp.float32), value_b.astype(jnp.float32))
    qd_sum = jnp.einsum('cthe,cthf->chef', query_b.astype(jnp.float32), grad_b.astype(jnp.float32))
    empty = jnp.zeros((1, heads, head_size, head_size), jnp.float32)
    before = jnp.concatenate([empty, jnp.cumsum(kv_sum, 0)[:-1]], 0)
    after = jnp.concatenate([jnp.cumsum(qd_sum[::-1], 0)[::-1][1:], empty], 0)
    state = (memory[None] + before).astype(jnp.bfloat16)
    adjoint = after.astype(jnp.bfloat16)
    causal = jnp.arange(TOK_DEV)[:, None] >= jnp.arange(TOK_DEV)[None, :]

    def one_block(parts):
        query, key, value, grad, state_c, adjoint_c = [p.astype(jnp.float32) for p in parts]
        scores = jnp.einsum('the,she->hts', query, key)
        scores = jnp.where(causal[None], scores, 0.0).astype(jnp.bfloat16).astype(jnp.float32)
        dscores = jnp.einsum('thf,shf->hts', grad, value)
        dscores = jnp.where(causal[None], dscores, 0.0).astype(jnp.bfloat16).astype(jnp.float32)
        attended = jnp.einsum('the,hef->thf', query, state_c) + jnp.einsum('hts,shf->thf', scores, value)
        query_g = jnp.einsum('thf,hef->the', grad, state_c) + jnp.einsum('hts,she->the', dscores, key)
        key_g = jnp.einsum('shf,hef->she', value, adjoint_c) + jnp.einsum('hts,the->she', dscores, query)
        value_g = jnp.einsum('she,hef->shf', key, adjoint_c) + jnp.einsum('hts,thf->shf', scores, grad)
        return (attended.astype(jnp.bfloat16), query_g.astype(jnp.bfloat16),
                key_g.astype(jnp.bfloat16), value_g.astype(jnp.bfloat16))

    attended, query_g, key_g, value_g = lax.map(one_block, (query_b, key_b, value_b, grad_b, state, adjoint))
    attended = attended.reshape(tok_all, col_width)
    weight_grad = jnp.dot(attended.T, cotangent, preferred_element_type=jnp.float32)
    return (query_g.reshape(tok_all, col_width), key_g.reshape(tok_all, col_width),
            value_g.reshape(tok_all, col_width), weight_grad)
```

```python
import functools

import jax
import jax.numpy as jnp
from jax import lax
from jax.experimental import pallas as pl
from jax.experimental.pallas import tpu as pltpu
from jax.sharding import PartitionSpec as P

BF = jnp.bfloat16
F32 = jnp.float32
VMEM_LIMIT = 56 * 1024 * 1024


def dot(a, b, ca, cb):
    return lax.dot_general(a, b, (((ca,), (cb,)), ((), ())), preferred_element_type=F32)


def params():
    return pltpu.CompilerParams(vmem_limit_bytes=VMEM_LIMIT)


def cost(flops, nbytes):
    return pl.CostEstimate(flops=int(flops), bytes_accessed=int(nbytes), transcendentals=0)


def kv_kernel(head, a_ref, b_ref, o_ref):
    for j in range(a_ref.shape[1] // head):
        at = slice(j * head, (j + 1) * head)
        o_ref[at, :] = dot(a_ref[:, at], b_ref[:, at], 0, 0).astype(o_ref.dtype)


def block_sums(a, b, head):
    tok, width = a.shape
    step = 2 * head
    return pl.pallas_call(
        functools.partial(kv_kernel, head),
        grid=(width // step,),
        in_specs=[pl.BlockSpec((tok, step), lambda i: (0, i))] * 2,
        out_specs=pl.BlockSpec((step, head), lambda i: (i, 0)),
        out_shape=jax.ShapeDtypeStruct((width, head), BF),
        compiler_params=params(),
        cost_estimate=cost(2 * tok * width * head, 4 * tok * width),
        name="block_sums",
    )(a, b)


def masked(tok, upper):
    row = lax.broadcasted_iota(jnp.int32, (tok, tok), 0)
    col = lax.broadcasted_iota(jnp.int32, (tok, tok), 1)
    return row <= col if upper else row >= col


def causal_apply(a, b, c, upper):
    tok = a.shape[0]
    half = tok // 2
    keep = masked(half, upper)

    def tile(x, y, diagonal):
        s = dot(x, y, 1, 1)
        if diagonal:
            s = jnp.where(keep, s, 0.0)
        return s.astype(BF)

    a0, a1, b0, b1, c0, c1 = a[:half], a[half:], b[:half], b[half:], c[:half], c[half:]
    first = dot(tile(a0, b0, True), c0, 1, 0)
    second = dot(tile(a1, b1, True), c1, 1, 0)
    if upper:
        first = first + dot(tile(a0, b1, False), c1, 1, 0)
    else:
        second = second + dot(tile(a1, b0, False), c0, 1, 0)
    return first, second


def intra_kernel(head, q_ref, k_ref, v_ref, o_ref):
    half = q_ref.shape[0] // 2
    for j in range(q_ref.shape[1] // head):
        at = slice(j * head, (j + 1) * head)
        first, second = causal_apply(q_ref[:, at], k_ref[:, at], v_ref[:, at], False)
        o_ref[:half, at] = first
        o_ref[half:, at] = second


def intra(q, k, v, head):
    tok, width = q.shape
    step = 2 * head
    spec = pl.BlockSpec((tok, step), lambda i: (0, i))
    return pl.pallas_call(
        functools.partial(intra_kernel, head),
        grid=(width // step,),
        in_specs=[spec] * 3,
        out_specs=spec,
        out_shape=jax.ShapeDtypeStruct((tok, width), F32),
        compiler_params=params(),
        cost_estimate=cost(4 * tok * tok * width, 10 * tok * width),
        name="intra",
    )(q, k, v)


def grad_kernel(head, tp_ref, own_ref, far_ref, wo_ref, wf_ref, q_ref, g_ref, s_ref):
    g = dot(own_ref[...], wo_ref[...], 1, 1) + dot(far_ref[...], wf_ref[...], 1, 1)
    g = g.astype(BF)
    g_ref[...] = g
    for j in range(g.shape[1] // head):
        at = slice(j * head, (j + 1) * head)
        s_ref[at, :] = dot(q_ref[:, at], g[:, at], 0, 0).astype(s_ref.dtype)


def out_grad_and_sums(tp, own, far, w, q, head):
    tok, feat = own.shape
    width = q.shape[1]
    step = 2 * head
    whole = pl.BlockSpec((tok, feat), lambda i, t: (0, 0))
    return pl.pallas_call(
        functools.partial(grad_kernel, head),
        grid_spec=pltpu.PrefetchScalarGridSpec(
            num_scalar_prefetch=1,
            grid=(width // step,),
            in_specs=[
                whole,
                whole,
                pl.BlockSpec((step, feat), lambda i, t: (i, t[0])),
                pl.BlockSpec((step, feat), lambda i, t: (i, 1 - t[0])),
                pl.BlockSpec((tok, step), lambda i, t: (0, i)),
            ],
            out_specs=[
                pl.BlockSpec((tok, step), lambda i, t: (0, i)),
                pl.BlockSpec((step, head), lambda i, t: (i, 0)),
            ],
        ),
        out_shape=[
            jax.ShapeDtypeStruct((tok, width), BF),
            jax.ShapeDtypeStruct((width, head), BF),
        ],
        compiler_params=params(),
        cost_estimate=cost(4 * tok * feat * width, 4 * feat * width + 4 * tok * width),
        name="out_grad",
    )(tp, own, far, w, w, q)


def attended_kernel(head, q_ref, s_ref, i_ref, o_ref):
    for j in range(q_ref.shape[1] // head):
        at = slice(j * head, (j + 1) * head)
        o_ref[:, at] = (dot(q_ref[:, at], s_ref[at, :], 1, 0) + i_ref[:, at]).astype(BF)


def attended_of(q, state, inner, head):
    tok, width = q.shape
    step = 2 * head
    spec = pl.BlockSpec((tok, step), lambda i: (0, i))
    return pl.pallas_call(
        functools.partial(attended_kernel, head),
        grid=(width // step,),
        in_specs=[spec, pl.BlockSpec((step, head), lambda i: (i, 0)), spec],
        out_specs=spec,
        out_shape=jax.ShapeDtypeStruct((tok, width), BF),
        compiler_params=params(),
        cost_estimate=cost(2 * tok * head * width, 8 * tok * width),
        name="attended",
    )(q, state, inner)


def weight_kernel(a_ref, own_ref, far_ref, o_ref):
    feat = own_ref.shape[1]
    a = a_ref[...]
    o_ref[:, :feat] = dot(a, own_ref[...], 0, 0).astype(o_ref.dtype)
    o_ref[:, feat:] = dot(a, far_ref[...], 0, 0).astype(o_ref.dtype)


def weight_term(a, own, far):
    tok, width = a.shape
    feat = own.shape[1]
    step = 256
    whole = pl.BlockSpec((tok, feat), lambda i: (0, 0))
    return pl.pallas_call(
        weight_kernel,
        grid=(width // step,),
        in_specs=[pl.BlockSpec((tok, step), lambda i: (0, i)), whole, whole],
        out_specs=pl.BlockSpec((step, 2 * feat), lambda i: (i, 0)),
        out_shape=jax.ShapeDtypeStruct((width, 2 * feat), BF),
        compiler_params=params(),
        cost_estimate=cost(4 * tok * feat * width, 4 * feat * width + 2 * tok * width),
        name="weight_term",
    )(a, own, far)


def query_kernel(head, g_ref, v_ref, k_ref, s_ref, o_ref):
    half = g_ref.shape[0] // 2
    for j in range(g_ref.shape[1] // head):
        at = slice(j * head, (j + 1) * head)
        g = g_ref[:, at]
        first, second = causal_apply(g, v_ref[:, at], k_ref[:, at], False)
        carried = dot(g, s_ref[at, :], 1, 1)
        o_ref[:half, at] = (first + carried[:half]).astype(BF)
        o_ref[half:, at] = (second + carried[half:]).astype(BF)


def query_grad_of(g, v, k, state, head):
    tok, width = g.shape
    step = 2 * head
    spec = pl.BlockSpec((tok, step), lambda i: (0, i))
    return pl.pallas_call(
        functools.partial(query_kernel, head),
        grid=(width // step,),
        in_specs=[spec, spec, spec, pl.BlockSpec((step, head), lambda i: (i, 0))],
        out_specs=spec,
        out_shape=jax.ShapeDtypeStruct((tok, width), BF),
        compiler_params=params(),
        cost_estimate=cost(4 * tok * tok * width, 8 * tok * width),
        name="query_grad",
    )(g, v, k, state)


def key_value_kernel(head, q_ref, k_ref, v_ref, g_ref, a_ref, ko_ref, vo_ref):
    half = g_ref.shape[0] // 2
    for j in range(g_ref.shape[1] // head):
        at = slice(j * head, (j + 1) * head)
        q, k, v, g, adj = q_ref[:, at], k_ref[:, at], v_ref[:, at], g_ref[:, at], a_ref[at, :]
        first, second = causal_apply(v, g, q, True)
        carried = dot(v, adj, 1, 1)
        ko_ref[:half, at] = (first + carried[:half]).astype(BF)
        ko_ref[half:, at] = (second + carried[half:]).astype(BF)
        first, second = causal_apply(k, q, g, True)
        carried = dot(k, adj, 1, 0)
        vo_ref[:half, at] = (first + carried[:half]).astype(BF)
        vo_ref[half:, at] = (second + carried[half:]).astype(BF)


def key_value_grad_of(q, k, v, g, adjoint, head):
    tok, width = g.shape
    step = 2 * head
    spec = pl.BlockSpec((tok, step), lambda i: (0, i))
    shape = jax.ShapeDtypeStruct((tok, width), BF)
    return pl.pallas_call(
        functools.partial(key_value_kernel, head),
        grid=(width // step,),
        in_specs=[spec, spec, spec, spec, pl.BlockSpec((step, head), lambda i: (i, 0))],
        out_specs=[spec, spec],
        out_shape=[shape, shape],
        compiler_params=params(),
        cost_estimate=cost(8 * tok * tok * width, 12 * tok * width),
        name="key_value_grad",
    )(q, k, v, g, adjoint)


def scan_kernel(n, reverse, x_ref, start_ref, o_ref):
    rows = start_ref.shape[0]
    total = start_ref[...]
    for i in range(n):
        c = n - 1 - i if reverse else i
        at = slice(c * rows, (c + 1) * rows)
        o_ref[at, :] = total.astype(BF)
        total = total + x_ref[at, :].astype(F32)


def scan_blocks(x, start, n, reverse):
    return pl.pallas_call(
        functools.partial(scan_kernel, n, reverse),
        out_shape=jax.ShapeDtypeStruct(x.shape, BF),
        compiler_params=params(),
        cost_estimate=cost(x.size, 4 * x.size),
        name="scan_blocks",
    )(x, start)


def carried(x, start, axis, reverse):
    n = lax.axis_size(axis)
    mine = lax.all_to_all(x, axis, 0, 0, tiled=True)
    return lax.all_to_all(scan_blocks(mine, start, n, reverse), axis, 0, 0, tiled=True)


def local(queries, keys, values, cotangent, out_weight, memory):
    head = memory.shape[2]
    width = queries.shape[1]
    feat = cotangent.shape[1]
    n = lax.axis_size("ctx")
    rows = width // n
    me, tp = lax.axis_index("ctx"), lax.axis_index("tp")

    far = lax.ppermute(cotangent, "tp", [(0, 1), (1, 0)])
    kv = block_sums(keys, values, head)
    start = lax.dynamic_slice_in_dim(memory.reshape(width, head), me * rows, rows, 0)
    state = carried(kv, start, "ctx", False)
    inner = intra(queries, keys, values, head)
    grad, qd = out_grad_and_sums(tp.reshape(1), cotangent, far, out_weight, queries, head)
    adjoint = carried(qd, jnp.zeros_like(start), "ctx", True)
    attended = attended_of(queries, state, inner, head)
    term = weight_term(attended, cotangent, far)
    total = lax.psum_scatter(term, "ctx", scatter_dimension=0, tiled=True)
    query_g = query_grad_of(grad, values, keys, state, head)
    key_g, value_g = key_value_grad_of(queries, keys, values, grad, adjoint, head)
    total = total.astype(F32)
    total = jnp.where(tp == 0, total, jnp.concatenate([total[:, feat:], total[:, :feat]], 1))
    return query_g, key_g, value_g, total


def solution(mesh):
    in_specs = (
        P("ctx", "tp"),
        P("ctx", "tp"),
        P("ctx", "tp"),
        P("ctx", "tp"),
        P("tp", None),
        P("tp", None, None),
    )
    out_specs = (P("ctx", "tp"), P("ctx", "tp"), P("ctx", "tp"), P(("tp", "ctx"), None))
    return jax.shard_map(local, mesh=mesh, in_specs=in_specs, out_specs=out_specs, check_vma=False)
```

```python
import functools

import jax
import jax.numpy as jnp
from jax import lax
from jax.experimental import pallas as pl
from jax.experimental.pallas import tpu as pltpu
from jax.sharding import PartitionSpec as P

BF = jnp.bfloat16
F32 = jnp.float32
VMEM_LIMIT = 56 * 1024 * 1024


def dot(a, b, ca, cb):
    return lax.dot_general(a, b, (((ca,), (cb,)), ((), ())), preferred_element_type=F32)


def params():
    return pltpu.CompilerParams(vmem_limit_bytes=VMEM_LIMIT)


def cost(flops, nbytes):
    return pl.CostEstimate(flops=int(flops), bytes_accessed=int(nbytes), transcendentals=0)


def kv_kernel(head, a_ref, b_ref, o_ref):
    for j in range(a_ref.shape[1] // head):
        at = slice(j * head, (j + 1) * head)
        o_ref[at, :] = dot(a_ref[:, at], b_ref[:, at], 0, 0).astype(o_ref.dtype)


def block_sums(a, b, head):
    tok, width = a.shape
    step = 2 * head
    return pl.pallas_call(
        functools.partial(kv_kernel, head),
        grid=(width // step,),
        in_specs=[pl.BlockSpec((tok, step), lambda i: (0, i))] * 2,
        out_specs=pl.BlockSpec((step, head), lambda i: (i, 0)),
        out_shape=jax.ShapeDtypeStruct((width, head), BF),
        compiler_params=params(),
        cost_estimate=cost(2 * tok * width * head, 4 * tok * width),
        name="block_sums",
    )(a, b)


def masked(tok, upper):
    row = lax.broadcasted_iota(jnp.int32, (tok, tok), 0)
    col = lax.broadcasted_iota(jnp.int32, (tok, tok), 1)
    return row <= col if upper else row >= col


def causal_apply(a, b, c, upper):
    tok = a.shape[0]
    half = tok // 2
    keep = masked(half, upper)

    def tile(x, y, diagonal):
        s = dot(x, y, 1, 1)
        if diagonal:
            s = jnp.where(keep, s, 0.0)
        return s.astype(BF)

    a0, a1, b0, b1, c0, c1 = a[:half], a[half:], b[:half], b[half:], c[:half], c[half:]
    first = dot(tile(a0, b0, True), c0, 1, 0)
    second = dot(tile(a1, b1, True), c1, 1, 0)
    if upper:
        first = first + dot(tile(a0, b1, False), c1, 1, 0)
    else:
        second = second + dot(tile(a1, b0, False), c0, 1, 0)
    return first, second


def intra_kernel(head, q_ref, k_ref, v_ref, o_ref):
    half = q_ref.shape[0] // 2
    for j in range(q_ref.shape[1] // head):
        at = slice(j * head, (j + 1) * head)
        first, second = causal_apply(q_ref[:, at], k_ref[:, at], v_ref[:, at], False)
        o_ref[:half, at] = first
        o_ref[half:, at] = second


def intra(q, k, v, head):
    tok, width = q.shape
    step = 2 * head
    spec = pl.BlockSpec((tok, step), lambda i: (0, i))
    return pl.pallas_call(
        functools.partial(intra_kernel, head),
        grid=(width // step,),
        in_specs=[spec] * 3,
        out_specs=spec,
        out_shape=jax.ShapeDtypeStruct((tok, width), F32),
        compiler_params=params(),
        cost_estimate=cost(4 * tok * tok * width, 10 * tok * width),
        name="intra",
    )(q, k, v)


def grad_kernel(head, tp_ref, own_ref, far_ref, wo_ref, wf_ref, q_ref, g_ref, s_ref):
    g = dot(own_ref[...], wo_ref[...], 1, 1) + dot(far_ref[...], wf_ref[...], 1, 1)
    g = g.astype(BF)
    g_ref[...] = g
    for j in range(g.shape[1] // head):
        at = slice(j * head, (j + 1) * head)
        s_ref[at, :] = dot(q_ref[:, at], g[:, at], 0, 0).astype(s_ref.dtype)


def out_grad_and_sums(tp, own, far, w, q, head):
    tok, feat = own.shape
    width = q.shape[1]
    step = 2 * head
    whole = pl.BlockSpec((tok, feat), lambda i, t: (0, 0))
    return pl.pallas_call(
        functools.partial(grad_kernel, head),
        grid_spec=pltpu.PrefetchScalarGridSpec(
            num_scalar_prefetch=1,
            grid=(width // step,),
            in_specs=[
                whole,
                whole,
                pl.BlockSpec((step, feat), lambda i, t: (i, t[0])),
                pl.BlockSpec((step, feat), lambda i, t: (i, 1 - t[0])),
                pl.BlockSpec((tok, step), lambda i, t: (0, i)),
            ],
            out_specs=[
                pl.BlockSpec((tok, step), lambda i, t: (0, i)),
                pl.BlockSpec((step, head), lambda i, t: (i, 0)),
            ],
        ),
        out_shape=[
            jax.ShapeDtypeStruct((tok, width), BF),
            jax.ShapeDtypeStruct((width, head), BF),
        ],
        compiler_params=params(),
        cost_estimate=cost(4 * tok * feat * width, 4 * feat * width + 4 * tok * width),
        name="out_grad",
    )(tp, own, far, w, w, q)


def attended_kernel(head, q_ref, s_ref, i_ref, o_ref):
    for j in range(q_ref.shape[1] // head):
        at = slice(j * head, (j + 1) * head)
        o_ref[:, at] = (dot(q_ref[:, at], s_ref[at, :], 1, 0) + i_ref[:, at]).astype(BF)


def attended_of(q, state, inner, head):
    tok, width = q.shape
    step = 2 * head
    spec = pl.BlockSpec((tok, step), lambda i: (0, i))
    return pl.pallas_call(
        functools.partial(attended_kernel, head),
        grid=(width // step,),
        in_specs=[spec, pl.BlockSpec((step, head), lambda i: (i, 0)), spec],
        out_specs=spec,
        out_shape=jax.ShapeDtypeStruct((tok, width), BF),
        compiler_params=params(),
        cost_estimate=cost(2 * tok * head * width, 8 * tok * width),
        name="attended",
    )(q, state, inner)


def weight_kernel(a_ref, own_ref, far_ref, o_ref):
    feat = own_ref.shape[1]
    a = a_ref[...]
    o_ref[:, :feat] = dot(a, own_ref[...], 0, 0).astype(o_ref.dtype)
    o_ref[:, feat:] = dot(a, far_ref[...], 0, 0).astype(o_ref.dtype)


def weight_term(a, own, far):
    tok, width = a.shape
    feat = own.shape[1]
    step = 256
    whole = pl.BlockSpec((tok, feat), lambda i: (0, 0))
    return pl.pallas_call(
        weight_kernel,
        grid=(width // step,),
        in_specs=[pl.BlockSpec((tok, step), lambda i: (0, i)), whole, whole],
        out_specs=pl.BlockSpec((step, 2 * feat), lambda i: (i, 0)),
        out_shape=jax.ShapeDtypeStruct((width, 2 * feat), BF),
        compiler_params=params(),
        cost_estimate=cost(4 * tok * feat * width, 4 * feat * width + 2 * tok * width),
        name="weight_term",
    )(a, own, far)


def query_kernel(head, g_ref, v_ref, k_ref, s_ref, o_ref):
    half = g_ref.shape[0] // 2
    for j in range(g_ref.shape[1] // head):
        at = slice(j * head, (j + 1) * head)
        g = g_ref[:, at]
        first, second = causal_apply(g, v_ref[:, at], k_ref[:, at], False)
        carried = dot(g, s_ref[at, :], 1, 1)
        o_ref[:half, at] = (first + carried[:half]).astype(BF)
        o_ref[half:, at] = (second + carried[half:]).astype(BF)


def query_grad_of(g, v, k, state, head):
    tok, width = g.shape
    step = 2 * head
    spec = pl.BlockSpec((tok, step), lambda i: (0, i))
    return pl.pallas_call(
        functools.partial(query_kernel, head),
        grid=(width // step,),
        in_specs=[spec, spec, spec, pl.BlockSpec((step, head), lambda i: (i, 0))],
        out_specs=spec,
        out_shape=jax.ShapeDtypeStruct((tok, width), BF),
        compiler_params=params(),
        cost_estimate=cost(4 * tok * tok * width, 8 * tok * width),
        name="query_grad",
    )(g, v, k, state)


def key_value_kernel(head, q_ref, k_ref, v_ref, g_ref, a_ref, ko_ref, vo_ref):
    half = g_ref.shape[0] // 2
    for j in range(g_ref.shape[1] // head):
        at = slice(j * head, (j + 1) * head)
        q, k, v, g, adj = q_ref[:, at], k_ref[:, at], v_ref[:, at], g_ref[:, at], a_ref[at, :]
        first, second = causal_apply(v, g, q, True)
        carried = dot(v, adj, 1, 1)
        ko_ref[:half, at] = (first + carried[:half]).astype(BF)
        ko_ref[half:, at] = (second + carried[half:]).astype(BF)
        first, second = causal_apply(k, q, g, True)
        carried = dot(k, adj, 1, 0)
        vo_ref[:half, at] = (first + carried[:half]).astype(BF)
        vo_ref[half:, at] = (second + carried[half:]).astype(BF)


def key_value_grad_of(q, k, v, g, adjoint, head):
    tok, width = g.shape
    step = 2 * head
    spec = pl.BlockSpec((tok, step), lambda i: (0, i))
    shape = jax.ShapeDtypeStruct((tok, width), BF)
    return pl.pallas_call(
        functools.partial(key_value_kernel, head),
        grid=(width // step,),
        in_specs=[spec, spec, spec, spec, pl.BlockSpec((step, head), lambda i: (i, 0))],
        out_specs=[spec, spec],
        out_shape=[shape, shape],
        compiler_params=params(),
        cost_estimate=cost(8 * tok * tok * width, 12 * tok * width),
        name="key_value_grad",
    )(q, k, v, g, adjoint)


def scan_kernel(n, reverse, x_ref, start_ref, o_ref):
    rows = start_ref.shape[0]
    total = start_ref[...]
    for i in range(n):
        c = n - 1 - i if reverse else i
        at = slice(c * rows, (c + 1) * rows)
        o_ref[at, :] = total.astype(BF)
        total = total + x_ref[at, :].astype(F32)


def scan_blocks(x, start, n, reverse):
    return pl.pallas_call(
        functools.partial(scan_kernel, n, reverse),
        out_shape=jax.ShapeDtypeStruct(x.shape, BF),
        compiler_params=params(),
        cost_estimate=cost(x.size, 4 * x.size),
        name="scan_blocks",
    )(x, start)


def carried(x, start, axis, reverse):
    n = lax.axis_size(axis)
    mine = lax.all_to_all(x, axis, 0, 0, tiled=True)
    return lax.all_to_all(scan_blocks(mine, start, n, reverse), axis, 0, 0, tiled=True)


def pair_sums_kernel(head, me_ref, a_ref, b_ref, mine_ref, send_ref):
    even = dot(a_ref[:, :head], b_ref[:, :head], 0, 0)
    odd = dot(a_ref[:, head:], b_ref[:, head:], 0, 0)
    first = me_ref[0] % 2 == 0
    mine_ref[...] = jnp.where(first, even, odd).astype(BF)
    send_ref[...] = jnp.where(first, odd, even).astype(BF)


def pair_sums(me, a, b, head):
    tok, width = a.shape
    spec = pl.BlockSpec((tok, 2 * head), lambda i, m: (0, i))
    out = pl.BlockSpec((head, head), lambda i, m: (i, 0))
    shape = jax.ShapeDtypeStruct((width // 2, head), BF)
    return pl.pallas_call(
        functools.partial(pair_sums_kernel, head),
        grid_spec=pltpu.PrefetchScalarGridSpec(
            num_scalar_prefetch=1,
            grid=(width // (2 * head),),
            in_specs=[spec] * 2,
            out_specs=[out] * 2,
        ),
        out_shape=[shape] * 2,
        compiler_params=params(),
        cost_estimate=cost(2 * tok * width * head, 4 * tok * width),
        name="pair_sums",
    )(me, a, b)


def pair_intra_kernel(head, me_ref, q_ref, k_ref, v_ref, mine_ref, send_ref):
    first = me_ref[0] % 2 == 0
    half = q_ref.shape[0] // 2
    even, odd = slice(0, head), slice(head, 2 * head)
    parts = [causal_apply(q_ref[:, at], k_ref[:, at], v_ref[:, at], False) for at in (even, odd)]
    for k, at in enumerate((slice(0, half), slice(half, 2 * half))):
        mine_ref[at, :] = jnp.where(first, parts[0][k], parts[1][k]).astype(BF)
        send_ref[at, odd] = jnp.where(first, parts[1][k], parts[0][k]).astype(BF)
    send_ref[:, even] = jnp.where(first, q_ref[:, odd], q_ref[:, even])


def pair_intra(me, q, k, v, head):
    tok, width = q.shape
    spec = pl.BlockSpec((tok, 2 * head), lambda i, m: (0, i))
    return pl.pallas_call(
        functools.partial(pair_intra_kernel, head),
        grid_spec=pltpu.PrefetchScalarGridSpec(
            num_scalar_prefetch=1,
            grid=(width // (2 * head),),
            in_specs=[spec] * 3,
            out_specs=[pl.BlockSpec((tok, head), lambda i, m: (0, i)), spec],
        ),
        out_shape=[
            jax.ShapeDtypeStruct((tok, width // 2), BF),
            jax.ShapeDtypeStruct((tok, width), BF),
        ],
        compiler_params=params(),
        cost_estimate=cost(4 * tok * tok * width, 9 * tok * width),
        name="pair_intra",
    )(me, q, k, v)


def pair_attended_kernel(head, me_ref, q0_ref, q1_ref, i_ref, far_ref, s_ref, own_ref, oth_ref,
                         mine_ref, send_ref, so_ref, sf_ref):
    core = (me_ref[0] % 2).astype(F32)
    south = (me_ref[0] // 2) % 2 == 0
    state = s_ref[...].astype(F32)
    near = (state + core * oth_ref[...].astype(F32)).astype(BF)
    away = (state + (1.0 - core) * own_ref[...].astype(F32)).astype(BF)
    so_ref[...] = near
    sf_ref[...] = away
    results = []
    for j, q_ref in enumerate((q0_ref, q1_ref)):
        at = slice(j * head, (j + 1) * head)
        here = dot(q_ref[...], near[at], 1, 0) + i_ref[:, at].astype(F32)
        base = 2 * j * head
        q_far = far_ref[:, base : base + head]
        there = dot(q_far, away[at], 1, 0) + far_ref[:, base + head : base + 2 * head].astype(F32)
        results.append((here, there))
    for k in range(2):
        mine_ref[k] = jnp.where(south, results[0][k], results[1][k]).astype(BF)
        send_ref[k] = jnp.where(south, results[1][k], results[0][k]).astype(BF)


def pair_attended(me, q, inner, far, state, own, oth, head):
    tok, width = q.shape
    steps = width // (4 * head)
    rows = pl.BlockSpec((2 * head, head), lambda i, m: (i, 0))
    out = pl.BlockSpec((2, tok, head), lambda i, m: (0, 0, i))
    return pl.pallas_call(
        functools.partial(pair_attended_kernel, head),
        grid_spec=pltpu.PrefetchScalarGridSpec(
            num_scalar_prefetch=1,
            grid=(steps,),
            in_specs=[
                pl.BlockSpec((tok, head), lambda i, m: (0, 4 * i + m[0] % 2)),
                pl.BlockSpec((tok, head), lambda i, m: (0, 4 * i + 2 + m[0] % 2)),
                pl.BlockSpec((tok, 2 * head), lambda i, m: (0, i)),
                pl.BlockSpec((tok, 4 * head), lambda i, m: (0, i)),
                rows,
                rows,
                rows,
            ],
            out_specs=[out, out, rows, rows],
        ),
        out_shape=[
            jax.ShapeDtypeStruct((2, tok, width // 4), BF),
            jax.ShapeDtypeStruct((2, tok, width // 4), BF),
            jax.ShapeDtypeStruct((width // 2, head), BF),
            jax.ShapeDtypeStruct((width // 2, head), BF),
        ],
        compiler_params=params(),
        cost_estimate=cost(2 * tok * head * width, 8 * tok * width),
        name="pair_attended",
    )(me, q, q, inner, far, state, own, oth)


def quad_weight_kernel(a_ref, b_ref, *refs):
    ins, (o_ref, at_ref) = refs[:8], refs[8:]
    tok = a_ref.shape[1]

    @pl.when(pl.program_id(0) == 0)
    def _():
        for k in range(4):
            block = (a_ref if k < 2 else b_ref)[k % 2]
            at_ref[:, k * tok : (k + 1) * tok] = block.T

    for part in range(2):
        total = None
        for k in range(4):
            term = dot(at_ref[:, k * tok : (k + 1) * tok], ins[2 * k + part][...], 1, 0)
            total = term if total is None else total + term
        o_ref[part] = total.astype(BF)


def quad_weight(a, b, cots):
    _, tok, cols = a.shape
    feat = cots[0].shape[1]
    step = min(256, feat)
    whole = pl.BlockSpec(a.shape, lambda i: (0, 0, 0))
    return pl.pallas_call(
        quad_weight_kernel,
        grid=(feat // step,),
        in_specs=[whole, whole] + [pl.BlockSpec((tok, step), lambda i: (0, i))] * 8,
        out_specs=pl.BlockSpec((2, cols, step), lambda i: (0, 0, i)),
        out_shape=jax.ShapeDtypeStruct((2, cols, feat), BF),
        scratch_shapes=[pltpu.VMEM((cols, 4 * tok), BF)],
        compiler_params=params(),
        cost_estimate=cost(16 * tok * feat * cols, 20 * feat * tok),
        name="quad_weight",
    )(a, b, *cots)


def pair_query_kernel(head, me_ref, g_ref, v_ref, k_ref, s_ref, t_ref, o_ref):
    first = me_ref[0] % 2 == 0
    half = g_ref.shape[0] // 2
    for j in range(2):
        at = slice(j * head, (j + 1) * head)
        g = g_ref[:, at]
        state = jnp.where(first == (j == 0), s_ref[...], t_ref[...])
        first_half, second_half = causal_apply(g, v_ref[:, at], k_ref[:, at], False)
        over = dot(g, state, 1, 1)
        o_ref[:half, at] = (first_half + over[:half]).astype(BF)
        o_ref[half:, at] = (second_half + over[half:]).astype(BF)


def pair_query_grad(me, g, v, k, mine, other, head):
    tok, width = g.shape
    spec = pl.BlockSpec((tok, 2 * head), lambda i, m: (0, i))
    rows = pl.BlockSpec((head, head), lambda i, m: (i, 0))
    return pl.pallas_call(
        functools.partial(pair_query_kernel, head),
        grid_spec=pltpu.PrefetchScalarGridSpec(
            num_scalar_prefetch=1,
            grid=(width // (2 * head),),
            in_specs=[spec, spec, spec, rows, rows],
            out_specs=spec,
        ),
        out_shape=jax.ShapeDtypeStruct((tok, width), BF),
        compiler_params=params(),
        cost_estimate=cost(4 * tok * tok * width, 8 * tok * width),
        name="query_grad",
    )(me, g, v, k, mine, other)


def line_reduce(term, line, n):
    places = n // 4
    right = left = None
    for r in range(1, places):
        to_right = lax.dynamic_index_in_dim(term, jnp.minimum(line + places - r, places - 1), 1, False)
        to_left = lax.dynamic_index_in_dim(term, jnp.maximum(line - places + r, 0), 1, False)
        if right is not None:
            to_right = (to_right.astype(F32) + right.astype(F32)).astype(BF)
            to_left = (to_left.astype(F32) + left.astype(F32)).astype(BF)
        right = lax.ppermute(to_right, "ctx", [(c, c + 4) for c in range(n) if c // 4 < r])
        left = lax.ppermute(to_left, "ctx", [(c, c - 4) for c in range(n) if c // 4 >= places - r])
    total = lax.dynamic_index_in_dim(term, line, 1, False).astype(F32)
    if right is not None:
        total = total + right.astype(F32) + left.astype(F32)
    return total


def local_paired(queries, keys, values, cotangent, out_weight, memory):
    head = memory.shape[2]
    tok, width = queries.shape
    n = lax.axis_size("ctx")
    me, tp = lax.axis_index("ctx"), lax.axis_index("tp")
    who = me.reshape(1)

    def swap(x, bit):
        return lax.ppermute(x, "ctx", [(c, c ^ bit) for c in range(n)])

    def swap_tp(x):
        return lax.ppermute(x, "tp", [(0, 1), (1, 0)])

    kv_mine, kv_send = pair_sums(who, keys, values, head)
    kv_other = swap(kv_send, 1)
    groups = [[c for c in range(n) if c % 2 == core] for core in range(2)]
    chip = (kv_mine.astype(F32) + kv_other.astype(F32)).astype(BF)
    chip = lax.all_to_all(chip, "ctx", 0, 0, axis_index_groups=groups, tiled=True)
    start = lax.dynamic_index_in_dim(memory, me, 0, False)
    chip = scan_blocks(chip, start, n // 2, False)
    state = lax.all_to_all(chip, "ctx", 0, 0, axis_index_groups=groups, tiled=True)

    far = swap_tp(cotangent)
    south = swap(cotangent, 2)
    far_south = swap_tp(south)
    cots = [cotangent, far, swap(cotangent, 1), swap(far, 1)]
    cots += [south, far_south, swap(south, 1), swap(far_south, 1)]

    inner, sent = pair_intra(who, queries, keys, values, head)
    got = swap(sent, 1)
    grad, qd = out_grad_and_sums(tp.reshape(1), cotangent, far, out_weight, queries, head)

    mine, send, state_mine, state_send = pair_attended(
        who, queries, inner, got, state, kv_mine, kv_other, head
    )
    received = swap(send, 2)
    state_other = swap(state_send, 1)
    adjoint = carried(qd, jnp.zeros_like(start), "ctx", True)
    term = quad_weight(mine, received, cots)
    feat = cotangent.shape[1]
    total = line_reduce(term.reshape(2, n // 4, head, feat), me // 4, n)
    query_g = pair_query_grad(who, grad, values, keys, state_mine, state_other, head)
    key_g, value_g = key_value_grad_of(queries, keys, values, grad, adjoint, head)
    first, second = jnp.where(tp == 0, total[0], total[1]), jnp.where(tp == 0, total[1], total[0])
    return query_g, key_g, value_g, jnp.concatenate([first, second], 1)


def local_any(queries, keys, values, cotangent, out_weight, memory):
    head = memory.shape[2]
    width = queries.shape[1]
    feat = cotangent.shape[1]
    n = lax.axis_size("ctx")
    rows = width // n
    me, tp = lax.axis_index("ctx"), lax.axis_index("tp")

    far = lax.ppermute(cotangent, "tp", [(0, 1), (1, 0)])
    kv = block_sums(keys, values, head)
    start = lax.dynamic_slice_in_dim(memory.reshape(width, head), me * rows, rows, 0)
    state = carried(kv, start, "ctx", False)
    inner = intra(queries, keys, values, head)
    grad, qd = out_grad_and_sums(tp.reshape(1), cotangent, far, out_weight, queries, head)
    adjoint = carried(qd, jnp.zeros_like(start), "ctx", True)
    attended = attended_of(queries, state, inner, head)
    term = weight_term(attended, cotangent, far)
    total = lax.psum_scatter(term, "ctx", scatter_dimension=0, tiled=True)
    query_g = query_grad_of(grad, values, keys, state, head)
    key_g, value_g = key_value_grad_of(queries, keys, values, grad, adjoint, head)
    total = total.astype(F32)
    total = jnp.where(tp == 0, total, jnp.concatenate([total[:, feat:], total[:, :feat]], 1))
    return query_g, key_g, value_g, total


def local(*args):
    heads = args[5].shape[0]
    n = lax.axis_size("ctx")
    if n == heads and n % 4 == 0 and lax.axis_size("tp") == 2:
        return local_paired(*args)
    return local_any(*args)


def solution(mesh):
    in_specs = (
        P("ctx", "tp"),
        P("ctx", "tp"),
        P("ctx", "tp"),
        P("ctx", "tp"),
        P("tp", None),
        P("tp", None, None),
    )
    out_specs = (P("ctx", "tp"), P("ctx", "tp"), P("ctx", "tp"), P(("tp", "ctx"), None))
    return jax.shard_map(local, mesh=mesh, in_specs=in_specs, out_specs=out_specs, check_vma=False)
```

```python
import functools

import jax
import jax.numpy as jnp
from jax import lax
from jax.experimental import pallas as pl
from jax.experimental.pallas import tpu as pltpu
from jax.sharding import PartitionSpec as P

BF = jnp.bfloat16
F32 = jnp.float32
VMEM_LIMIT = 56 * 1024 * 1024


def dot(a, b, ca, cb):
    return lax.dot_general(a, b, (((ca,), (cb,)), ((), ())), preferred_element_type=F32)


def params():
    return pltpu.CompilerParams(vmem_limit_bytes=VMEM_LIMIT)


def cost(flops, nbytes):
    return pl.CostEstimate(flops=int(flops), bytes_accessed=int(nbytes), transcendentals=0)


def kv_kernel(head, a_ref, b_ref, o_ref):
    for j in range(a_ref.shape[1] // head):
        at = slice(j * head, (j + 1) * head)
        o_ref[at, :] = dot(a_ref[:, at], b_ref[:, at], 0, 0).astype(o_ref.dtype)


def block_sums(a, b, head):
    tok, width = a.shape
    step = 2 * head
    return pl.pallas_call(
        functools.partial(kv_kernel, head),
        grid=(width // step,),
        in_specs=[pl.BlockSpec((tok, step), lambda i: (0, i))] * 2,
        out_specs=pl.BlockSpec((step, head), lambda i: (i, 0)),
        out_shape=jax.ShapeDtypeStruct((width, head), BF),
        compiler_params=params(),
        cost_estimate=cost(2 * tok * width * head, 4 * tok * width),
        name="block_sums",
    )(a, b)


def masked(tok, upper):
    row = lax.broadcasted_iota(jnp.int32, (tok, tok), 0)
    col = lax.broadcasted_iota(jnp.int32, (tok, tok), 1)
    return row <= col if upper else row >= col


def causal_apply(a, b, c, upper):
    tok = a.shape[0]
    half = tok // 2
    keep = masked(half, upper)

    def tile(x, y, diagonal):
        s = dot(x, y, 1, 1)
        if diagonal:
            s = jnp.where(keep, s, 0.0)
        return s.astype(BF)

    a0, a1, b0, b1, c0, c1 = a[:half], a[half:], b[:half], b[half:], c[:half], c[half:]
    first = dot(tile(a0, b0, True), c0, 1, 0)
    second = dot(tile(a1, b1, True), c1, 1, 0)
    if upper:
        first = first + dot(tile(a0, b1, False), c1, 1, 0)
    else:
        second = second + dot(tile(a1, b0, False), c0, 1, 0)
    return first, second


def intra_kernel(head, q_ref, k_ref, v_ref, o_ref):
    half = q_ref.shape[0] // 2
    for j in range(q_ref.shape[1] // head):
        at = slice(j * head, (j + 1) * head)
        first, second = causal_apply(q_ref[:, at], k_ref[:, at], v_ref[:, at], False)
        o_ref[:half, at] = first
        o_ref[half:, at] = second


def intra(q, k, v, head):
    tok, width = q.shape
    step = 2 * head
    spec = pl.BlockSpec((tok, step), lambda i: (0, i))
    return pl.pallas_call(
        functools.partial(intra_kernel, head),
        grid=(width // step,),
        in_specs=[spec] * 3,
        out_specs=spec,
        out_shape=jax.ShapeDtypeStruct((tok, width), F32),
        compiler_params=params(),
        cost_estimate=cost(4 * tok * tok * width, 10 * tok * width),
        name="intra",
    )(q, k, v)


def grad_kernel(head, tp_ref, own_ref, far_ref, wo_ref, wf_ref, q_ref, g_ref, s_ref):
    g = dot(own_ref[...], wo_ref[...], 1, 1) + dot(far_ref[...], wf_ref[...], 1, 1)
    g = g.astype(BF)
    g_ref[...] = g
    for j in range(g.shape[1] // head):
        at = slice(j * head, (j + 1) * head)
        s_ref[at, :] = dot(q_ref[:, at], g[:, at], 0, 0).astype(s_ref.dtype)


def out_grad_and_sums(tp, own, far, w, q, head):
    tok, feat = own.shape
    width = q.shape[1]
    step = 2 * head
    whole = pl.BlockSpec((tok, feat), lambda i, t: (0, 0))
    return pl.pallas_call(
        functools.partial(grad_kernel, head),
        grid_spec=pltpu.PrefetchScalarGridSpec(
            num_scalar_prefetch=1,
            grid=(width // step,),
            in_specs=[
                whole,
                whole,
                pl.BlockSpec((step, feat), lambda i, t: (i, t[0])),
                pl.BlockSpec((step, feat), lambda i, t: (i, 1 - t[0])),
                pl.BlockSpec((tok, step), lambda i, t: (0, i)),
            ],
            out_specs=[
                pl.BlockSpec((tok, step), lambda i, t: (0, i)),
                pl.BlockSpec((step, head), lambda i, t: (i, 0)),
            ],
        ),
        out_shape=[
            jax.ShapeDtypeStruct((tok, width), BF),
            jax.ShapeDtypeStruct((width, head), BF),
        ],
        compiler_params=params(),
        cost_estimate=cost(4 * tok * feat * width, 4 * feat * width + 4 * tok * width),
        name="out_grad",
    )(tp, own, far, w, w, q)


def attended_kernel(head, q_ref, s_ref, i_ref, o_ref):
    for j in range(q_ref.shape[1] // head):
        at = slice(j * head, (j + 1) * head)
        o_ref[:, at] = (dot(q_ref[:, at], s_ref[at, :], 1, 0) + i_ref[:, at]).astype(BF)


def attended_of(q, state, inner, head):
    tok, width = q.shape
    step = 2 * head
    spec = pl.BlockSpec((tok, step), lambda i: (0, i))
    return pl.pallas_call(
        functools.partial(attended_kernel, head),
        grid=(width // step,),
        in_specs=[spec, pl.BlockSpec((step, head), lambda i: (i, 0)), spec],
        out_specs=spec,
        out_shape=jax.ShapeDtypeStruct((tok, width), BF),
        compiler_params=params(),
        cost_estimate=cost(2 * tok * head * width, 8 * tok * width),
        name="attended",
    )(q, state, inner)


def weight_kernel(a_ref, own_ref, far_ref, o_ref):
    feat = own_ref.shape[1]
    a = a_ref[...]
    o_ref[:, :feat] = dot(a, own_ref[...], 0, 0).astype(o_ref.dtype)
    o_ref[:, feat:] = dot(a, far_ref[...], 0, 0).astype(o_ref.dtype)


def weight_term(a, own, far):
    tok, width = a.shape
    feat = own.shape[1]
    step = 256
    whole = pl.BlockSpec((tok, feat), lambda i: (0, 0))
    return pl.pallas_call(
        weight_kernel,
        grid=(width // step,),
        in_specs=[pl.BlockSpec((tok, step), lambda i: (0, i)), whole, whole],
        out_specs=pl.BlockSpec((step, 2 * feat), lambda i: (i, 0)),
        out_shape=jax.ShapeDtypeStruct((width, 2 * feat), BF),
        compiler_params=params(),
        cost_estimate=cost(4 * tok * feat * width, 4 * feat * width + 2 * tok * width),
        name="weight_term",
    )(a, own, far)


def query_kernel(head, g_ref, v_ref, k_ref, s_ref, o_ref):
    half = g_ref.shape[0] // 2
    for j in range(g_ref.shape[1] // head):
        at = slice(j * head, (j + 1) * head)
        g = g_ref[:, at]
        first, second = causal_apply(g, v_ref[:, at], k_ref[:, at], False)
        carried = dot(g, s_ref[at, :], 1, 1)
        o_ref[:half, at] = (first + carried[:half]).astype(BF)
        o_ref[half:, at] = (second + carried[half:]).astype(BF)


def query_grad_of(g, v, k, state, head):
    tok, width = g.shape
    step = 2 * head
    spec = pl.BlockSpec((tok, step), lambda i: (0, i))
    return pl.pallas_call(
        functools.partial(query_kernel, head),
        grid=(width // step,),
        in_specs=[spec, spec, spec, pl.BlockSpec((step, head), lambda i: (i, 0))],
        out_specs=spec,
        out_shape=jax.ShapeDtypeStruct((tok, width), BF),
        compiler_params=params(),
        cost_estimate=cost(4 * tok * tok * width, 8 * tok * width),
        name="query_grad",
    )(g, v, k, state)


def key_value_kernel(head, q_ref, k_ref, v_ref, g_ref, a_ref, ko_ref, vo_ref):
    half = g_ref.shape[0] // 2
    for j in range(g_ref.shape[1] // head):
        at = slice(j * head, (j + 1) * head)
        q, k, v, g, adj = q_ref[:, at], k_ref[:, at], v_ref[:, at], g_ref[:, at], a_ref[at, :]
        first, second = causal_apply(v, g, q, True)
        carried = dot(v, adj, 1, 1)
        ko_ref[:half, at] = (first + carried[:half]).astype(BF)
        ko_ref[half:, at] = (second + carried[half:]).astype(BF)
        first, second = causal_apply(k, q, g, True)
        carried = dot(k, adj, 1, 0)
        vo_ref[:half, at] = (first + carried[:half]).astype(BF)
        vo_ref[half:, at] = (second + carried[half:]).astype(BF)


def key_value_grad_of(q, k, v, g, adjoint, head):
    tok, width = g.shape
    step = 2 * head
    spec = pl.BlockSpec((tok, step), lambda i: (0, i))
    shape = jax.ShapeDtypeStruct((tok, width), BF)
    return pl.pallas_call(
        functools.partial(key_value_kernel, head),
        grid=(width // step,),
        in_specs=[spec, spec, spec, spec, pl.BlockSpec((step, head), lambda i: (i, 0))],
        out_specs=[spec, spec],
        out_shape=[shape, shape],
        compiler_params=params(),
        cost_estimate=cost(8 * tok * tok * width, 12 * tok * width),
        name="key_value_grad",
    )(q, k, v, g, adjoint)


ANY = pl.BlockSpec(memory_space=pl.ANY)


def scan_kernel(n, reverse, waits, x_ref, start_ref, *refs):
    o_ref = refs[waits]
    rows = start_ref.shape[0]
    total = start_ref[...]
    for i in range(n):
        c = n - 1 - i if reverse else i
        at = slice(c * rows, (c + 1) * rows)
        o_ref[at, :] = total.astype(BF)
        total = total + x_ref[at, :].astype(F32)


def scan_blocks(x, start, n, reverse, after=(), passed=None):
    more = () if passed is None else (passed,)
    out = pl.pallas_call(
        functools.partial(scan_kernel, n, reverse, len(after) + len(more)),
        in_specs=[pl.BlockSpec(x.shape, lambda: (0, 0)), pl.BlockSpec(start.shape, lambda: (0, 0))]
        + [ANY] * (len(after) + len(more)),
        out_specs=[pl.BlockSpec(x.shape, lambda: (0, 0))] + [ANY] * len(more),
        out_shape=[jax.ShapeDtypeStruct(x.shape, BF)]
        + [jax.ShapeDtypeStruct(p.shape, p.dtype) for p in more],
        input_output_aliases={2 + len(after): 1} if more else {},
        compiler_params=params(),
        cost_estimate=cost(0, 0),
        name="scan_blocks",
    )(x, start, *after, *more)
    return out if more else out[0]


def carried(x, start, axis, reverse):
    n = lax.axis_size(axis)
    mine = lax.all_to_all(x, axis, 0, 0, tiled=True)
    return lax.all_to_all(scan_blocks(mine, start, n, reverse), axis, 0, 0, tiled=True)


def pair_sums_kernel(head, me_ref, a_ref, b_ref, mine_ref, send_ref):
    even = dot(a_ref[:, :head], b_ref[:, :head], 0, 0)
    odd = dot(a_ref[:, head:], b_ref[:, head:], 0, 0)
    first = me_ref[0] % 2 == 0
    mine_ref[...] = jnp.where(first, even, odd).astype(BF)
    send_ref[...] = jnp.where(first, odd, even).astype(BF)


def pair_sums(me, a, b, head):
    tok, width = a.shape
    spec = pl.BlockSpec((tok, 2 * head), lambda i, m: (0, i))
    out = pl.BlockSpec((head, head), lambda i, m: (i, 0))
    shape = jax.ShapeDtypeStruct((width // 2, head), BF)
    return pl.pallas_call(
        functools.partial(pair_sums_kernel, head),
        grid_spec=pltpu.PrefetchScalarGridSpec(
            num_scalar_prefetch=1,
            grid=(width // (2 * head),),
            in_specs=[spec] * 2,
            out_specs=[out] * 2,
        ),
        out_shape=[shape] * 2,
        compiler_params=params(),
        cost_estimate=cost(2 * tok * width * head, 4 * tok * width),
        name="pair_sums",
    )(me, a, b)


def pair_intra_kernel(head, waits, me_ref, *refs):
    q_ref, k_ref, v_ref, mine_ref, send_ref = refs[waits:]
    first = me_ref[0] % 2 == 0
    half = q_ref.shape[0] // 2
    even, odd = slice(0, head), slice(head, 2 * head)
    parts = [causal_apply(q_ref[:, at], k_ref[:, at], v_ref[:, at], False) for at in (even, odd)]
    for k, at in enumerate((slice(0, half), slice(half, 2 * half))):
        mine_ref[at, :] = jnp.where(first, parts[0][k], parts[1][k]).astype(BF)
        send_ref[at, odd] = jnp.where(first, parts[1][k], parts[0][k]).astype(BF)
    send_ref[:, even] = jnp.where(first, q_ref[:, odd], q_ref[:, even])


def pair_intra(me, after, q, k, v, head):
    tok, width = q.shape
    steps = width // (2 * head)
    spec = pl.BlockSpec((tok, 2 * head), lambda i, m: (0, i))
    return pl.pallas_call(
        functools.partial(pair_intra_kernel, head, len(after)),
        grid_spec=pltpu.PrefetchScalarGridSpec(
            num_scalar_prefetch=1,
            grid=(steps,),
            in_specs=[ANY] * len(after) + [spec] * 3,
            out_specs=[
                pl.BlockSpec((tok, head), lambda i, m: (0, i)),
                pl.BlockSpec((tok, 2 * head), lambda i, m: (0, i)),
            ],
        ),
        out_shape=[
            jax.ShapeDtypeStruct((tok, width // 2), BF),
            jax.ShapeDtypeStruct((tok, width), BF),
        ],
        compiler_params=params(),
        cost_estimate=cost(4 * tok * tok * width, 9 * tok * width),
        name="pair_intra",
    )(me, *after, q, k, v)


def pair_attended_kernel(head, me_ref, after_ref, q0_ref, q1_ref, i_ref, far_ref, s_ref, own_ref, oth_ref, mine_ref, send_ref):
    core = (me_ref[0] % 2).astype(F32)
    south = (me_ref[0] // 2) % 2 == 0
    state = s_ref[...].astype(F32)
    near = (state + core * oth_ref[...].astype(F32)).astype(BF)
    away = (state + (1.0 - core) * own_ref[...].astype(F32)).astype(BF)
    results = []
    for j, q_ref in enumerate((q0_ref, q1_ref)):
        at = slice(j * head, (j + 1) * head)
        here = dot(q_ref[...], near[at], 1, 0) + i_ref[:, at].astype(F32)
        base = 2 * j * head
        there = dot(far_ref[:, base : base + head], away[at], 1, 0)
        there = there + far_ref[:, base + head : base + 2 * head].astype(F32)
        results.append((here, there))
    for k in range(2):
        mine_ref[0, k] = jnp.where(south, results[0][k], results[1][k]).astype(BF)
        send_ref[0, k] = jnp.where(south, results[1][k], results[0][k]).astype(BF)


def pair_attended(me, after, q, inner, far, state, own, oth, head):
    tok, width = q.shape
    places = width // (4 * head)

    def place(i, m):
        return (m[0] // 4) ^ i

    rows = pl.BlockSpec((2 * head, head), lambda i, m: (place(i, m), 0))
    out = pl.BlockSpec((1, 2, tok, head), lambda i, m: (i, 0, 0, 0))
    shape = jax.ShapeDtypeStruct((places, 2, tok, head), BF)
    return pl.pallas_call(
        functools.partial(pair_attended_kernel, head),
        grid_spec=pltpu.PrefetchScalarGridSpec(
            num_scalar_prefetch=1,
            grid=(places,),
            in_specs=[
                ANY,
                pl.BlockSpec((tok, head), lambda i, m: (0, 4 * place(i, m) + m[0] % 2)),
                pl.BlockSpec((tok, head), lambda i, m: (0, 4 * place(i, m) + 2 + m[0] % 2)),
                pl.BlockSpec((tok, 2 * head), lambda i, m: (0, place(i, m))),
                pl.BlockSpec((tok, 4 * head), lambda i, m: (0, place(i, m))),
            ]
            + [rows] * 3,
            out_specs=[out, out],
        ),
        out_shape=[shape, shape],
        compiler_params=params(),
        cost_estimate=cost(2 * tok * head * width, 10 * tok * width),
        name="pair_attended",
    )(me, after, q, q, inner, far, state, own, oth)


def quad_weight_kernel(waits, a_ref, b_ref, *refs):
    half, _, tok, head = a_ref.shape
    ins, outs, at_ref = refs[:8], refs[8 + waits : -1], refs[-1]

    @pl.when(pl.program_id(0) == 0)
    def _():
        for i in range(half):
            for k in range(4):
                block = (a_ref if k < 2 else b_ref)[i, k % 2]
                at_ref[i * head : (i + 1) * head, k * tok : (k + 1) * tok] = block.T

    for part in range(2):
        total = None
        for k in range(4):
            term = dot(at_ref[:, k * tok : (k + 1) * tok], ins[2 * k + part][...], 1, 0)
            total = term if total is None else total + term
        for i, o_ref in enumerate(outs):
            o_ref[part] = total[i * head : (i + 1) * head].astype(BF)


def quad_weight(after, a, b, cots, far_side):
    places, _, tok, head = a.shape
    half = places // 2
    feat = cots[0].shape[1]
    step = min(256, feat)
    whole = pl.BlockSpec((half,) + a.shape[1:], lambda i: (far_side, 0, 0, 0))
    return pl.pallas_call(
        functools.partial(quad_weight_kernel, len(after)),
        grid=(feat // step,),
        in_specs=[whole, whole]
        + [pl.BlockSpec((tok, step), lambda i: (0, i))] * 8
        + [ANY] * len(after),
        out_specs=[pl.BlockSpec((2, head, step), lambda i: (0, 0, i))] * half,
        out_shape=[jax.ShapeDtypeStruct((2, head, feat), BF)] * half,
        scratch_shapes=[pltpu.VMEM((half * head, 4 * tok), BF)],
        compiler_params=params(),
        cost_estimate=cost(16 * tok * feat * half * head * far_side, 20 * feat * tok * far_side),
        name="quad_weight",
    )(a, b, *cots, *after)


def final_kernel(tp_ref, *refs):
    total = refs[0][0].astype(F32)
    for r in refs[1:-1]:
        total = total + r[0].astype(F32)
    refs[-1][...] = total


def final_sum(tp, parts):
    _, rows, feat = parts[0].shape
    return pl.pallas_call(
        final_kernel,
        grid_spec=pltpu.PrefetchScalarGridSpec(
            num_scalar_prefetch=1,
            grid=(2,),
            in_specs=[pl.BlockSpec((1, rows, feat), lambda i, t: (i, 0, 0))] * len(parts),
            out_specs=pl.BlockSpec((rows, feat), lambda i, t: (0, i ^ t[0])),
        ),
        out_shape=jax.ShapeDtypeStruct((rows, 2 * feat), F32),
        compiler_params=params(),
        cost_estimate=cost(len(parts) * rows * feat, 20 * rows * feat),
        name="final_sum",
    )(tp, *parts)


def pair_query_kernel(head, me_ref, after_ref, g_ref, v_ref, k_ref, s_ref, kv_ref, t_ref, o_ref):
    core = me_ref[0] % 2
    half = g_ref.shape[0] // 2
    near = (s_ref[...].astype(F32) + core.astype(F32) * kv_ref[...].astype(F32)).astype(BF)
    for j in range(2):
        at = slice(j * head, (j + 1) * head)
        g = g_ref[:, at]
        state = jnp.where(core == j, near, t_ref[...])
        first_half, second_half = causal_apply(g, v_ref[:, at], k_ref[:, at], False)
        over = dot(g, state, 1, 1)
        o_ref[:half, at] = (first_half + over[:half]).astype(BF)
        o_ref[half:, at] = (second_half + over[half:]).astype(BF)


def pair_query_grad(me, after, g, v, k, state, kv, other, head):
    tok, width = g.shape
    spec = pl.BlockSpec((tok, 2 * head), lambda i, m: (0, i))
    rows = pl.BlockSpec((head, head), lambda i, m: (i, 0))
    return pl.pallas_call(
        functools.partial(pair_query_kernel, head),
        grid_spec=pltpu.PrefetchScalarGridSpec(
            num_scalar_prefetch=1,
            grid=(width // (2 * head),),
            in_specs=[ANY, spec, spec, spec, rows, rows, rows],
            out_specs=spec,
        ),
        out_shape=jax.ShapeDtypeStruct((tok, width), BF),
        compiler_params=params(),
        cost_estimate=cost(0, 0),
        name="query_grad",
    )(me, after, g, v, k, state, kv, other)


def pair_grad_kernel(head, me_ref, tp_ref, after_ref, own_ref, far_ref, wo_ref, wf_ref, q_ref,
                     g_ref, mine_ref, send_ref):
    g = dot(own_ref[...], wo_ref[...], 1, 1) + dot(far_ref[...], wf_ref[...], 1, 1)
    g = g.astype(BF)
    g_ref[...] = g
    first = me_ref[0] % 2 == 0
    even = dot(q_ref[:, :head], g[:, :head], 0, 0)
    odd = dot(q_ref[:, head:], g[:, head:], 0, 0)
    mine_ref[...] = jnp.where(first, even, odd).astype(BF)
    send_ref[...] = jnp.where(first, odd, even).astype(BF)


def pair_grad(me, tp, after, own, far, w, q, head):
    tok, feat = own.shape
    width = q.shape[1]
    step = 2 * head
    whole = pl.BlockSpec((tok, feat), lambda i, m, t: (0, 0))
    rows = pl.BlockSpec((head, head), lambda i, m, t: (i, 0))
    sums = jax.ShapeDtypeStruct((width // 2, head), BF)
    return pl.pallas_call(
        functools.partial(pair_grad_kernel, head),
        grid_spec=pltpu.PrefetchScalarGridSpec(
            num_scalar_prefetch=2,
            grid=(width // step,),
            in_specs=[
                ANY,
                whole,
                whole,
                pl.BlockSpec((step, feat), lambda i, m, t: (i, t[0])),
                pl.BlockSpec((step, feat), lambda i, m, t: (i, 1 - t[0])),
                pl.BlockSpec((tok, step), lambda i, m, t: (0, i)),
            ],
            out_specs=[
                pl.BlockSpec((tok, step), lambda i, m, t: (0, i)),
                rows,
                rows,
            ],
        ),
        out_shape=[
            jax.ShapeDtypeStruct((tok, width), BF),
            sums,
            sums,
        ],
        compiler_params=params(),
        cost_estimate=cost(4 * tok * feat * width, 4 * feat * width + 4 * tok * width),
        name="out_grad",
    )(me, tp, after, own, far, w, w, q)


def add_kernel(after_ref, a_ref, b_ref, o_ref):
    o_ref[...] = (a_ref[...].astype(F32) + b_ref[...].astype(F32)).astype(BF)


def add_after(after, a, b):
    spec = pl.BlockSpec(a.shape, lambda: (0, 0))
    return pl.pallas_call(
        add_kernel,
        in_specs=[ANY, spec, spec],
        out_specs=spec,
        out_shape=jax.ShapeDtypeStruct(a.shape, BF),
        compiler_params=params(),
        cost_estimate=cost(0, 0),
        name="add_after",
    )(after, a, b)


def pair_key_value_kernel(head, me_ref, after_ref, q_ref, k_ref, v_ref, g_ref, s_ref, qd_ref, t_ref, ko_ref, vo_ref):
    core = me_ref[0] % 2
    half = g_ref.shape[0] // 2
    near = (s_ref[...].astype(F32) + (1 - core).astype(F32) * qd_ref[...].astype(F32)).astype(BF)
    for j in range(2):
        at = slice(j * head, (j + 1) * head)
        q, k, v, g = q_ref[:, at], k_ref[:, at], v_ref[:, at], g_ref[:, at]
        adj = jnp.where(core == j, near, t_ref[...])
        first, second = causal_apply(v, g, q, True)
        over = dot(v, adj, 1, 1)
        ko_ref[:half, at] = (first + over[:half]).astype(BF)
        ko_ref[half:, at] = (second + over[half:]).astype(BF)
        first, second = causal_apply(k, q, g, True)
        over = dot(k, adj, 1, 0)
        vo_ref[:half, at] = (first + over[:half]).astype(BF)
        vo_ref[half:, at] = (second + over[half:]).astype(BF)


def pair_key_value_grad(me, after, q, k, v, g, adjoint, qd, other, head):
    tok, width = g.shape
    spec = pl.BlockSpec((tok, 2 * head), lambda i, m: (0, i))
    rows = pl.BlockSpec((head, head), lambda i, m: (i, 0))
    shape = jax.ShapeDtypeStruct((tok, width), BF)
    return pl.pallas_call(
        functools.partial(pair_key_value_kernel, head),
        grid_spec=pltpu.PrefetchScalarGridSpec(
            num_scalar_prefetch=1,
            grid=(width // (2 * head),),
            in_specs=[ANY, spec, spec, spec, spec, rows, rows, rows],
            out_specs=[spec, spec],
        ),
        out_shape=[shape, shape],
        compiler_params=params(),
        cost_estimate=cost(0, 0),
        name="key_value_grad",
    )(me, after, q, k, v, g, adjoint, qd, other)


def local_paired(queries, keys, values, cotangent, out_weight, memory):
    head = memory.shape[2]
    n = lax.axis_size("ctx")
    me, tp = lax.axis_index("ctx"), lax.axis_index("tp")
    who, which = me.reshape(1), tp.reshape(1)
    core = (me % 2).astype(F32)
    groups = [[c for c in range(n) if c % 2 == side] for side in range(2)]

    def swap(x, bit):
        return lax.ppermute(x, "ctx", [(c, c ^ bit) for c in range(n)])

    def swap_tp(x):
        return lax.ppermute(x, "tp", [(0, 1), (1, 0)])

    def across(x):
        return lax.all_to_all(x, "ctx", 0, 0, axis_index_groups=groups, tiled=True)

    def added(x, factor, y):
        return (x.astype(F32) + factor * y.astype(F32)).astype(BF)

    far = swap_tp(cotangent)
    south = swap(cotangent, 2)

    kv_mine, kv_send = pair_sums(who, keys, values, head)
    kv_other = swap(kv_send, 1)
    chip = added(kv_mine, 1.0, kv_other)
    inner, sent = pair_intra(who, (chip,), queries, keys, values, head)
    start = lax.dynamic_index_in_dim(memory, me, 0, False)
    scanned, sent = scan_blocks(across(chip), start, n // 2, False, (inner, far, south), sent)
    state = across(scanned)

    far_south = swap_tp(south)
    grad, qd_mine, qd_send = pair_grad(who, which, scanned, cotangent, far, out_weight, queries, head)
    mine, send = pair_attended(who, grad, queries, inner, swap(sent, 1), state, kv_mine, kv_other, head)
    received = swap(send, 2)
    state_other = swap(added(state, 1.0 - core, kv_mine), 1)

    qd_other = swap(qd_send, 1)
    chip = add_after(send, qd_mine, qd_other)
    query_g = pair_query_grad(who, chip, grad, values, keys, state, kv_other, state_other, head)
    scanned, far_south = scan_blocks(
        across(chip), jnp.zeros_like(start), n // 2, True, (query_g,), far_south
    )
    after_chip = across(scanned)
    cots = [cotangent, far, swap(cotangent, 1), swap(far, 1)]
    cots += [south, far_south, swap(south, 1), swap(far_south, 1)]

    crossing = quad_weight((scanned,), mine, received, cots, 1)
    crossed = swap(added(crossing[0], 1.0, swap(crossing[1], 4)), 8)
    same = quad_weight((crossing[0],), mine, received, cots, 0)
    neighbour = swap(same[1], 4)
    adjoint_other = swap(added(after_chip, core, qd_mine), 1)
    key_g, value_g = pair_key_value_grad(
        who, same[0], queries, keys, values, grad, after_chip, qd_other, adjoint_other, head
    )
    return query_g, key_g, value_g, final_sum(which, [same[0], neighbour, crossed])


def local_any(queries, keys, values, cotangent, out_weight, memory):
    head = memory.shape[2]
    width = queries.shape[1]
    feat = cotangent.shape[1]
    n = lax.axis_size("ctx")
    rows = width // n
    me, tp = lax.axis_index("ctx"), lax.axis_index("tp")

    far = lax.ppermute(cotangent, "tp", [(0, 1), (1, 0)])
    kv = block_sums(keys, values, head)
    start = lax.dynamic_slice_in_dim(memory.reshape(width, head), me * rows, rows, 0)
    state = carried(kv, start, "ctx", False)
    inner = intra(queries, keys, values, head)
    grad, qd = out_grad_and_sums(tp.reshape(1), cotangent, far, out_weight, queries, head)
    adjoint = carried(qd, jnp.zeros_like(start), "ctx", True)
    attended = attended_of(queries, state, inner, head)
    term = weight_term(attended, cotangent, far)
    total = lax.psum_scatter(term, "ctx", scatter_dimension=0, tiled=True)
    query_g = query_grad_of(grad, values, keys, state, head)
    key_g, value_g = key_value_grad_of(queries, keys, values, grad, adjoint, head)
    total = total.astype(F32)
    total = jnp.where(tp == 0, total, jnp.concatenate([total[:, feat:], total[:, :feat]], 1))
    return query_g, key_g, value_g, total


def local(*args):
    heads = args[5].shape[0]
    n = lax.axis_size("ctx")
    if n == heads == 16 and lax.axis_size("tp") == 2:
        return local_paired(*args)
    return local_any(*args)


def solution(mesh):
    in_specs = (
        P("ctx", "tp"),
        P("ctx", "tp"),
        P("ctx", "tp"),
        P("ctx", "tp"),
        P("tp", None),
        P("tp", None, None),
    )
    out_specs = (P("ctx", "tp"), P("ctx", "tp"), P("ctx", "tp"), P(("tp", "ctx"), None))
    return jax.shard_map(local, mesh=mesh, in_specs=in_specs, out_specs=out_specs, check_vma=False)
```

```python
import functools

import jax
import jax.numpy as jnp
from jax import lax
from jax.experimental import pallas as pl
from jax.experimental.pallas import tpu as pltpu
from jax.sharding import PartitionSpec as P

BF = jnp.bfloat16
F32 = jnp.float32
VMEM_LIMIT = 56 * 1024 * 1024


def dot(a, b, ca, cb):
    return lax.dot_general(a, b, (((ca,), (cb,)), ((), ())), preferred_element_type=F32)


def lanes(index, head):
    return pl.ds(pl.multiple_of(index * head, head), head)


def params():
    return pltpu.CompilerParams(vmem_limit_bytes=VMEM_LIMIT)


def cost(flops, nbytes):
    return pl.CostEstimate(flops=int(flops), bytes_accessed=int(nbytes), transcendentals=0)


def kv_kernel(head, a_ref, b_ref, o_ref):
    for j in range(a_ref.shape[1] // head):
        at = slice(j * head, (j + 1) * head)
        o_ref[at, :] = dot(a_ref[:, at], b_ref[:, at], 0, 0).astype(o_ref.dtype)


def block_sums(a, b, head):
    tok, width = a.shape
    step = 2 * head
    return pl.pallas_call(
        functools.partial(kv_kernel, head),
        grid=(width // step,),
        in_specs=[pl.BlockSpec((tok, step), lambda i: (0, i))] * 2,
        out_specs=pl.BlockSpec((step, head), lambda i: (i, 0)),
        out_shape=jax.ShapeDtypeStruct((width, head), BF),
        compiler_params=params(),
        cost_estimate=cost(2 * tok * width * head, 4 * tok * width),
        name="block_sums",
    )(a, b)


def masked(tok, upper):
    row = lax.broadcasted_iota(jnp.int32, (tok, tok), 0)
    col = lax.broadcasted_iota(jnp.int32, (tok, tok), 1)
    return row <= col if upper else row >= col


def causal_apply(a, b, c, upper):
    tok = a.shape[0]
    half = tok // 2
    keep = masked(half, upper)

    def tile(x, y, diagonal):
        s = dot(x, y, 1, 1)
        if diagonal:
            s = jnp.where(keep, s, 0.0)
        return s.astype(BF)

    a0, a1, b0, b1, c0, c1 = a[:half], a[half:], b[:half], b[half:], c[:half], c[half:]
    first = dot(tile(a0, b0, True), c0, 1, 0)
    second = dot(tile(a1, b1, True), c1, 1, 0)
    if upper:
        first = first + dot(tile(a0, b1, False), c1, 1, 0)
    else:
        second = second + dot(tile(a1, b0, False), c0, 1, 0)
    return first, second


def intra_kernel(head, q_ref, k_ref, v_ref, o_ref):
    half = q_ref.shape[0] // 2
    for j in range(q_ref.shape[1] // head):
        at = slice(j * head, (j + 1) * head)
        first, second = causal_apply(q_ref[:, at], k_ref[:, at], v_ref[:, at], False)
        o_ref[:half, at] = first
        o_ref[half:, at] = second


def intra(q, k, v, head):
    tok, width = q.shape
    step = 2 * head
    spec = pl.BlockSpec((tok, step), lambda i: (0, i))
    return pl.pallas_call(
        functools.partial(intra_kernel, head),
        grid=(width // step,),
        in_specs=[spec] * 3,
        out_specs=spec,
        out_shape=jax.ShapeDtypeStruct((tok, width), F32),
        compiler_params=params(),
        cost_estimate=cost(4 * tok * tok * width, 10 * tok * width),
        name="intra",
    )(q, k, v)


def grad_kernel(head, tp_ref, own_ref, far_ref, wo_ref, wf_ref, q_ref, g_ref, s_ref):
    g = dot(own_ref[...], wo_ref[...], 1, 1) + dot(far_ref[...], wf_ref[...], 1, 1)
    g = g.astype(BF)
    g_ref[...] = g
    for j in range(g.shape[1] // head):
        at = slice(j * head, (j + 1) * head)
        s_ref[at, :] = dot(q_ref[:, at], g[:, at], 0, 0).astype(s_ref.dtype)


def out_grad_and_sums(tp, own, far, w, q, head):
    tok, feat = own.shape
    width = q.shape[1]
    step = 2 * head
    whole = pl.BlockSpec((tok, feat), lambda i, t: (0, 0))
    return pl.pallas_call(
        functools.partial(grad_kernel, head),
        grid_spec=pltpu.PrefetchScalarGridSpec(
            num_scalar_prefetch=1,
            grid=(width // step,),
            in_specs=[
                whole,
                whole,
                pl.BlockSpec((step, feat), lambda i, t: (i, t[0])),
                pl.BlockSpec((step, feat), lambda i, t: (i, 1 - t[0])),
                pl.BlockSpec((tok, step), lambda i, t: (0, i)),
            ],
            out_specs=[
                pl.BlockSpec((tok, step), lambda i, t: (0, i)),
                pl.BlockSpec((step, head), lambda i, t: (i, 0)),
            ],
        ),
        out_shape=[
            jax.ShapeDtypeStruct((tok, width), BF),
            jax.ShapeDtypeStruct((width, head), BF),
        ],
        compiler_params=params(),
        cost_estimate=cost(4 * tok * feat * width, 4 * feat * width + 4 * tok * width),
        name="out_grad",
    )(tp, own, far, w, w, q)


def attended_kernel(head, q_ref, s_ref, i_ref, o_ref):
    for j in range(q_ref.shape[1] // head):
        at = slice(j * head, (j + 1) * head)
        o_ref[:, at] = (dot(q_ref[:, at], s_ref[at, :], 1, 0) + i_ref[:, at]).astype(BF)


def attended_of(q, state, inner, head):
    tok, width = q.shape
    step = 2 * head
    spec = pl.BlockSpec((tok, step), lambda i: (0, i))
    return pl.pallas_call(
        functools.partial(attended_kernel, head),
        grid=(width // step,),
        in_specs=[spec, pl.BlockSpec((step, head), lambda i: (i, 0)), spec],
        out_specs=spec,
        out_shape=jax.ShapeDtypeStruct((tok, width), BF),
        compiler_params=params(),
        cost_estimate=cost(2 * tok * head * width, 8 * tok * width),
        name="attended",
    )(q, state, inner)


def weight_kernel(a_ref, own_ref, far_ref, o_ref):
    feat = own_ref.shape[1]
    a = a_ref[...]
    o_ref[:, :feat] = dot(a, own_ref[...], 0, 0).astype(o_ref.dtype)
    o_ref[:, feat:] = dot(a, far_ref[...], 0, 0).astype(o_ref.dtype)


def weight_term(a, own, far):
    tok, width = a.shape
    feat = own.shape[1]
    step = 256
    whole = pl.BlockSpec((tok, feat), lambda i: (0, 0))
    return pl.pallas_call(
        weight_kernel,
        grid=(width // step,),
        in_specs=[pl.BlockSpec((tok, step), lambda i: (0, i)), whole, whole],
        out_specs=pl.BlockSpec((step, 2 * feat), lambda i: (i, 0)),
        out_shape=jax.ShapeDtypeStruct((width, 2 * feat), BF),
        compiler_params=params(),
        cost_estimate=cost(4 * tok * feat * width, 4 * feat * width + 2 * tok * width),
        name="weight_term",
    )(a, own, far)


def query_kernel(head, g_ref, v_ref, k_ref, s_ref, o_ref):
    half = g_ref.shape[0] // 2
    for j in range(g_ref.shape[1] // head):
        at = slice(j * head, (j + 1) * head)
        g = g_ref[:, at]
        first, second = causal_apply(g, v_ref[:, at], k_ref[:, at], False)
        carried = dot(g, s_ref[at, :], 1, 1)
        o_ref[:half, at] = (first + carried[:half]).astype(BF)
        o_ref[half:, at] = (second + carried[half:]).astype(BF)


def query_grad_of(g, v, k, state, head):
    tok, width = g.shape
    step = 2 * head
    spec = pl.BlockSpec((tok, step), lambda i: (0, i))
    return pl.pallas_call(
        functools.partial(query_kernel, head),
        grid=(width // step,),
        in_specs=[spec, spec, spec, pl.BlockSpec((step, head), lambda i: (i, 0))],
        out_specs=spec,
        out_shape=jax.ShapeDtypeStruct((tok, width), BF),
        compiler_params=params(),
        cost_estimate=cost(4 * tok * tok * width, 8 * tok * width),
        name="query_grad",
    )(g, v, k, state)


def key_value_kernel(head, q_ref, k_ref, v_ref, g_ref, a_ref, ko_ref, vo_ref):
    half = g_ref.shape[0] // 2
    for j in range(g_ref.shape[1] // head):
        at = slice(j * head, (j + 1) * head)
        q, k, v, g, adj = q_ref[:, at], k_ref[:, at], v_ref[:, at], g_ref[:, at], a_ref[at, :]
        first, second = causal_apply(v, g, q, True)
        carried = dot(v, adj, 1, 1)
        ko_ref[:half, at] = (first + carried[:half]).astype(BF)
        ko_ref[half:, at] = (second + carried[half:]).astype(BF)
        first, second = causal_apply(k, q, g, True)
        carried = dot(k, adj, 1, 0)
        vo_ref[:half, at] = (first + carried[:half]).astype(BF)
        vo_ref[half:, at] = (second + carried[half:]).astype(BF)


def key_value_grad_of(q, k, v, g, adjoint, head):
    tok, width = g.shape
    step = 2 * head
    spec = pl.BlockSpec((tok, step), lambda i: (0, i))
    shape = jax.ShapeDtypeStruct((tok, width), BF)
    return pl.pallas_call(
        functools.partial(key_value_kernel, head),
        grid=(width // step,),
        in_specs=[spec, spec, spec, spec, pl.BlockSpec((step, head), lambda i: (i, 0))],
        out_specs=[spec, spec],
        out_shape=[shape, shape],
        compiler_params=params(),
        cost_estimate=cost(8 * tok * tok * width, 12 * tok * width),
        name="key_value_grad",
    )(q, k, v, g, adjoint)


ANY = pl.BlockSpec(memory_space=pl.ANY)


def scan_kernel(n, reverse, waits, x_ref, start_ref, *refs):
    o_ref = refs[waits]
    rows = start_ref.shape[0]
    total = start_ref[...]
    for i in range(n):
        c = n - 1 - i if reverse else i
        at = slice(c * rows, (c + 1) * rows)
        o_ref[at, :] = total.astype(BF)
        total = total + x_ref[at, :].astype(F32)


def scan_blocks(x, start, n, reverse, after=(), passed=None):
    more = () if passed is None else (passed,)
    out = pl.pallas_call(
        functools.partial(scan_kernel, n, reverse, len(after) + len(more)),
        in_specs=[pl.BlockSpec(x.shape, lambda: (0, 0)), pl.BlockSpec(start.shape, lambda: (0, 0))]
        + [ANY] * (len(after) + len(more)),
        out_specs=[pl.BlockSpec(x.shape, lambda: (0, 0))] + [ANY] * len(more),
        out_shape=[jax.ShapeDtypeStruct(x.shape, BF)]
        + [jax.ShapeDtypeStruct(p.shape, p.dtype) for p in more],
        input_output_aliases={2 + len(after): 1} if more else {},
        compiler_params=params(),
        cost_estimate=cost(0, 0),
        name="scan_blocks",
    )(x, start, *after, *more)
    return out if more else out[0]


def carried(x, start, axis, reverse):
    n = lax.axis_size(axis)
    mine = lax.all_to_all(x, axis, 0, 0, tiled=True)
    return lax.all_to_all(scan_blocks(mine, start, n, reverse), axis, 0, 0, tiled=True)


def pair_sums_kernel(head, me_ref, a_ref, b_ref, mine_ref, send_ref):
    core = me_ref[0] % 2
    for j in range(a_ref.shape[1] // (2 * head)):
        at = slice(j * head, (j + 1) * head)
        for o_ref, side in ((send_ref, 1 - core), (mine_ref, core)):
            pick = lanes(2 * j + side, head)
            o_ref[at, :] = dot(a_ref[:, pick], b_ref[:, pick], 0, 0).astype(BF)


def pair_sums(me, a, b, head):
    tok, width = a.shape
    step = min(4 * head, width)
    spec = pl.BlockSpec((tok, step), lambda i, m: (0, i))
    out = pl.BlockSpec((step // 2, head), lambda i, m: (i, 0))
    shape = jax.ShapeDtypeStruct((width // 2, head), BF)
    return pl.pallas_call(
        functools.partial(pair_sums_kernel, head),
        grid_spec=pltpu.PrefetchScalarGridSpec(
            num_scalar_prefetch=1,
            grid=(width // step,),
            in_specs=[spec] * 2,
            out_specs=[out] * 2,
        ),
        out_shape=[shape] * 2,
        compiler_params=params(),
        cost_estimate=cost(2 * tok * width * head, 4 * tok * width),
        name="pair_sums",
    )(me, a, b)


def pair_intra_kernel(head, waits, me_ref, *refs):
    q_ref, k_ref, v_ref, mine_ref, send_ref = refs[waits:]
    core = me_ref[0] % 2
    half = q_ref.shape[0] // 2
    mine, other = lanes(core, head), lanes(1 - core, head)
    first, second = causal_apply(q_ref[:, other], k_ref[:, other], v_ref[:, other], False)
    send_ref[:half, head:] = first.astype(BF)
    send_ref[half:, head:] = second.astype(BF)
    send_ref[:, :head] = q_ref[:, other]
    first, second = causal_apply(q_ref[:, mine], k_ref[:, mine], v_ref[:, mine], False)
    mine_ref[:half, :] = first.astype(BF)
    mine_ref[half:, :] = second.astype(BF)


def pair_intra(me, after, q, k, v, head):
    tok, width = q.shape
    steps = width // (2 * head)
    spec = pl.BlockSpec((tok, 2 * head), lambda i, m: (0, i))
    return pl.pallas_call(
        functools.partial(pair_intra_kernel, head, len(after)),
        grid_spec=pltpu.PrefetchScalarGridSpec(
            num_scalar_prefetch=1,
            grid=(steps,),
            in_specs=[ANY] * len(after) + [spec] * 3,
            out_specs=[
                pl.BlockSpec((tok, head), lambda i, m: (0, i)),
                pl.BlockSpec((tok, 2 * head), lambda i, m: (0, i)),
            ],
        ),
        out_shape=[
            jax.ShapeDtypeStruct((tok, width // 2), BF),
            jax.ShapeDtypeStruct((tok, width), BF),
        ],
        compiler_params=params(),
        cost_estimate=cost(4 * tok * tok * width, 9 * tok * width),
        name="pair_intra",
    )(me, *after, q, k, v)


def pair_attended_kernel(head, me_ref, after_ref, q0_ref, q1_ref, i_ref, far_ref, s_ref, own_ref, oth_ref, mine_ref, send_ref):
    core = (me_ref[0] % 2).astype(F32)
    south = (me_ref[0] // 2) % 2
    for q_ref, side, o_ref in ((q0_ref, south, mine_ref), (q1_ref, 1 - south, send_ref)):
        rows = lanes(side, head)
        state = s_ref[rows, :].astype(F32)
        near = (state + core * oth_ref[rows, :].astype(F32)).astype(BF)
        away = (state + (1.0 - core) * own_ref[rows, :].astype(F32)).astype(BF)
        here = dot(q_ref[...], near, 1, 0) + i_ref[:, lanes(side, head)].astype(F32)
        there = dot(far_ref[:, lanes(2 * side, head)], away, 1, 0)
        there = there + far_ref[:, lanes(2 * side + 1, head)].astype(F32)
        o_ref[0, 0] = here.astype(BF)
        o_ref[0, 1] = there.astype(BF)


def pair_attended(me, after, q, inner, far, state, own, oth, head):
    tok, width = q.shape
    places = width // (4 * head)

    def place(i, m):
        return (m[0] // 4) ^ i

    rows = pl.BlockSpec((2 * head, head), lambda i, m: (place(i, m), 0))
    out = pl.BlockSpec((1, 2, tok, head), lambda i, m: (i, 0, 0, 0))
    shape = jax.ShapeDtypeStruct((places, 2, tok, head), BF)
    return pl.pallas_call(
        functools.partial(pair_attended_kernel, head),
        grid_spec=pltpu.PrefetchScalarGridSpec(
            num_scalar_prefetch=1,
            grid=(places,),
            in_specs=[
                ANY,
                pl.BlockSpec((tok, head), lambda i, m: (0, 4 * place(i, m) + m[0] % 4)),
                pl.BlockSpec((tok, head), lambda i, m: (0, 4 * place(i, m) + (m[0] % 4 ^ 2))),
                pl.BlockSpec((tok, 2 * head), lambda i, m: (0, place(i, m))),
                pl.BlockSpec((tok, 4 * head), lambda i, m: (0, place(i, m))),
            ]
            + [rows] * 3,
            out_specs=[out, out],
        ),
        out_shape=[shape, shape],
        compiler_params=params(),
        cost_estimate=cost(2 * tok * head * width, 10 * tok * width),
        name="pair_attended",
    )(me, after, q, q, inner, far, state, own, oth)


def quad_weight_kernel(waits, a_ref, b_ref, *refs):
    half, _, tok, head = a_ref.shape
    ins, outs, at_ref = refs[:8], refs[8 + waits : -1], refs[-1]

    @pl.when(pl.program_id(0) == 0)
    def _():
        for i in range(half):
            for k in range(4):
                block = (a_ref if k < 2 else b_ref)[i, k % 2]
                at_ref[i * head : (i + 1) * head, k * tok : (k + 1) * tok] = block.T

    for part in range(2):
        total = None
        for k in range(4):
            term = dot(at_ref[:, k * tok : (k + 1) * tok], ins[2 * k + part][...], 1, 0)
            total = term if total is None else total + term
        for i, o_ref in enumerate(outs):
            o_ref[part] = total[i * head : (i + 1) * head].astype(BF)


def quad_weight(after, a, b, cots, far_side):
    places, _, tok, head = a.shape
    half = places // 2
    feat = cots[0].shape[1]
    step = min(256, feat)
    whole = pl.BlockSpec((half,) + a.shape[1:], lambda i: (far_side, 0, 0, 0))
    return pl.pallas_call(
        functools.partial(quad_weight_kernel, len(after)),
        grid=(feat // step,),
        in_specs=[whole, whole]
        + [pl.BlockSpec((tok, step), lambda i: (0, i))] * 8
        + [ANY] * len(after),
        out_specs=[pl.BlockSpec((2, head, step), lambda i: (0, 0, i))] * half,
        out_shape=[jax.ShapeDtypeStruct((2, head, feat), BF)] * half,
        scratch_shapes=[pltpu.VMEM((half * head, 4 * tok), BF)],
        compiler_params=params(),
        cost_estimate=cost(16 * tok * feat * half * head * far_side, 20 * feat * tok * far_side),
        name="quad_weight",
    )(a, b, *cots, *after)


def final_kernel(tp_ref, *refs):
    total = refs[0][0].astype(F32)
    for r in refs[1:-1]:
        total = total + r[0].astype(F32)
    refs[-1][...] = total


def final_sum(tp, parts):
    _, rows, feat = parts[0].shape
    return pl.pallas_call(
        final_kernel,
        grid_spec=pltpu.PrefetchScalarGridSpec(
            num_scalar_prefetch=1,
            grid=(2,),
            in_specs=[pl.BlockSpec((1, rows, feat), lambda i, t: (i, 0, 0))] * len(parts),
            out_specs=pl.BlockSpec((rows, feat), lambda i, t: (0, i ^ t[0])),
        ),
        out_shape=jax.ShapeDtypeStruct((rows, 2 * feat), F32),
        compiler_params=params(),
        cost_estimate=cost(len(parts) * rows * feat, 20 * rows * feat),
        name="final_sum",
    )(tp, *parts)


def pair_query_kernel(head, me_ref, after_ref, g_ref, v_ref, k_ref, s_ref, kv_ref, t_ref, o_ref):
    core = me_ref[0] % 2
    half = g_ref.shape[0] // 2
    near = (s_ref[...].astype(F32) + core.astype(F32) * kv_ref[...].astype(F32)).astype(BF)
    for j in range(2):
        at = slice(j * head, (j + 1) * head)
        g = g_ref[:, at]
        state = jnp.where(core == j, near, t_ref[...])
        first_half, second_half = causal_apply(g, v_ref[:, at], k_ref[:, at], False)
        over = dot(g, state, 1, 1)
        o_ref[:half, at] = (first_half + over[:half]).astype(BF)
        o_ref[half:, at] = (second_half + over[half:]).astype(BF)


def pair_query_grad(me, after, g, v, k, state, kv, other, head):
    tok, width = g.shape
    spec = pl.BlockSpec((tok, 2 * head), lambda i, m: (0, i))
    rows = pl.BlockSpec((head, head), lambda i, m: (i, 0))
    return pl.pallas_call(
        functools.partial(pair_query_kernel, head),
        grid_spec=pltpu.PrefetchScalarGridSpec(
            num_scalar_prefetch=1,
            grid=(width // (2 * head),),
            in_specs=[ANY, spec, spec, spec, rows, rows, rows],
            out_specs=spec,
        ),
        out_shape=jax.ShapeDtypeStruct((tok, width), BF),
        compiler_params=params(),
        cost_estimate=cost(0, 0),
        name="query_grad",
    )(me, after, g, v, k, state, kv, other)


def pair_grad_kernel(head, me_ref, tp_ref, after_ref, own_ref, far_ref, w_ref, q_ref, g_ref, mine_ref, send_ref, cot_ref):
    feat = own_ref.shape[1]

    @pl.when(pl.program_id(0) == 0)
    def _():
        cot_ref[:, lanes(tp_ref[0], feat)] = own_ref[...]
        cot_ref[:, lanes(1 - tp_ref[0], feat)] = far_ref[...]

    core = me_ref[0] % 2
    g_ref[...] = dot(cot_ref[...], w_ref[...], 1, 1).astype(BF)
    for j in range(g_ref.shape[1] // (2 * head)):
        at = slice(j * head, (j + 1) * head)
        for o_ref, side in ((send_ref, 1 - core), (mine_ref, core)):
            pick = lanes(2 * j + side, head)
            o_ref[at, :] = dot(q_ref[:, pick], g_ref[:, pick], 0, 0).astype(BF)


def pair_grad(me, tp, after, own, far, w, q, head):
    tok, feat = own.shape
    width = q.shape[1]
    step = min(4 * head, width)
    whole = pl.BlockSpec((tok, feat), lambda i, m, t: (0, 0))
    rows = pl.BlockSpec((step // 2, head), lambda i, m, t: (i, 0))
    cols = pl.BlockSpec((tok, step), lambda i, m, t: (0, i))
    sums = jax.ShapeDtypeStruct((width // 2, head), BF)
    return pl.pallas_call(
        functools.partial(pair_grad_kernel, head),
        grid_spec=pltpu.PrefetchScalarGridSpec(
            num_scalar_prefetch=2,
            grid=(width // step,),
            in_specs=[
                ANY,
                whole,
                whole,
                pl.BlockSpec((step, 2 * feat), lambda i, m, t: (i, 0)),
                cols,
            ],
            out_specs=[cols, rows, rows],
            scratch_shapes=[pltpu.VMEM((tok, 2 * feat), BF)],
        ),
        out_shape=[jax.ShapeDtypeStruct((tok, width), BF), sums, sums],
        compiler_params=params(),
        cost_estimate=cost(4 * tok * feat * width, 4 * feat * width + 4 * tok * width),
        name="out_grad",
    )(me, tp, after, own, far, w, q)


def add_kernel(after_ref, a_ref, b_ref, o_ref):
    o_ref[...] = (a_ref[...].astype(F32) + b_ref[...].astype(F32)).astype(BF)


def add_after(after, a, b):
    spec = pl.BlockSpec(a.shape, lambda: (0, 0))
    return pl.pallas_call(
        add_kernel,
        in_specs=[ANY, spec, spec],
        out_specs=spec,
        out_shape=jax.ShapeDtypeStruct(a.shape, BF),
        compiler_params=params(),
        cost_estimate=cost(0, 0),
        name="add_after",
    )(after, a, b)


def pair_key_value_kernel(head, me_ref, after_ref, q_ref, k_ref, v_ref, g_ref, s_ref, qd_ref, t_ref, ko_ref, vo_ref):
    core = me_ref[0] % 2
    half = g_ref.shape[0] // 2
    near = (s_ref[...].astype(F32) + (1 - core).astype(F32) * qd_ref[...].astype(F32)).astype(BF)
    for j in range(2):
        at = slice(j * head, (j + 1) * head)
        q, k, v, g = q_ref[:, at], k_ref[:, at], v_ref[:, at], g_ref[:, at]
        adj = jnp.where(core == j, near, t_ref[...])
        first, second = causal_apply(v, g, q, True)
        over = dot(v, adj, 1, 1)
        ko_ref[:half, at] = (first + over[:half]).astype(BF)
        ko_ref[half:, at] = (second + over[half:]).astype(BF)
        first, second = causal_apply(k, q, g, True)
        over = dot(k, adj, 1, 0)
        vo_ref[:half, at] = (first + over[:half]).astype(BF)
        vo_ref[half:, at] = (second + over[half:]).astype(BF)


def pair_key_value_grad(me, after, q, k, v, g, adjoint, qd, other, head):
    tok, width = g.shape
    spec = pl.BlockSpec((tok, 2 * head), lambda i, m: (0, i))
    rows = pl.BlockSpec((head, head), lambda i, m: (i, 0))
    shape = jax.ShapeDtypeStruct((tok, width), BF)
    return pl.pallas_call(
        functools.partial(pair_key_value_kernel, head),
        grid_spec=pltpu.PrefetchScalarGridSpec(
            num_scalar_prefetch=1,
            grid=(width // (2 * head),),
            in_specs=[ANY, spec, spec, spec, spec, rows, rows, rows],
            out_specs=[spec, spec],
        ),
        out_shape=[shape, shape],
        compiler_params=params(),
        cost_estimate=cost(0, 0),
        name="key_value_grad",
    )(me, after, q, k, v, g, adjoint, qd, other)


def local_paired(queries, keys, values, cotangent, out_weight, memory):
    head = memory.shape[2]
    n = lax.axis_size("ctx")
    me, tp = lax.axis_index("ctx"), lax.axis_index("tp")
    who, which = me.reshape(1), tp.reshape(1)
    core = (me % 2).astype(F32)
    groups = [[c for c in range(n) if c % 2 == side] for side in range(2)]

    def swap(x, bit):
        return lax.ppermute(x, "ctx", [(c, c ^ bit) for c in range(n)])

    def swap_tp(x):
        return lax.ppermute(x, "tp", [(0, 1), (1, 0)])

    def across(x):
        return lax.all_to_all(x, "ctx", 0, 0, axis_index_groups=groups, tiled=True)

    def added(x, factor, y):
        return (x.astype(F32) + factor * y.astype(F32)).astype(BF)

    far = swap_tp(cotangent)
    south = swap(cotangent, 2)

    kv_mine, kv_send = pair_sums(who, keys, values, head)
    kv_other = swap(kv_send, 1)
    chip = added(kv_mine, 1.0, kv_other)
    inner, sent = pair_intra(who, (chip,), queries, keys, values, head)
    start = lax.dynamic_index_in_dim(memory, me, 0, False)
    scanned, sent = scan_blocks(across(chip), start, n // 2, False, (inner, far, south), sent)
    state = across(scanned)

    far_south = swap_tp(south)
    grad, qd_mine, qd_send = pair_grad(who, which, scanned, cotangent, far, out_weight, queries, head)
    mine, send = pair_attended(who, grad, queries, inner, swap(sent, 1), state, kv_mine, kv_other, head)
    received = swap(send, 2)
    state_other = swap(added(state, 1.0 - core, kv_mine), 1)

    qd_other = swap(qd_send, 1)
    chip = add_after(send, qd_mine, qd_other)
    query_g = pair_query_grad(who, chip, grad, values, keys, state, kv_other, state_other, head)
    scanned, far_south = scan_blocks(
        across(chip), jnp.zeros_like(start), n // 2, True, (query_g, received), far_south
    )
    after_chip = across(scanned)
    cots = [cotangent, far, swap(cotangent, 1), swap(far, 1)]
    cots += [south, far_south, swap(south, 1), swap(far_south, 1)]

    crossing = quad_weight((scanned,), mine, received, cots, 1)
    crossed = swap(added(crossing[0], 1.0, swap(crossing[1], 4)), 8)
    same = quad_weight((crossing[0],), mine, received, cots, 0)
    neighbour = swap(same[1], 4)
    adjoint_other = swap(added(after_chip, core, qd_mine), 1)
    key_g, value_g = pair_key_value_grad(
        who, same[0], queries, keys, values, grad, after_chip, qd_other, adjoint_other, head
    )
    return query_g, key_g, value_g, final_sum(which, [same[0], neighbour, crossed])


def local_any(queries, keys, values, cotangent, out_weight, memory):
    head = memory.shape[2]
    width = queries.shape[1]
    feat = cotangent.shape[1]
    n = lax.axis_size("ctx")
    rows = width // n
    me, tp = lax.axis_index("ctx"), lax.axis_index("tp")

    far = lax.ppermute(cotangent, "tp", [(0, 1), (1, 0)])
    kv = block_sums(keys, values, head)
    start = lax.dynamic_slice_in_dim(memory.reshape(width, head), me * rows, rows, 0)
    state = carried(kv, start, "ctx", False)
    inner = intra(queries, keys, values, head)
    grad, qd = out_grad_and_sums(tp.reshape(1), cotangent, far, out_weight, queries, head)
    adjoint = carried(qd, jnp.zeros_like(start), "ctx", True)
    attended = attended_of(queries, state, inner, head)
    term = weight_term(attended, cotangent, far)
    total = lax.psum_scatter(term, "ctx", scatter_dimension=0, tiled=True)
    query_g = query_grad_of(grad, values, keys, state, head)
    key_g, value_g = key_value_grad_of(queries, keys, values, grad, adjoint, head)
    total = total.astype(F32)
    total = jnp.where(tp == 0, total, jnp.concatenate([total[:, feat:], total[:, :feat]], 1))
    return query_g, key_g, value_g, total


def local(*args):
    heads = args[5].shape[0]
    n = lax.axis_size("ctx")
    if n == heads == 16 and lax.axis_size("tp") == 2:
        return local_paired(*args)
    return local_any(*args)


def solution(mesh):
    in_specs = (
        P("ctx", "tp"),
        P("ctx", "tp"),
        P("ctx", "tp"),
        P("ctx", "tp"),
        P("tp", None),
        P("tp", None, None),
    )
    out_specs = (P("ctx", "tp"), P("ctx", "tp"), P("ctx", "tp"), P(("tp", "ctx"), None))
    return jax.shard_map(local, mesh=mesh, in_specs=in_specs, out_specs=out_specs, check_vma=False)
```

```python
import functools

import jax
import jax.numpy as jnp
from jax import lax
from jax.experimental import pallas as pl
from jax.experimental.pallas import tpu as pltpu
from jax.sharding import PartitionSpec as P

BF = jnp.bfloat16
F32 = jnp.float32
VMEM_LIMIT = 56 * 1024 * 1024


def dot(a, b, ca, cb):
    return lax.dot_general(a, b, (((ca,), (cb,)), ((), ())), preferred_element_type=F32)


def lanes(index, head):
    return pl.ds(pl.multiple_of(index * head, head), head)


def params():
    return pltpu.CompilerParams(vmem_limit_bytes=VMEM_LIMIT)


def cost(flops, nbytes):
    return pl.CostEstimate(flops=int(flops), bytes_accessed=int(nbytes), transcendentals=0)


def kv_kernel(head, a_ref, b_ref, o_ref):
    for j in range(a_ref.shape[1] // head):
        at = slice(j * head, (j + 1) * head)
        o_ref[at, :] = dot(a_ref[:, at], b_ref[:, at], 0, 0).astype(o_ref.dtype)


def block_sums(a, b, head):
    tok, width = a.shape
    step = 2 * head
    return pl.pallas_call(
        functools.partial(kv_kernel, head),
        grid=(width // step,),
        in_specs=[pl.BlockSpec((tok, step), lambda i: (0, i))] * 2,
        out_specs=pl.BlockSpec((step, head), lambda i: (i, 0)),
        out_shape=jax.ShapeDtypeStruct((width, head), BF),
        compiler_params=params(),
        cost_estimate=cost(2 * tok * width * head, 4 * tok * width),
        name="block_sums",
    )(a, b)


def masked(tok, upper):
    row = lax.broadcasted_iota(jnp.int32, (tok, tok), 0)
    col = lax.broadcasted_iota(jnp.int32, (tok, tok), 1)
    return row <= col if upper else row >= col


def causal_apply(a, b, c, upper):
    tok = a.shape[0]
    half = tok // 2
    keep = masked(half, upper)

    def tile(x, y, diagonal):
        s = dot(x, y, 1, 1)
        if diagonal:
            s = jnp.where(keep, s, 0.0)
        return s.astype(BF)

    a0, a1, b0, b1, c0, c1 = a[:half], a[half:], b[:half], b[half:], c[:half], c[half:]
    first = dot(tile(a0, b0, True), c0, 1, 0)
    second = dot(tile(a1, b1, True), c1, 1, 0)
    if upper:
        first = first + dot(tile(a0, b1, False), c1, 1, 0)
    else:
        second = second + dot(tile(a1, b0, False), c0, 1, 0)
    return first, second


def intra_kernel(head, q_ref, k_ref, v_ref, o_ref):
    half = q_ref.shape[0] // 2
    for j in range(q_ref.shape[1] // head):
        at = slice(j * head, (j + 1) * head)
        first, second = causal_apply(q_ref[:, at], k_ref[:, at], v_ref[:, at], False)
        o_ref[:half, at] = first
        o_ref[half:, at] = second


def intra(q, k, v, head):
    tok, width = q.shape
    step = 2 * head
    spec = pl.BlockSpec((tok, step), lambda i: (0, i))
    return pl.pallas_call(
        functools.partial(intra_kernel, head),
        grid=(width // step,),
        in_specs=[spec] * 3,
        out_specs=spec,
        out_shape=jax.ShapeDtypeStruct((tok, width), F32),
        compiler_params=params(),
        cost_estimate=cost(4 * tok * tok * width, 10 * tok * width),
        name="intra",
    )(q, k, v)


def grad_kernel(head, tp_ref, own_ref, far_ref, wo_ref, wf_ref, q_ref, g_ref, s_ref):
    g = dot(own_ref[...], wo_ref[...], 1, 1) + dot(far_ref[...], wf_ref[...], 1, 1)
    g = g.astype(BF)
    g_ref[...] = g
    for j in range(g.shape[1] // head):
        at = slice(j * head, (j + 1) * head)
        s_ref[at, :] = dot(q_ref[:, at], g[:, at], 0, 0).astype(s_ref.dtype)


def out_grad_and_sums(tp, own, far, w, q, head):
    tok, feat = own.shape
    width = q.shape[1]
    step = 2 * head
    whole = pl.BlockSpec((tok, feat), lambda i, t: (0, 0))
    return pl.pallas_call(
        functools.partial(grad_kernel, head),
        grid_spec=pltpu.PrefetchScalarGridSpec(
            num_scalar_prefetch=1,
            grid=(width // step,),
            in_specs=[
                whole,
                whole,
                pl.BlockSpec((step, feat), lambda i, t: (i, t[0])),
                pl.BlockSpec((step, feat), lambda i, t: (i, 1 - t[0])),
                pl.BlockSpec((tok, step), lambda i, t: (0, i)),
            ],
            out_specs=[
                pl.BlockSpec((tok, step), lambda i, t: (0, i)),
                pl.BlockSpec((step, head), lambda i, t: (i, 0)),
            ],
        ),
        out_shape=[
            jax.ShapeDtypeStruct((tok, width), BF),
            jax.ShapeDtypeStruct((width, head), BF),
        ],
        compiler_params=params(),
        cost_estimate=cost(4 * tok * feat * width, 4 * feat * width + 4 * tok * width),
        name="out_grad",
    )(tp, own, far, w, w, q)


def attended_kernel(head, q_ref, s_ref, i_ref, o_ref):
    for j in range(q_ref.shape[1] // head):
        at = slice(j * head, (j + 1) * head)
        o_ref[:, at] = (dot(q_ref[:, at], s_ref[at, :], 1, 0) + i_ref[:, at]).astype(BF)


def attended_of(q, state, inner, head):
    tok, width = q.shape
    step = 2 * head
    spec = pl.BlockSpec((tok, step), lambda i: (0, i))
    return pl.pallas_call(
        functools.partial(attended_kernel, head),
        grid=(width // step,),
        in_specs=[spec, pl.BlockSpec((step, head), lambda i: (i, 0)), spec],
        out_specs=spec,
        out_shape=jax.ShapeDtypeStruct((tok, width), BF),
        compiler_params=params(),
        cost_estimate=cost(2 * tok * head * width, 8 * tok * width),
        name="attended",
    )(q, state, inner)


def weight_kernel(a_ref, own_ref, far_ref, o_ref):
    feat = own_ref.shape[1]
    a = a_ref[...]
    o_ref[:, :feat] = dot(a, own_ref[...], 0, 0).astype(o_ref.dtype)
    o_ref[:, feat:] = dot(a, far_ref[...], 0, 0).astype(o_ref.dtype)


def weight_term(a, own, far):
    tok, width = a.shape
    feat = own.shape[1]
    step = 256
    whole = pl.BlockSpec((tok, feat), lambda i: (0, 0))
    return pl.pallas_call(
        weight_kernel,
        grid=(width // step,),
        in_specs=[pl.BlockSpec((tok, step), lambda i: (0, i)), whole, whole],
        out_specs=pl.BlockSpec((step, 2 * feat), lambda i: (i, 0)),
        out_shape=jax.ShapeDtypeStruct((width, 2 * feat), BF),
        compiler_params=params(),
        cost_estimate=cost(4 * tok * feat * width, 4 * feat * width + 2 * tok * width),
        name="weight_term",
    )(a, own, far)


def query_kernel(head, g_ref, v_ref, k_ref, s_ref, o_ref):
    half = g_ref.shape[0] // 2
    for j in range(g_ref.shape[1] // head):
        at = slice(j * head, (j + 1) * head)
        g = g_ref[:, at]
        first, second = causal_apply(g, v_ref[:, at], k_ref[:, at], False)
        carried = dot(g, s_ref[at, :], 1, 1)
        o_ref[:half, at] = (first + carried[:half]).astype(BF)
        o_ref[half:, at] = (second + carried[half:]).astype(BF)


def query_grad_of(g, v, k, state, head):
    tok, width = g.shape
    step = 2 * head
    spec = pl.BlockSpec((tok, step), lambda i: (0, i))
    return pl.pallas_call(
        functools.partial(query_kernel, head),
        grid=(width // step,),
        in_specs=[spec, spec, spec, pl.BlockSpec((step, head), lambda i: (i, 0))],
        out_specs=spec,
        out_shape=jax.ShapeDtypeStruct((tok, width), BF),
        compiler_params=params(),
        cost_estimate=cost(4 * tok * tok * width, 8 * tok * width),
        name="query_grad",
    )(g, v, k, state)


def key_value_kernel(head, q_ref, k_ref, v_ref, g_ref, a_ref, ko_ref, vo_ref):
    half = g_ref.shape[0] // 2
    for j in range(g_ref.shape[1] // head):
        at = slice(j * head, (j + 1) * head)
        q, k, v, g, adj = q_ref[:, at], k_ref[:, at], v_ref[:, at], g_ref[:, at], a_ref[at, :]
        first, second = causal_apply(v, g, q, True)
        carried = dot(v, adj, 1, 1)
        ko_ref[:half, at] = (first + carried[:half]).astype(BF)
        ko_ref[half:, at] = (second + carried[half:]).astype(BF)
        first, second = causal_apply(k, q, g, True)
        carried = dot(k, adj, 1, 0)
        vo_ref[:half, at] = (first + carried[:half]).astype(BF)
        vo_ref[half:, at] = (second + carried[half:]).astype(BF)


def key_value_grad_of(q, k, v, g, adjoint, head):
    tok, width = g.shape
    step = 2 * head
    spec = pl.BlockSpec((tok, step), lambda i: (0, i))
    shape = jax.ShapeDtypeStruct((tok, width), BF)
    return pl.pallas_call(
        functools.partial(key_value_kernel, head),
        grid=(width // step,),
        in_specs=[spec, spec, spec, spec, pl.BlockSpec((step, head), lambda i: (i, 0))],
        out_specs=[spec, spec],
        out_shape=[shape, shape],
        compiler_params=params(),
        cost_estimate=cost(8 * tok * tok * width, 12 * tok * width),
        name="key_value_grad",
    )(q, k, v, g, adjoint)


ANY = pl.BlockSpec(memory_space=pl.ANY)


def scan_kernel(n, reverse, waits, x_ref, start_ref, *refs):
    o_ref = refs[waits]
    rows = start_ref.shape[0]
    total = start_ref[...]
    for i in range(n):
        c = n - 1 - i if reverse else i
        at = slice(c * rows, (c + 1) * rows)
        o_ref[at, :] = total.astype(BF)
        total = total + x_ref[at, :].astype(F32)


def scan_blocks(x, start, n, reverse, after=(), passed=None):
    more = () if passed is None else (passed,)
    out = pl.pallas_call(
        functools.partial(scan_kernel, n, reverse, len(after) + len(more)),
        in_specs=[pl.BlockSpec(x.shape, lambda: (0, 0)), pl.BlockSpec(start.shape, lambda: (0, 0))]
        + [ANY] * (len(after) + len(more)),
        out_specs=[pl.BlockSpec(x.shape, lambda: (0, 0))] + [ANY] * len(more),
        out_shape=[jax.ShapeDtypeStruct(x.shape, BF)]
        + [jax.ShapeDtypeStruct(p.shape, p.dtype) for p in more],
        input_output_aliases={2 + len(after): 1} if more else {},
        compiler_params=params(),
        cost_estimate=cost(0, 0),
        name="scan_blocks",
    )(x, start, *after, *more)
    return out if more else out[0]


def carried(x, start, axis, reverse):
    n = lax.axis_size(axis)
    mine = lax.all_to_all(x, axis, 0, 0, tiled=True)
    return lax.all_to_all(scan_blocks(mine, start, n, reverse), axis, 0, 0, tiled=True)


def pair_sums_kernel(head, me_ref, a_ref, b_ref, mine_ref, send_ref):
    core = me_ref[0] % 2
    for j in range(a_ref.shape[1] // (2 * head)):
        at = slice(j * head, (j + 1) * head)
        for o_ref, side in ((send_ref, 1 - core), (mine_ref, core)):
            pick = lanes(2 * j + side, head)
            o_ref[at, :] = dot(a_ref[:, pick], b_ref[:, pick], 0, 0).astype(BF)


def pair_sums(me, a, b, head):
    tok, width = a.shape
    step = min(4 * head, width)
    spec = pl.BlockSpec((tok, step), lambda i, m: (0, i))
    out = pl.BlockSpec((step // 2, head), lambda i, m: (i, 0))
    shape = jax.ShapeDtypeStruct((width // 2, head), BF)
    return pl.pallas_call(
        functools.partial(pair_sums_kernel, head),
        grid_spec=pltpu.PrefetchScalarGridSpec(
            num_scalar_prefetch=1,
            grid=(width // step,),
            in_specs=[spec] * 2,
            out_specs=[out] * 2,
        ),
        out_shape=[shape] * 2,
        compiler_params=params(),
        cost_estimate=cost(2 * tok * width * head, 4 * tok * width),
        name="pair_sums",
    )(me, a, b)


def pair_intra_kernel(head, waits, me_ref, *refs):
    q_ref, k_ref, v_ref, mine_ref, send_ref = refs[waits:]
    core = me_ref[0] % 2
    half = q_ref.shape[0] // 2
    mine, other = lanes(core, head), lanes(1 - core, head)
    first, second = causal_apply(q_ref[:, other], k_ref[:, other], v_ref[:, other], False)
    send_ref[head:, :half] = first.astype(BF).T
    send_ref[head:, half:] = second.astype(BF).T
    send_ref[:head, :] = q_ref[:, other].T
    first, second = causal_apply(q_ref[:, mine], k_ref[:, mine], v_ref[:, mine], False)
    mine_ref[:, :half] = first.astype(BF).T
    mine_ref[:, half:] = second.astype(BF).T


def pair_intra(me, after, q, k, v, head):
    tok, width = q.shape
    steps = width // (2 * head)
    spec = pl.BlockSpec((tok, 2 * head), lambda i, m: (0, i))
    return pl.pallas_call(
        functools.partial(pair_intra_kernel, head, len(after)),
        grid_spec=pltpu.PrefetchScalarGridSpec(
            num_scalar_prefetch=1,
            grid=(steps,),
            in_specs=[ANY] * len(after) + [spec] * 3,
            out_specs=[
                pl.BlockSpec((head, tok), lambda i, m: (i, 0)),
                pl.BlockSpec((2 * head, tok), lambda i, m: (i, 0)),
            ],
        ),
        out_shape=[
            jax.ShapeDtypeStruct((width // 2, tok), BF),
            jax.ShapeDtypeStruct((width, tok), BF),
        ],
        compiler_params=params(),
        cost_estimate=cost(4 * tok * tok * width, 9 * tok * width),
        name="pair_intra",
    )(me, *after, q, k, v)


def pair_attended_kernel(head, me_ref, after_ref, q0_ref, q1_ref, i_ref, far_ref, s_ref, own_ref, oth_ref, mine_ref, send_ref):
    core = (me_ref[0] % 2).astype(F32)
    south = (me_ref[0] // 2) % 2
    for q_ref, side, o_ref in ((q0_ref, south, mine_ref), (q1_ref, 1 - south, send_ref)):
        rows = lanes(side, head)
        state = s_ref[rows, :].astype(F32)
        near = (state + core * oth_ref[rows, :].astype(F32)).astype(BF)
        away = (state + (1.0 - core) * own_ref[rows, :].astype(F32)).astype(BF)
        here = dot(near, q_ref[...], 0, 1) + i_ref[rows, :].astype(F32)
        there = dot(away, far_ref[lanes(2 * side, head), :], 0, 0)
        there = there + far_ref[lanes(2 * side + 1, head), :].astype(F32)
        o_ref[0, 0] = here.astype(BF)
        o_ref[0, 1] = there.astype(BF)


def pair_attended(me, after, q, inner, far, state, own, oth, head):
    tok, width = q.shape
    places = width // (4 * head)

    def place(i, m):
        return (m[0] // 4) ^ i

    rows = pl.BlockSpec((2 * head, head), lambda i, m: (place(i, m), 0))
    out = pl.BlockSpec((1, 2, head, tok), lambda i, m: (i, 0, 0, 0))
    shape = jax.ShapeDtypeStruct((places, 2, head, tok), BF)
    return pl.pallas_call(
        functools.partial(pair_attended_kernel, head),
        grid_spec=pltpu.PrefetchScalarGridSpec(
            num_scalar_prefetch=1,
            grid=(places,),
            in_specs=[
                ANY,
                pl.BlockSpec((tok, head), lambda i, m: (0, 4 * place(i, m) + m[0] % 4)),
                pl.BlockSpec((tok, head), lambda i, m: (0, 4 * place(i, m) + (m[0] % 4 ^ 2))),
                pl.BlockSpec((2 * head, tok), lambda i, m: (place(i, m), 0)),
                pl.BlockSpec((4 * head, tok), lambda i, m: (place(i, m), 0)),
            ]
            + [rows] * 3,
            out_specs=[out, out],
        ),
        out_shape=[shape, shape],
        compiler_params=params(),
        cost_estimate=cost(2 * tok * head * width, 10 * tok * width),
        name="pair_attended",
    )(me, after, q, q, inner, far, state, own, oth)


def quad_weight_kernel(waits, tp_ref, a_ref, b_ref, *refs):
    half, _, head, tok = a_ref.shape
    ins, outs = refs[:8], refs[8 + waits :]

    def product(part):
        total = None
        for k in range(4):
            block = (a_ref if k < 2 else b_ref)[:, k % 2].reshape(half * head, tok)
            term = dot(block, ins[2 * k + part][...], 1, 0)
            total = term if total is None else total + term
        for i, o_ref in enumerate(outs):
            o_ref[...] = total[i * head : (i + 1) * head].astype(BF)

    steps = pl.num_programs(0) // 2
    pl.when(pl.program_id(0) < steps)(lambda: product(0))
    pl.when(pl.program_id(0) >= steps)(lambda: product(1))


def quad_weight(tp, after, a, b, cots, far_side):
    places, _, head, tok = a.shape
    half = places // 2
    feat = cots[0].shape[1]
    step = min(512, feat)
    steps = feat // step
    whole = pl.BlockSpec((half,) + a.shape[1:], lambda i, t: (far_side, 0, 0, 0))
    own = pl.BlockSpec((tok, step), lambda i, t: (0, jnp.minimum(i, steps - 1)))
    other = pl.BlockSpec((tok, step), lambda i, t: (0, jnp.maximum(i - steps, 0)))
    return pl.pallas_call(
        functools.partial(quad_weight_kernel, len(after)),
        grid_spec=pltpu.PrefetchScalarGridSpec(
            num_scalar_prefetch=1,
            grid=(2 * steps,),
            in_specs=[whole, whole] + [own, other] * 4 + [ANY] * len(after),
            out_specs=[
                pl.BlockSpec((head, step), lambda i, t: (0, (i + t[0] * steps) % (2 * steps)))
            ]
            * half,
        ),
        out_shape=[jax.ShapeDtypeStruct((head, 2 * feat), BF)] * half,
        compiler_params=params(),
        cost_estimate=cost(16 * tok * feat * half * head * far_side, 20 * feat * tok * far_side),
        name="quad_weight",
    )(tp, a, b, *cots, *after)


def pair_query_kernel(head, me_ref, after_ref, g_ref, v_ref, k_ref, s_ref, kv_ref, t_ref, o_ref):
    core = me_ref[0] % 2
    half = g_ref.shape[0] // 2
    near = (s_ref[...].astype(F32) + core.astype(F32) * kv_ref[...].astype(F32)).astype(BF)
    for j in range(2):
        at = slice(j * head, (j + 1) * head)
        g = g_ref[:, at]
        state = jnp.where(core == j, near, t_ref[...])
        first_half, second_half = causal_apply(g, v_ref[:, at], k_ref[:, at], False)
        over = dot(g, state, 1, 1)
        o_ref[:half, at] = (first_half + over[:half]).astype(BF)
        o_ref[half:, at] = (second_half + over[half:]).astype(BF)


def pair_query_grad(me, after, g, v, k, state, kv, other, head):
    tok, width = g.shape
    spec = pl.BlockSpec((tok, 2 * head), lambda i, m: (0, i))
    rows = pl.BlockSpec((head, head), lambda i, m: (i, 0))
    return pl.pallas_call(
        functools.partial(pair_query_kernel, head),
        grid_spec=pltpu.PrefetchScalarGridSpec(
            num_scalar_prefetch=1,
            grid=(width // (2 * head),),
            in_specs=[ANY, spec, spec, spec, rows, rows, rows],
            out_specs=spec,
        ),
        out_shape=jax.ShapeDtypeStruct((tok, width), BF),
        compiler_params=params(),
        cost_estimate=cost(0, 0),
        name="query_grad",
    )(me, after, g, v, k, state, kv, other)


def pair_grad_kernel(head, waits, me_ref, tp_ref, own_ref, far_ref, w_ref, q_ref, *refs):
    g_ref, mine_ref, send_ref = refs[waits : waits + 3]
    cot_ref = refs[-1]
    feat = own_ref.shape[1]

    @pl.when(pl.program_id(0) == 0)
    def _():
        cot_ref[:, lanes(tp_ref[0], feat)] = own_ref[...]
        cot_ref[:, lanes(1 - tp_ref[0], feat)] = far_ref[...]

    core = me_ref[0] % 2
    g_ref[...] = dot(cot_ref[...], w_ref[...], 1, 1).astype(BF)
    for j in range(g_ref.shape[1] // (2 * head)):
        at = slice(j * head, (j + 1) * head)
        for o_ref, side in ((send_ref, 1 - core), (mine_ref, core)):
            pick = lanes(2 * j + side, head)
            o_ref[at, :] = dot(q_ref[:, pick], g_ref[:, pick], 0, 0).astype(BF)


def pair_grad(me, tp, part, after, passed, own, far, w, q, head):
    tok, feat = own.shape
    width = q.shape[1]
    step = min(4 * head, width // 2)
    base = part * (width // 2 // step)
    whole = pl.BlockSpec((tok, feat), lambda i, m, t: (0, 0))
    rows = pl.BlockSpec((step // 2, head), lambda i, m, t: (i + base, 0))
    cols = pl.BlockSpec((tok, step), lambda i, m, t: (0, i + base))
    sums = jax.ShapeDtypeStruct((width // 2, head), BF)
    shapes = [jax.ShapeDtypeStruct((tok, width), BF), sums, sums]
    shapes += [jax.ShapeDtypeStruct(p.shape, p.dtype) for p in passed[3:]]
    return pl.pallas_call(
        functools.partial(pair_grad_kernel, head, len(after) + len(passed)),
        grid_spec=pltpu.PrefetchScalarGridSpec(
            num_scalar_prefetch=2,
            grid=(width // 2 // step,),
            in_specs=[
                whole,
                whole,
                pl.BlockSpec((step, 2 * feat), lambda i, m, t: (i + base, 0)),
                cols,
            ]
            + [ANY] * (len(after) + len(passed)),
            out_specs=[cols, rows, rows] + [ANY] * len(passed[3:]),
            scratch_shapes=[pltpu.VMEM((tok, 2 * feat), BF)],
        ),
        out_shape=shapes,
        input_output_aliases={6 + len(after) + i: i for i in range(len(passed))},
        compiler_params=params(),
        cost_estimate=cost(2 * tok * feat * width * (1 - part), 3 * feat * width * (1 - part)),
        name="out_grad",
    )(me, tp, own, far, w, q, *after, *passed)


def pass_kernel(*refs):
    pass


def passed_after(x, after, flops):
    return pl.pallas_call(
        pass_kernel,
        in_specs=[ANY] * (1 + len(after)),
        out_specs=ANY,
        out_shape=jax.ShapeDtypeStruct(x.shape, x.dtype),
        input_output_aliases={0: 0},
        compiler_params=params(),
        cost_estimate=cost(flops, 0),
        name="passed_after",
    )(x, *after)


def add_kernel(after_ref, a_ref, b_ref, o_ref):
    o_ref[...] = (a_ref[...].astype(F32) + b_ref[...].astype(F32)).astype(BF)


def add_after(after, a, b):
    spec = pl.BlockSpec(a.shape, lambda: (0, 0))
    return pl.pallas_call(
        add_kernel,
        in_specs=[ANY, spec, spec],
        out_specs=spec,
        out_shape=jax.ShapeDtypeStruct(a.shape, BF),
        compiler_params=params(),
        cost_estimate=cost(0, 0),
        name="add_after",
    )(after, a, b)


def pair_key_value_kernel(head, me_ref, after_ref, q_ref, k_ref, v_ref, g_ref, s_ref, qd_ref, t_ref, ko_ref, vo_ref):
    core = me_ref[0] % 2
    half = g_ref.shape[0] // 2
    near = (s_ref[...].astype(F32) + (1 - core).astype(F32) * qd_ref[...].astype(F32)).astype(BF)
    for j in range(2):
        at = slice(j * head, (j + 1) * head)
        q, k, v, g = q_ref[:, at], k_ref[:, at], v_ref[:, at], g_ref[:, at]
        adj = jnp.where(core == j, near, t_ref[...])
        first, second = causal_apply(v, g, q, True)
        over = dot(v, adj, 1, 1)
        ko_ref[:half, at] = (first + over[:half]).astype(BF)
        ko_ref[half:, at] = (second + over[half:]).astype(BF)
        first, second = causal_apply(k, q, g, True)
        over = dot(k, adj, 1, 0)
        vo_ref[:half, at] = (first + over[:half]).astype(BF)
        vo_ref[half:, at] = (second + over[half:]).astype(BF)


def pair_key_value_grad(me, after, q, k, v, g, adjoint, qd, other, head):
    tok, width = g.shape
    spec = pl.BlockSpec((tok, 2 * head), lambda i, m: (0, i))
    rows = pl.BlockSpec((head, head), lambda i, m: (i, 0))
    shape = jax.ShapeDtypeStruct((tok, width), BF)
    return pl.pallas_call(
        functools.partial(pair_key_value_kernel, head),
        grid_spec=pltpu.PrefetchScalarGridSpec(
            num_scalar_prefetch=1,
            grid=(width // (2 * head),),
            in_specs=[ANY, spec, spec, spec, spec, rows, rows, rows],
            out_specs=[spec, spec],
        ),
        out_shape=[shape, shape],
        compiler_params=params(),
        cost_estimate=cost(0, 0),
        name="key_value_grad",
    )(me, after, q, k, v, g, adjoint, qd, other)


def local_paired(queries, keys, values, cotangent, out_weight, memory):
    head = memory.shape[2]
    n = lax.axis_size("ctx")
    me, tp = lax.axis_index("ctx"), lax.axis_index("tp")
    who, which = me.reshape(1), tp.reshape(1)
    core = (me % 2).astype(F32)
    groups = [[c for c in range(n) if c % 2 == side] for side in range(2)]

    def swap(x, bit):
        return lax.ppermute(x, "ctx", [(c, c ^ bit) for c in range(n)])

    def swap_tp(x):
        return lax.ppermute(x, "tp", [(0, 1), (1, 0)])

    def across(x):
        return lax.all_to_all(x, "ctx", 0, 0, axis_index_groups=groups, tiled=True)

    def added(x, factor, y):
        return (x.astype(F32) + factor * y.astype(F32)).astype(BF)

    kv_mine, kv_send = pair_sums(who, keys, values, head)
    kv_other = swap(kv_send, 1)
    far = swap_tp(cotangent)
    south = swap(cotangent, 2)
    chip = added(kv_mine, 1.0, kv_other)
    inner, sent = pair_intra(who, (chip,), queries, keys, values, head)
    start = lax.dynamic_index_in_dim(memory, me, 0, False)
    scanned, sent = scan_blocks(across(chip), start, n // 2, False, (inner, far, south), sent)
    state = across(scanned)

    far_south = swap_tp(south)
    early = pair_grad(who, which, 0, (scanned, south), (), cotangent, far, out_weight, queries, head)
    mine, send = pair_attended(
        who, early[0], queries, inner, swap(sent, 1), state, kv_mine, kv_other, head
    )
    received = swap(send, 2)
    state_other = swap(added(state, 1.0 - core, kv_mine), 1)

    grad, qd_mine, qd_send = pair_grad(
        who, which, 1, (send,), early, cotangent, far, out_weight, queries, head
    )
    qd_other = swap(qd_send, 1)
    chip = add_after(send, qd_mine, qd_other)
    query_g = pair_query_grad(who, chip, grad, values, keys, state, kv_other, state_other, head)
    received = passed_after(received, (query_g,), 2e10)
    scanned = scan_blocks(
        across(chip), jnp.zeros_like(start), n // 2, True, (query_g, received)
    )
    after_chip = across(scanned)
    cots = [cotangent, far, swap(cotangent, 1), swap(far, 1)]
    cots += [south, far_south, swap(south, 1), swap(far_south, 1)]

    crossing = quad_weight(which, (scanned,), mine, received, cots, 1)
    crossed = swap(added(crossing[0], 1.0, swap(crossing[1], 4)), 8)
    same = quad_weight(which, (crossing[0],), mine, received, cots, 0)
    neighbour = swap(same[1], 4)
    adjoint_other = swap(added(after_chip, core, qd_mine), 1)
    key_g, value_g = pair_key_value_grad(
        who, same[0], queries, keys, values, grad, after_chip, qd_other, adjoint_other, head
    )
    total = same[0].astype(F32) + neighbour.astype(F32) + crossed.astype(F32)
    return query_g, key_g, value_g, total


def local_any(queries, keys, values, cotangent, out_weight, memory):
    head = memory.shape[2]
    width = queries.shape[1]
    feat = cotangent.shape[1]
    n = lax.axis_size("ctx")
    rows = width // n
    me, tp = lax.axis_index("ctx"), lax.axis_index("tp")

    far = lax.ppermute(cotangent, "tp", [(0, 1), (1, 0)])
    kv = block_sums(keys, values, head)
    start = lax.dynamic_slice_in_dim(memory.reshape(width, head), me * rows, rows, 0)
    state = carried(kv, start, "ctx", False)
    inner = intra(queries, keys, values, head)
    grad, qd = out_grad_and_sums(tp.reshape(1), cotangent, far, out_weight, queries, head)
    adjoint = carried(qd, jnp.zeros_like(start), "ctx", True)
    attended = attended_of(queries, state, inner, head)
    term = weight_term(attended, cotangent, far)
    total = lax.psum_scatter(term, "ctx", scatter_dimension=0, tiled=True)
    query_g = query_grad_of(grad, values, keys, state, head)
    key_g, value_g = key_value_grad_of(queries, keys, values, grad, adjoint, head)
    total = total.astype(F32)
    total = jnp.where(tp == 0, total, jnp.concatenate([total[:, feat:], total[:, :feat]], 1))
    return query_g, key_g, value_g, total


def local(*args):
    heads = args[5].shape[0]
    n = lax.axis_size("ctx")
    if n == heads == 16 and lax.axis_size("tp") == 2:
        return local_paired(*args)
    return local_any(*args)


def solution(mesh):
    in_specs = (
        P("ctx", "tp"),
        P("ctx", "tp"),
        P("ctx", "tp"),
        P("ctx", "tp"),
        P("tp", None),
        P("tp", None, None),
    )
    out_specs = (P("ctx", "tp"), P("ctx", "tp"), P("ctx", "tp"), P(("tp", "ctx"), None))
    return jax.shard_map(local, mesh=mesh, in_specs=in_specs, out_specs=out_specs, check_vma=False)
```

```python
import functools

import jax
import jax.numpy as jnp
from jax import lax
from jax.experimental import pallas as pl
from jax.experimental.pallas import tpu as pltpu
from jax.sharding import PartitionSpec as P

BF = jnp.bfloat16
F32 = jnp.float32
VMEM_LIMIT = 56 * 1024 * 1024


def dot(a, b, ca, cb):
    return lax.dot_general(a, b, (((ca,), (cb,)), ((), ())), preferred_element_type=F32)


def lanes(index, head):
    return pl.ds(pl.multiple_of(index * head, head), head)


def params():
    return pltpu.CompilerParams(vmem_limit_bytes=VMEM_LIMIT)


def cost(flops, nbytes):
    return pl.CostEstimate(flops=int(flops), bytes_accessed=int(nbytes), transcendentals=0)


def kv_kernel(head, a_ref, b_ref, o_ref):
    for j in range(a_ref.shape[1] // head):
        at = slice(j * head, (j + 1) * head)
        o_ref[at, :] = dot(a_ref[:, at], b_ref[:, at], 0, 0).astype(o_ref.dtype)


def block_sums(a, b, head):
    tok, width = a.shape
    step = 2 * head
    return pl.pallas_call(
        functools.partial(kv_kernel, head),
        grid=(width // step,),
        in_specs=[pl.BlockSpec((tok, step), lambda i: (0, i))] * 2,
        out_specs=pl.BlockSpec((step, head), lambda i: (i, 0)),
        out_shape=jax.ShapeDtypeStruct((width, head), BF),
        compiler_params=params(),
        cost_estimate=cost(2 * tok * width * head, 4 * tok * width),
        name="block_sums",
    )(a, b)


def masked(tok, upper):
    row = lax.broadcasted_iota(jnp.int32, (tok, tok), 0)
    col = lax.broadcasted_iota(jnp.int32, (tok, tok), 1)
    return row <= col if upper else row >= col


def causal_apply(a, b, c, upper):
    tok = a.shape[0]
    half = tok // 2
    keep = masked(half, upper)

    def tile(x, y, diagonal):
        s = dot(x, y, 1, 1)
        if diagonal:
            s = jnp.where(keep, s, 0.0)
        return s.astype(BF)

    a0, a1, b0, b1, c0, c1 = a[:half], a[half:], b[:half], b[half:], c[:half], c[half:]
    first = dot(tile(a0, b0, True), c0, 1, 0)
    second = dot(tile(a1, b1, True), c1, 1, 0)
    if upper:
        first = first + dot(tile(a0, b1, False), c1, 1, 0)
    else:
        second = second + dot(tile(a1, b0, False), c0, 1, 0)
    return first, second


def intra_kernel(head, q_ref, k_ref, v_ref, o_ref):
    half = q_ref.shape[0] // 2
    for j in range(q_ref.shape[1] // head):
        at = slice(j * head, (j + 1) * head)
        first, second = causal_apply(q_ref[:, at], k_ref[:, at], v_ref[:, at], False)
        o_ref[:half, at] = first
        o_ref[half:, at] = second


def intra(q, k, v, head):
    tok, width = q.shape
    step = 2 * head
    spec = pl.BlockSpec((tok, step), lambda i: (0, i))
    return pl.pallas_call(
        functools.partial(intra_kernel, head),
        grid=(width // step,),
        in_specs=[spec] * 3,
        out_specs=spec,
        out_shape=jax.ShapeDtypeStruct((tok, width), F32),
        compiler_params=params(),
        cost_estimate=cost(4 * tok * tok * width, 10 * tok * width),
        name="intra",
    )(q, k, v)


def grad_kernel(head, tp_ref, own_ref, far_ref, wo_ref, wf_ref, q_ref, g_ref, s_ref):
    g = dot(own_ref[...], wo_ref[...], 1, 1) + dot(far_ref[...], wf_ref[...], 1, 1)
    g = g.astype(BF)
    g_ref[...] = g
    for j in range(g.shape[1] // head):
        at = slice(j * head, (j + 1) * head)
        s_ref[at, :] = dot(q_ref[:, at], g[:, at], 0, 0).astype(s_ref.dtype)


def out_grad_and_sums(tp, own, far, w, q, head):
    tok, feat = own.shape
    width = q.shape[1]
    step = 2 * head
    whole = pl.BlockSpec((tok, feat), lambda i, t: (0, 0))
    return pl.pallas_call(
        functools.partial(grad_kernel, head),
        grid_spec=pltpu.PrefetchScalarGridSpec(
            num_scalar_prefetch=1,
            grid=(width // step,),
            in_specs=[
                whole,
                whole,
                pl.BlockSpec((step, feat), lambda i, t: (i, t[0])),
                pl.BlockSpec((step, feat), lambda i, t: (i, 1 - t[0])),
                pl.BlockSpec((tok, step), lambda i, t: (0, i)),
            ],
            out_specs=[
                pl.BlockSpec((tok, step), lambda i, t: (0, i)),
                pl.BlockSpec((step, head), lambda i, t: (i, 0)),
            ],
        ),
        out_shape=[
            jax.ShapeDtypeStruct((tok, width), BF),
            jax.ShapeDtypeStruct((width, head), BF),
        ],
        compiler_params=params(),
        cost_estimate=cost(4 * tok * feat * width, 4 * feat * width + 4 * tok * width),
        name="out_grad",
    )(tp, own, far, w, w, q)


def attended_kernel(head, q_ref, s_ref, i_ref, o_ref):
    for j in range(q_ref.shape[1] // head):
        at = slice(j * head, (j + 1) * head)
        o_ref[:, at] = (dot(q_ref[:, at], s_ref[at, :], 1, 0) + i_ref[:, at]).astype(BF)


def attended_of(q, state, inner, head):
    tok, width = q.shape
    step = 2 * head
    spec = pl.BlockSpec((tok, step), lambda i: (0, i))
    return pl.pallas_call(
        functools.partial(attended_kernel, head),
        grid=(width // step,),
        in_specs=[spec, pl.BlockSpec((step, head), lambda i: (i, 0)), spec],
        out_specs=spec,
        out_shape=jax.ShapeDtypeStruct((tok, width), BF),
        compiler_params=params(),
        cost_estimate=cost(2 * tok * head * width, 8 * tok * width),
        name="attended",
    )(q, state, inner)


def weight_kernel(a_ref, own_ref, far_ref, o_ref):
    feat = own_ref.shape[1]
    a = a_ref[...]
    o_ref[:, :feat] = dot(a, own_ref[...], 0, 0).astype(o_ref.dtype)
    o_ref[:, feat:] = dot(a, far_ref[...], 0, 0).astype(o_ref.dtype)


def weight_term(a, own, far):
    tok, width = a.shape
    feat = own.shape[1]
    step = 256
    whole = pl.BlockSpec((tok, feat), lambda i: (0, 0))
    return pl.pallas_call(
        weight_kernel,
        grid=(width // step,),
        in_specs=[pl.BlockSpec((tok, step), lambda i: (0, i)), whole, whole],
        out_specs=pl.BlockSpec((step, 2 * feat), lambda i: (i, 0)),
        out_shape=jax.ShapeDtypeStruct((width, 2 * feat), BF),
        compiler_params=params(),
        cost_estimate=cost(4 * tok * feat * width, 4 * feat * width + 2 * tok * width),
        name="weight_term",
    )(a, own, far)


def query_kernel(head, g_ref, v_ref, k_ref, s_ref, o_ref):
    half = g_ref.shape[0] // 2
    for j in range(g_ref.shape[1] // head):
        at = slice(j * head, (j + 1) * head)
        g = g_ref[:, at]
        first, second = causal_apply(g, v_ref[:, at], k_ref[:, at], False)
        carried = dot(g, s_ref[at, :], 1, 1)
        o_ref[:half, at] = (first + carried[:half]).astype(BF)
        o_ref[half:, at] = (second + carried[half:]).astype(BF)


def query_grad_of(g, v, k, state, head):
    tok, width = g.shape
    step = 2 * head
    spec = pl.BlockSpec((tok, step), lambda i: (0, i))
    return pl.pallas_call(
        functools.partial(query_kernel, head),
        grid=(width // step,),
        in_specs=[spec, spec, spec, pl.BlockSpec((step, head), lambda i: (i, 0))],
        out_specs=spec,
        out_shape=jax.ShapeDtypeStruct((tok, width), BF),
        compiler_params=params(),
        cost_estimate=cost(4 * tok * tok * width, 8 * tok * width),
        name="query_grad",
    )(g, v, k, state)


def key_value_kernel(head, q_ref, k_ref, v_ref, g_ref, a_ref, ko_ref, vo_ref):
    half = g_ref.shape[0] // 2
    for j in range(g_ref.shape[1] // head):
        at = slice(j * head, (j + 1) * head)
        q, k, v, g, adj = q_ref[:, at], k_ref[:, at], v_ref[:, at], g_ref[:, at], a_ref[at, :]
        first, second = causal_apply(v, g, q, True)
        carried = dot(v, adj, 1, 1)
        ko_ref[:half, at] = (first + carried[:half]).astype(BF)
        ko_ref[half:, at] = (second + carried[half:]).astype(BF)
        first, second = causal_apply(k, q, g, True)
        carried = dot(k, adj, 1, 0)
        vo_ref[:half, at] = (first + carried[:half]).astype(BF)
        vo_ref[half:, at] = (second + carried[half:]).astype(BF)


def key_value_grad_of(q, k, v, g, adjoint, head):
    tok, width = g.shape
    step = 2 * head
    spec = pl.BlockSpec((tok, step), lambda i: (0, i))
    shape = jax.ShapeDtypeStruct((tok, width), BF)
    return pl.pallas_call(
        functools.partial(key_value_kernel, head),
        grid=(width // step,),
        in_specs=[spec, spec, spec, spec, pl.BlockSpec((step, head), lambda i: (i, 0))],
        out_specs=[spec, spec],
        out_shape=[shape, shape],
        compiler_params=params(),
        cost_estimate=cost(8 * tok * tok * width, 12 * tok * width),
        name="key_value_grad",
    )(q, k, v, g, adjoint)


ANY = pl.BlockSpec(memory_space=pl.ANY)


def scan_kernel(n, reverse, waits, x_ref, start_ref, *refs):
    o_ref = refs[waits]
    rows = start_ref.shape[0]
    total = start_ref[...]
    for i in range(n):
        c = n - 1 - i if reverse else i
        at = slice(c * rows, (c + 1) * rows)
        o_ref[at, :] = total.astype(BF)
        total = total + x_ref[at, :].astype(F32)


def scan_blocks(x, start, n, reverse, after=(), passed=None):
    more = () if passed is None else (passed,)
    out = pl.pallas_call(
        functools.partial(scan_kernel, n, reverse, len(after) + len(more)),
        in_specs=[pl.BlockSpec(x.shape, lambda: (0, 0)), pl.BlockSpec(start.shape, lambda: (0, 0))]
        + [ANY] * (len(after) + len(more)),
        out_specs=[pl.BlockSpec(x.shape, lambda: (0, 0))] + [ANY] * len(more),
        out_shape=[jax.ShapeDtypeStruct(x.shape, BF)]
        + [jax.ShapeDtypeStruct(p.shape, p.dtype) for p in more],
        input_output_aliases={2 + len(after): 1} if more else {},
        compiler_params=params(),
        cost_estimate=cost(0, 0),
        name="scan_blocks",
    )(x, start, *after, *more)
    return out if more else out[0]


def carried(x, start, axis, reverse):
    n = lax.axis_size(axis)
    mine = lax.all_to_all(x, axis, 0, 0, tiled=True)
    return lax.all_to_all(scan_blocks(mine, start, n, reverse), axis, 0, 0, tiled=True)


def pair_sums_kernel(head, me_ref, a_ref, b_ref, mine_ref, send_ref):
    core = me_ref[0] % 2
    for j in range(a_ref.shape[1] // (2 * head)):
        at = slice(j * head, (j + 1) * head)
        for o_ref, side in ((send_ref, 1 - core), (mine_ref, core)):
            pick = lanes(2 * j + side, head)
            o_ref[at, :] = dot(a_ref[:, pick], b_ref[:, pick], 0, 0).astype(BF)


def pair_sums(me, a, b, head):
    tok, width = a.shape
    step = min(4 * head, width)
    spec = pl.BlockSpec((tok, step), lambda i, m: (0, i))
    out = pl.BlockSpec((step // 2, head), lambda i, m: (i, 0))
    shape = jax.ShapeDtypeStruct((width // 2, head), BF)
    return pl.pallas_call(
        functools.partial(pair_sums_kernel, head),
        grid_spec=pltpu.PrefetchScalarGridSpec(
            num_scalar_prefetch=1,
            grid=(width // step,),
            in_specs=[spec] * 2,
            out_specs=[out] * 2,
        ),
        out_shape=[shape] * 2,
        compiler_params=params(),
        cost_estimate=cost(2 * tok * width * head, 4 * tok * width),
        name="pair_sums",
    )(me, a, b)


def pair_intra_kernel(head, waits, me_ref, *refs):
    q_ref, k_ref, v_ref, mine_ref, send_ref = refs[waits:]
    core = me_ref[0] % 2
    half = q_ref.shape[0] // 2
    for j in range(q_ref.shape[1] // (2 * head)):
        for o_ref, side, base in ((send_ref, 1 - core, (2 * j + 1) * head), (mine_ref, core, j * head)):
            pick = lanes(2 * j + side, head)
            first, second = causal_apply(q_ref[:, pick], k_ref[:, pick], v_ref[:, pick], False)
            o_ref[base : base + head, :half] = first.astype(BF).T
            o_ref[base : base + head, half:] = second.astype(BF).T
        send_ref[2 * j * head : (2 * j + 1) * head, :] = q_ref[:, lanes(2 * j + 1 - core, head)].T


def pair_intra(me, after, q, k, v, head):
    tok, width = q.shape
    step = min(4 * head, width)
    spec = pl.BlockSpec((tok, step), lambda i, m: (0, i))
    return pl.pallas_call(
        functools.partial(pair_intra_kernel, head, len(after)),
        grid_spec=pltpu.PrefetchScalarGridSpec(
            num_scalar_prefetch=1,
            grid=(width // step,),
            in_specs=[ANY] * len(after) + [spec] * 3,
            out_specs=[
                pl.BlockSpec((step // 2, tok), lambda i, m: (i, 0)),
                pl.BlockSpec((step, tok), lambda i, m: (i, 0)),
            ],
        ),
        out_shape=[
            jax.ShapeDtypeStruct((width // 2, tok), BF),
            jax.ShapeDtypeStruct((width, tok), BF),
        ],
        compiler_params=params(),
        cost_estimate=cost(4 * tok * tok * width, 9 * tok * width),
        name="pair_intra",
    )(me, *after, q, k, v)


def pair_attended_kernel(head, me_ref, after_ref, q0_ref, q1_ref, i_ref, far_ref, s_ref, own_ref, oth_ref,
                         mine_ref, cross_ref, near_ref):
    core = (me_ref[0] % 2).astype(F32)
    south = (me_ref[0] // 2) % 2

    def fill(q_ref, side, o_ref):
        rows = lanes(side, head)
        state = s_ref[rows, :].astype(F32)
        near = (state + core * oth_ref[rows, :].astype(F32)).astype(BF)
        away = (state + (1.0 - core) * own_ref[rows, :].astype(F32)).astype(BF)
        here = dot(near, q_ref[...], 0, 1) + i_ref[rows, :].astype(F32)
        there = dot(away, far_ref[lanes(2 * side, head), :], 0, 0)
        there = there + far_ref[lanes(2 * side + 1, head), :].astype(F32)
        o_ref[0, 0] = here.astype(BF)
        o_ref[0, 1] = there.astype(BF)

    fill(q0_ref, south, mine_ref)
    crossing = pl.program_id(0) < pl.num_programs(0) // 2
    pl.when(crossing)(lambda: fill(q1_ref, 1 - south, cross_ref))
    pl.when(jnp.logical_not(crossing))(lambda: fill(q1_ref, 1 - south, near_ref))


def pair_attended(me, after, q, inner, far, state, own, oth, head):
    tok, width = q.shape
    places = width // (4 * head)
    half = places // 2

    def place(i, m):
        return (m[0] // 4) ^ i ^ half

    rows = pl.BlockSpec((2 * head, head), lambda i, m: (place(i, m), 0))

    def out(index):
        return pl.BlockSpec((1, 2, head, tok), lambda i, m: (index(i), 0, 0, 0))

    def shape(count):
        return jax.ShapeDtypeStruct((count, 2, head, tok), BF)

    return pl.pallas_call(
        functools.partial(pair_attended_kernel, head),
        grid_spec=pltpu.PrefetchScalarGridSpec(
            num_scalar_prefetch=1,
            grid=(places,),
            in_specs=[
                ANY,
                pl.BlockSpec((tok, head), lambda i, m: (0, 4 * place(i, m) + m[0] % 4)),
                pl.BlockSpec((tok, head), lambda i, m: (0, 4 * place(i, m) + (m[0] % 4 ^ 2))),
                pl.BlockSpec((2 * head, tok), lambda i, m: (place(i, m), 0)),
                pl.BlockSpec((4 * head, tok), lambda i, m: (place(i, m), 0)),
            ]
            + [rows] * 3,
            out_specs=[
                out(lambda i: i ^ half),
                out(lambda i: jnp.minimum(i, half - 1)),
                out(lambda i: jnp.maximum(i - half, 0)),
            ],
        ),
        out_shape=[shape(places), shape(half), shape(half)],
        compiler_params=params(),
        cost_estimate=cost(2 * tok * head * width, 10 * tok * width),
        name="pair_attended",
    )(me, after, q, q, inner, far, state, own, oth)


def quad_weight_kernel(waits, tp_ref, a_ref, b_ref, *refs):
    half, _, head, tok = a_ref.shape
    ins, outs = refs[:8], refs[8 + waits :]

    def product(part):
        total = None
        for k in range(4):
            block = (a_ref if k < 2 else b_ref)[:, k % 2].reshape(half * head, tok)
            term = dot(block, ins[2 * k + part][...], 1, 0)
            total = term if total is None else total + term
        for i, o_ref in enumerate(outs):
            o_ref[...] = total[i * head : (i + 1) * head].astype(BF)

    steps = pl.num_programs(0) // 2
    pl.when(pl.program_id(0) < steps)(lambda: product(0))
    pl.when(pl.program_id(0) >= steps)(lambda: product(1))


def quad_weight(tp, after, a, b, cots, far_side):
    places, _, head, tok = a.shape
    half = places // 2
    feat = cots[0].shape[1]
    step = min(512, feat)
    steps = feat // step
    whole = pl.BlockSpec((half,) + a.shape[1:], lambda i, t: (far_side, 0, 0, 0))
    own = pl.BlockSpec((tok, step), lambda i, t: (0, jnp.minimum(i, steps - 1)))
    other = pl.BlockSpec((tok, step), lambda i, t: (0, jnp.maximum(i - steps, 0)))
    return pl.pallas_call(
        functools.partial(quad_weight_kernel, len(after)),
        grid_spec=pltpu.PrefetchScalarGridSpec(
            num_scalar_prefetch=1,
            grid=(2 * steps,),
            in_specs=[whole, pl.BlockSpec(b.shape, lambda i, t: (0, 0, 0, 0))] + [own, other] * 4 + [ANY] * len(after),
            out_specs=[
                pl.BlockSpec((head, step), lambda i, t: (0, (i + t[0] * steps) % (2 * steps)))
            ]
            * half,
        ),
        out_shape=[jax.ShapeDtypeStruct((head, 2 * feat), BF)] * half,
        compiler_params=params(),
        cost_estimate=cost(2e10, 0),
        name="quad_weight",
    )(tp, a, b, *cots, *after)


def pair_query_kernel(head, me_ref, after_ref, g_ref, v_ref, k_ref, s_ref, kv_ref, t_ref, o_ref):
    core = me_ref[0] % 2
    half = g_ref.shape[0] // 2
    for j in range(g_ref.shape[1] // head):
        at, row = slice(j * head, (j + 1) * head), slice(j // 2 * head, (j // 2 + 1) * head)
        g = g_ref[:, at]
        near = s_ref[row, :].astype(F32) + core.astype(F32) * kv_ref[row, :].astype(F32)
        state = jnp.where(core == j % 2, near.astype(BF), t_ref[row, :])
        first_half, second_half = causal_apply(g, v_ref[:, at], k_ref[:, at], False)
        over = dot(g, state, 1, 1)
        o_ref[:half, at] = (first_half + over[:half]).astype(BF)
        o_ref[half:, at] = (second_half + over[half:]).astype(BF)


def pair_query_grad(me, after, g, v, k, state, kv, other, head):
    tok, width = g.shape
    step = min(4 * head, width)
    spec = pl.BlockSpec((tok, step), lambda i, m: (0, i))
    rows = pl.BlockSpec((step // 2, head), lambda i, m: (i, 0))
    return pl.pallas_call(
        functools.partial(pair_query_kernel, head),
        grid_spec=pltpu.PrefetchScalarGridSpec(
            num_scalar_prefetch=1,
            grid=(width // step,),
            in_specs=[ANY, spec, spec, spec, rows, rows, rows],
            out_specs=spec,
        ),
        out_shape=jax.ShapeDtypeStruct((tok, width), BF),
        compiler_params=params(),
        cost_estimate=cost(0, 0),
        name="query_grad",
    )(me, after, g, v, k, state, kv, other)


def pair_grad_kernel(head, waits, me_ref, tp_ref, own_ref, far_ref, w_ref, q_ref, *refs):
    g_ref, mine_ref, send_ref = refs[waits : waits + 3]
    cot_ref = refs[-1]
    feat = own_ref.shape[1]

    @pl.when(pl.program_id(0) == 0)
    def _():
        cot_ref[:, lanes(tp_ref[0], feat)] = own_ref[...]
        cot_ref[:, lanes(1 - tp_ref[0], feat)] = far_ref[...]

    core = me_ref[0] % 2
    g_ref[...] = dot(cot_ref[...], w_ref[...], 1, 1).astype(BF)
    for j in range(g_ref.shape[1] // (2 * head)):
        at = slice(j * head, (j + 1) * head)
        for o_ref, side in ((send_ref, 1 - core), (mine_ref, core)):
            pick = lanes(2 * j + side, head)
            o_ref[at, :] = dot(q_ref[:, pick], g_ref[:, pick], 0, 0).astype(BF)


def pair_grad(me, tp, part, after, passed, own, far, w, q, head):
    tok, feat = own.shape
    width = q.shape[1]
    step = min(4 * head, width // 2)
    base = part * (width // 2 // step)
    whole = pl.BlockSpec((tok, feat), lambda i, m, t: (0, 0))
    rows = pl.BlockSpec((step // 2, head), lambda i, m, t: (i + base, 0))
    cols = pl.BlockSpec((tok, step), lambda i, m, t: (0, i + base))
    sums = jax.ShapeDtypeStruct((width // 2, head), BF)
    shapes = [jax.ShapeDtypeStruct((tok, width), BF), sums, sums]
    shapes += [jax.ShapeDtypeStruct(p.shape, p.dtype) for p in passed[3:]]
    return pl.pallas_call(
        functools.partial(pair_grad_kernel, head, len(after) + len(passed)),
        grid_spec=pltpu.PrefetchScalarGridSpec(
            num_scalar_prefetch=2,
            grid=(width // 2 // step,),
            in_specs=[
                whole,
                whole,
                pl.BlockSpec((step, 2 * feat), lambda i, m, t: (i + base, 0)),
                cols,
            ]
            + [ANY] * (len(after) + len(passed)),
            out_specs=[cols, rows, rows] + [ANY] * len(passed[3:]),
            scratch_shapes=[pltpu.VMEM((tok, 2 * feat), BF)],
        ),
        out_shape=shapes,
        input_output_aliases={6 + len(after) + i: i for i in range(len(passed))},
        compiler_params=params(),
        cost_estimate=cost(2 * tok * feat * width * (1 - part), 3 * feat * width * (1 - part)),
        name="out_grad",
    )(me, tp, own, far, w, q, *after, *passed)


def pass_kernel(*refs):
    pass


def passed_after(x, after, flops):
    return pl.pallas_call(
        pass_kernel,
        in_specs=[ANY] * (1 + len(after)),
        out_specs=ANY,
        out_shape=jax.ShapeDtypeStruct(x.shape, x.dtype),
        input_output_aliases={0: 0},
        compiler_params=params(),
        cost_estimate=cost(flops, 0),
        name="passed_after",
    )(x, *after)


def add_kernel(after_ref, a_ref, b_ref, o_ref):
    o_ref[...] = (a_ref[...].astype(F32) + b_ref[...].astype(F32)).astype(BF)


def add_after(after, a, b):
    spec = pl.BlockSpec(a.shape, lambda: (0, 0))
    return pl.pallas_call(
        add_kernel,
        in_specs=[ANY, spec, spec],
        out_specs=spec,
        out_shape=jax.ShapeDtypeStruct(a.shape, BF),
        compiler_params=params(),
        cost_estimate=cost(0, 0),
        name="add_after",
    )(after, a, b)


def pair_key_value_kernel(head, me_ref, after_ref, q_ref, k_ref, v_ref, g_ref, s_ref, qd_ref, t_ref, ko_ref, vo_ref):
    core = me_ref[0] % 2
    half = g_ref.shape[0] // 2
    for j in range(g_ref.shape[1] // head):
        at, row = slice(j * head, (j + 1) * head), slice(j // 2 * head, (j // 2 + 1) * head)
        near = s_ref[row, :].astype(F32) + (1 - core).astype(F32) * qd_ref[row, :].astype(F32)
        q, k, v, g = q_ref[:, at], k_ref[:, at], v_ref[:, at], g_ref[:, at]
        adj = jnp.where(core == j % 2, near.astype(BF), t_ref[row, :])
        first, second = causal_apply(v, g, q, True)
        over = dot(v, adj, 1, 1)
        ko_ref[:half, at] = (first + over[:half]).astype(BF)
        ko_ref[half:, at] = (second + over[half:]).astype(BF)
        first, second = causal_apply(k, q, g, True)
        over = dot(k, adj, 1, 0)
        vo_ref[:half, at] = (first + over[:half]).astype(BF)
        vo_ref[half:, at] = (second + over[half:]).astype(BF)


def pair_key_value_grad(me, after, q, k, v, g, adjoint, qd, other, head):
    tok, width = g.shape
    step = min(4 * head, width)
    spec = pl.BlockSpec((tok, step), lambda i, m: (0, i))
    rows = pl.BlockSpec((step // 2, head), lambda i, m: (i, 0))
    shape = jax.ShapeDtypeStruct((tok, width), BF)
    return pl.pallas_call(
        functools.partial(pair_key_value_kernel, head),
        grid_spec=pltpu.PrefetchScalarGridSpec(
            num_scalar_prefetch=1,
            grid=(width // step,),
            in_specs=[ANY, spec, spec, spec, spec, rows, rows, rows],
            out_specs=[spec, spec],
        ),
        out_shape=[shape, shape],
        compiler_params=params(),
        cost_estimate=cost(0, 0),
        name="key_value_grad",
    )(me, after, q, k, v, g, adjoint, qd, other)


def local_paired(queries, keys, values, cotangent, out_weight, memory):
    head = memory.shape[2]
    n = lax.axis_size("ctx")
    me, tp = lax.axis_index("ctx"), lax.axis_index("tp")
    who, which = me.reshape(1), tp.reshape(1)
    core = (me % 2).astype(F32)
    groups = [[c for c in range(n) if c % 2 == side] for side in range(2)]

    def swap(x, bit):
        return lax.ppermute(x, "ctx", [(c, c ^ bit) for c in range(n)])

    def swap_tp(x):
        return lax.ppermute(x, "tp", [(0, 1), (1, 0)])

    def across(x):
        return lax.all_to_all(x, "ctx", 0, 0, axis_index_groups=groups, tiled=True)

    def added(x, factor, y):
        return (x.astype(F32) + factor * y.astype(F32)).astype(BF)

    kv_mine, kv_send = pair_sums(who, keys, values, head)
    kv_other = swap(kv_send, 1)
    far = swap_tp(cotangent)
    south = swap(cotangent, 2)
    chip = added(kv_mine, 1.0, kv_other)
    inner, sent = pair_intra(who, (chip,), queries, keys, values, head)
    start = lax.dynamic_index_in_dim(memory, me, 0, False)
    scanned, sent = scan_blocks(across(chip), start, n // 2, False, (inner, far, south), sent)
    state = across(scanned)

    far_south = swap_tp(south)
    early = pair_grad(who, which, 0, (scanned, south), (), cotangent, far, out_weight, queries, head)
    mine, send, send_near = pair_attended(
        who, early[0], queries, inner, swap(sent, 1), state, kv_mine, kv_other, head
    )
    received, received_near = swap(send, 2), swap(send_near, 2)
    state_other = swap(added(state, 1.0 - core, kv_mine), 1)

    grad, qd_mine, qd_send = pair_grad(
        who, which, 1, (send,), early, cotangent, far, out_weight, queries, head
    )
    qd_other = swap(qd_send, 1)
    chip = add_after(send, qd_mine, qd_other)
    cots = [cotangent, far, swap(cotangent, 1), swap(far, 1)]
    cots += [south, far_south, swap(south, 1), swap(far_south, 1)]

    received = passed_after(received, (chip, state_other), 2e10)
    crossing = quad_weight(which, (), mine, received, cots, 1)
    summed = added(crossing[0], 1.0, swap(crossing[1], 4))
    crossed = swap(summed, 8)
    scanned = scan_blocks(across(chip), jnp.zeros_like(start), n // 2, True, (crossing[0],))
    after_chip = across(scanned)
    same = quad_weight(which, (scanned,), mine, received_near, cots, 0)
    neighbour = swap(same[1], 4)
    query_g = pair_query_grad(who, summed, grad, values, keys, state, kv_other, state_other, head)
    after_chip = passed_after(after_chip, (query_g,), 0)
    adjoint_other = swap(added(after_chip, core, qd_mine), 1)
    key_g, value_g = pair_key_value_grad(
        who, query_g, queries, keys, values, grad, after_chip, qd_other, adjoint_other, head
    )
    total = same[0].astype(F32) + neighbour.astype(F32) + crossed.astype(F32)
    return query_g, key_g, value_g, total


def local_any(queries, keys, values, cotangent, out_weight, memory):
    head = memory.shape[2]
    width = queries.shape[1]
    feat = cotangent.shape[1]
    n = lax.axis_size("ctx")
    rows = width // n
    me, tp = lax.axis_index("ctx"), lax.axis_index("tp")

    far = lax.ppermute(cotangent, "tp", [(0, 1), (1, 0)])
    kv = block_sums(keys, values, head)
    start = lax.dynamic_slice_in_dim(memory.reshape(width, head), me * rows, rows, 0)
    state = carried(kv, start, "ctx", False)
    inner = intra(queries, keys, values, head)
    grad, qd = out_grad_and_sums(tp.reshape(1), cotangent, far, out_weight, queries, head)
    adjoint = carried(qd, jnp.zeros_like(start), "ctx", True)
    attended = attended_of(queries, state, inner, head)
    term = weight_term(attended, cotangent, far)
    total = lax.psum_scatter(term, "ctx", scatter_dimension=0, tiled=True)
    query_g = query_grad_of(grad, values, keys, state, head)
    key_g, value_g = key_value_grad_of(queries, keys, values, grad, adjoint, head)
    total = total.astype(F32)
    total = jnp.where(tp == 0, total, jnp.concatenate([total[:, feat:], total[:, :feat]], 1))
    return query_g, key_g, value_g, total


def local(*args):
    heads = args[5].shape[0]
    n = lax.axis_size("ctx")
    if n == heads == 16 and lax.axis_size("tp") == 2:
        return local_paired(*args)
    return local_any(*args)


def solution(mesh):
    in_specs = (
        P("ctx", "tp"),
        P("ctx", "tp"),
        P("ctx", "tp"),
        P("ctx", "tp"),
        P("tp", None),
        P("tp", None, None),
    )
    out_specs = (P("ctx", "tp"), P("ctx", "tp"), P("ctx", "tp"), P(("tp", "ctx"), None))
    return jax.shard_map(local, mesh=mesh, in_specs=in_specs, out_specs=out_specs, check_vma=False)
```

```python
import functools

import jax
import jax.numpy as jnp
from jax import lax
from jax.experimental import pallas as pl
from jax.experimental.pallas import tpu as pltpu
from jax.sharding import PartitionSpec as P

BF = jnp.bfloat16
F32 = jnp.float32
NEAR = 0
SCAN = 2e10
VMEM_LIMIT = 56 * 1024 * 1024


def dot(a, b, ca, cb):
    return lax.dot_general(a, b, (((ca,), (cb,)), ((), ())), preferred_element_type=F32)


def lanes(index, head):
    return pl.ds(pl.multiple_of(index * head, head), head)


def params():
    return pltpu.CompilerParams(vmem_limit_bytes=VMEM_LIMIT)


def cost(flops, nbytes):
    return pl.CostEstimate(flops=int(flops), bytes_accessed=int(nbytes), transcendentals=0)


def kv_kernel(head, a_ref, b_ref, o_ref):
    for j in range(a_ref.shape[1] // head):
        at = slice(j * head, (j + 1) * head)
        o_ref[at, :] = dot(a_ref[:, at], b_ref[:, at], 0, 0).astype(o_ref.dtype)


def block_sums(a, b, head):
    tok, width = a.shape
    step = 2 * head
    return pl.pallas_call(
        functools.partial(kv_kernel, head),
        grid=(width // step,),
        in_specs=[pl.BlockSpec((tok, step), lambda i: (0, i))] * 2,
        out_specs=pl.BlockSpec((step, head), lambda i: (i, 0)),
        out_shape=jax.ShapeDtypeStruct((width, head), BF),
        compiler_params=params(),
        cost_estimate=cost(2 * tok * width * head, 4 * tok * width),
        name="block_sums",
    )(a, b)


def masked(tok, upper):
    row = lax.broadcasted_iota(jnp.int32, (tok, tok), 0)
    col = lax.broadcasted_iota(jnp.int32, (tok, tok), 1)
    return row <= col if upper else row >= col


def causal_apply(a, b, c, upper):
    tok = a.shape[0]
    half = tok // 2
    keep = masked(half, upper)

    def tile(x, y, diagonal):
        s = dot(x, y, 1, 1)
        if diagonal:
            s = jnp.where(keep, s, 0.0)
        return s.astype(BF)

    a0, a1, b0, b1, c0, c1 = a[:half], a[half:], b[:half], b[half:], c[:half], c[half:]
    first = dot(tile(a0, b0, True), c0, 1, 0)
    second = dot(tile(a1, b1, True), c1, 1, 0)
    if upper:
        first = first + dot(tile(a0, b1, False), c1, 1, 0)
    else:
        second = second + dot(tile(a1, b0, False), c0, 1, 0)
    return first, second


def intra_kernel(head, q_ref, k_ref, v_ref, o_ref):
    half = q_ref.shape[0] // 2
    for j in range(q_ref.shape[1] // head):
        at = slice(j * head, (j + 1) * head)
        first, second = causal_apply(q_ref[:, at], k_ref[:, at], v_ref[:, at], False)
        o_ref[:half, at] = first
        o_ref[half:, at] = second


def intra(q, k, v, head):
    tok, width = q.shape
    step = 2 * head
    spec = pl.BlockSpec((tok, step), lambda i: (0, i))
    return pl.pallas_call(
        functools.partial(intra_kernel, head),
        grid=(width // step,),
        in_specs=[spec] * 3,
        out_specs=spec,
        out_shape=jax.ShapeDtypeStruct((tok, width), F32),
        compiler_params=params(),
        cost_estimate=cost(4 * tok * tok * width, 10 * tok * width),
        name="intra",
    )(q, k, v)


def grad_kernel(head, tp_ref, own_ref, far_ref, wo_ref, wf_ref, q_ref, g_ref, s_ref):
    g = dot(own_ref[...], wo_ref[...], 1, 1) + dot(far_ref[...], wf_ref[...], 1, 1)
    g = g.astype(BF)
    g_ref[...] = g
    for j in range(g.shape[1] // head):
        at = slice(j * head, (j + 1) * head)
        s_ref[at, :] = dot(q_ref[:, at], g[:, at], 0, 0).astype(s_ref.dtype)


def out_grad_and_sums(tp, own, far, w, q, head):
    tok, feat = own.shape
    width = q.shape[1]
    step = 2 * head
    whole = pl.BlockSpec((tok, feat), lambda i, t: (0, 0))
    return pl.pallas_call(
        functools.partial(grad_kernel, head),
        grid_spec=pltpu.PrefetchScalarGridSpec(
            num_scalar_prefetch=1,
            grid=(width // step,),
            in_specs=[
                whole,
                whole,
                pl.BlockSpec((step, feat), lambda i, t: (i, t[0])),
                pl.BlockSpec((step, feat), lambda i, t: (i, 1 - t[0])),
                pl.BlockSpec((tok, step), lambda i, t: (0, i)),
            ],
            out_specs=[
                pl.BlockSpec((tok, step), lambda i, t: (0, i)),
                pl.BlockSpec((step, head), lambda i, t: (i, 0)),
            ],
        ),
        out_shape=[
            jax.ShapeDtypeStruct((tok, width), BF),
            jax.ShapeDtypeStruct((width, head), BF),
        ],
        compiler_params=params(),
        cost_estimate=cost(4 * tok * feat * width, 4 * feat * width + 4 * tok * width),
        name="out_grad",
    )(tp, own, far, w, w, q)


def attended_kernel(head, q_ref, s_ref, i_ref, o_ref):
    for j in range(q_ref.shape[1] // head):
        at = slice(j * head, (j + 1) * head)
        o_ref[:, at] = (dot(q_ref[:, at], s_ref[at, :], 1, 0) + i_ref[:, at]).astype(BF)


def attended_of(q, state, inner, head):
    tok, width = q.shape
    step = 2 * head
    spec = pl.BlockSpec((tok, step), lambda i: (0, i))
    return pl.pallas_call(
        functools.partial(attended_kernel, head),
        grid=(width // step,),
        in_specs=[spec, pl.BlockSpec((step, head), lambda i: (i, 0)), spec],
        out_specs=spec,
        out_shape=jax.ShapeDtypeStruct((tok, width), BF),
        compiler_params=params(),
        cost_estimate=cost(2 * tok * head * width, 8 * tok * width),
        name="attended",
    )(q, state, inner)


def weight_kernel(a_ref, own_ref, far_ref, o_ref):
    feat = own_ref.shape[1]
    a = a_ref[...]
    o_ref[:, :feat] = dot(a, own_ref[...], 0, 0).astype(o_ref.dtype)
    o_ref[:, feat:] = dot(a, far_ref[...], 0, 0).astype(o_ref.dtype)


def weight_term(a, own, far):
    tok, width = a.shape
    feat = own.shape[1]
    step = 256
    whole = pl.BlockSpec((tok, feat), lambda i: (0, 0))
    return pl.pallas_call(
        weight_kernel,
        grid=(width // step,),
        in_specs=[pl.BlockSpec((tok, step), lambda i: (0, i)), whole, whole],
        out_specs=pl.BlockSpec((step, 2 * feat), lambda i: (i, 0)),
        out_shape=jax.ShapeDtypeStruct((width, 2 * feat), BF),
        compiler_params=params(),
        cost_estimate=cost(4 * tok * feat * width, 4 * feat * width + 2 * tok * width),
        name="weight_term",
    )(a, own, far)


def query_kernel(head, g_ref, v_ref, k_ref, s_ref, o_ref):
    half = g_ref.shape[0] // 2
    for j in range(g_ref.shape[1] // head):
        at = slice(j * head, (j + 1) * head)
        g = g_ref[:, at]
        first, second = causal_apply(g, v_ref[:, at], k_ref[:, at], False)
        carried = dot(g, s_ref[at, :], 1, 1)
        o_ref[:half, at] = (first + carried[:half]).astype(BF)
        o_ref[half:, at] = (second + carried[half:]).astype(BF)


def query_grad_of(g, v, k, state, head):
    tok, width = g.shape
    step = 2 * head
    spec = pl.BlockSpec((tok, step), lambda i: (0, i))
    return pl.pallas_call(
        functools.partial(query_kernel, head),
        grid=(width // step,),
        in_specs=[spec, spec, spec, pl.BlockSpec((step, head), lambda i: (i, 0))],
        out_specs=spec,
        out_shape=jax.ShapeDtypeStruct((tok, width), BF),
        compiler_params=params(),
        cost_estimate=cost(4 * tok * tok * width, 8 * tok * width),
        name="query_grad",
    )(g, v, k, state)


def key_value_kernel(head, q_ref, k_ref, v_ref, g_ref, a_ref, ko_ref, vo_ref):
    half = g_ref.shape[0] // 2
    for j in range(g_ref.shape[1] // head):
        at = slice(j * head, (j + 1) * head)
        q, k, v, g, adj = q_ref[:, at], k_ref[:, at], v_ref[:, at], g_ref[:, at], a_ref[at, :]
        first, second = causal_apply(v, g, q, True)
        carried = dot(v, adj, 1, 1)
        ko_ref[:half, at] = (first + carried[:half]).astype(BF)
        ko_ref[half:, at] = (second + carried[half:]).astype(BF)
        first, second = causal_apply(k, q, g, True)
        carried = dot(k, adj, 1, 0)
        vo_ref[:half, at] = (first + carried[:half]).astype(BF)
        vo_ref[half:, at] = (second + carried[half:]).astype(BF)


def key_value_grad_of(q, k, v, g, adjoint, head):
    tok, width = g.shape
    step = 2 * head
    spec = pl.BlockSpec((tok, step), lambda i: (0, i))
    shape = jax.ShapeDtypeStruct((tok, width), BF)
    return pl.pallas_call(
        functools.partial(key_value_kernel, head),
        grid=(width // step,),
        in_specs=[spec, spec, spec, spec, pl.BlockSpec((step, head), lambda i: (i, 0))],
        out_specs=[spec, spec],
        out_shape=[shape, shape],
        compiler_params=params(),
        cost_estimate=cost(8 * tok * tok * width, 12 * tok * width),
        name="key_value_grad",
    )(q, k, v, g, adjoint)


ANY = pl.BlockSpec(memory_space=pl.ANY)


def scan_kernel(n, reverse, waits, x_ref, start_ref, *refs):
    o_ref = refs[waits]
    rows = start_ref.shape[0]
    total = start_ref[...]
    for i in range(n):
        c = n - 1 - i if reverse else i
        at = slice(c * rows, (c + 1) * rows)
        o_ref[at, :] = total.astype(BF)
        total = total + x_ref[at, :].astype(F32)


def scan_blocks(x, start, n, reverse, after=(), passed=None):
    more = () if passed is None else (passed,)
    out = pl.pallas_call(
        functools.partial(scan_kernel, n, reverse, len(after) + len(more)),
        in_specs=[pl.BlockSpec(x.shape, lambda: (0, 0)), pl.BlockSpec(start.shape, lambda: (0, 0))]
        + [ANY] * (len(after) + len(more)),
        out_specs=[pl.BlockSpec(x.shape, lambda: (0, 0))] + [ANY] * len(more),
        out_shape=[jax.ShapeDtypeStruct(x.shape, BF)]
        + [jax.ShapeDtypeStruct(p.shape, p.dtype) for p in more],
        input_output_aliases={2 + len(after): 1} if more else {},
        compiler_params=params(),
        cost_estimate=cost(SCAN, 0),
        name="scan_blocks",
    )(x, start, *after, *more)
    return out if more else out[0]


def carried(x, start, axis, reverse):
    n = lax.axis_size(axis)
    mine = lax.all_to_all(x, axis, 0, 0, tiled=True)
    return lax.all_to_all(scan_blocks(mine, start, n, reverse), axis, 0, 0, tiled=True)


def pair_sums_kernel(head, me_ref, a_ref, b_ref, mine_ref, send_ref):
    core = me_ref[0] % 2
    for j in range(a_ref.shape[1] // (2 * head)):
        at = slice(j * head, (j + 1) * head)
        for o_ref, side in ((send_ref, 1 - core), (mine_ref, core)):
            pick = lanes(2 * j + side, head)
            o_ref[at, :] = dot(a_ref[:, pick], b_ref[:, pick], 0, 0).astype(BF)


def pair_sums(me, a, b, head):
    tok, width = a.shape
    step = min(4 * head, width)
    spec = pl.BlockSpec((tok, step), lambda i, m: (0, i))
    out = pl.BlockSpec((step // 2, head), lambda i, m: (i, 0))
    shape = jax.ShapeDtypeStruct((width // 2, head), BF)
    return pl.pallas_call(
        functools.partial(pair_sums_kernel, head),
        grid_spec=pltpu.PrefetchScalarGridSpec(
            num_scalar_prefetch=1,
            grid=(width // step,),
            in_specs=[spec] * 2,
            out_specs=[out] * 2,
        ),
        out_shape=[shape] * 2,
        compiler_params=params(),
        cost_estimate=cost(2 * tok * width * head, 4 * tok * width),
        name="pair_sums",
    )(me, a, b)


def pair_intra_kernel(head, waits, me_ref, *refs):
    q_ref, k_ref, v_ref, mine_ref, send_ref = refs[waits:]
    core = me_ref[0] % 2
    half = q_ref.shape[0] // 2
    for j in range(q_ref.shape[1] // (2 * head)):
        for o_ref, side, base in ((send_ref, 1 - core, (2 * j + 1) * head), (mine_ref, core, j * head)):
            pick = lanes(2 * j + side, head)
            first, second = causal_apply(q_ref[:, pick], k_ref[:, pick], v_ref[:, pick], False)
            o_ref[base : base + head, :half] = first.astype(BF).T
            o_ref[base : base + head, half:] = second.astype(BF).T
        send_ref[2 * j * head : (2 * j + 1) * head, :] = q_ref[:, lanes(2 * j + 1 - core, head)].T


def pair_intra(me, after, q, k, v, head):
    tok, width = q.shape
    step = min(4 * head, width)
    spec = pl.BlockSpec((tok, step), lambda i, m: (0, i))
    return pl.pallas_call(
        functools.partial(pair_intra_kernel, head, len(after)),
        grid_spec=pltpu.PrefetchScalarGridSpec(
            num_scalar_prefetch=1,
            grid=(width // step,),
            in_specs=[ANY] * len(after) + [spec] * 3,
            out_specs=[
                pl.BlockSpec((step // 2, tok), lambda i, m: (i, 0)),
                pl.BlockSpec((step, tok), lambda i, m: (i, 0)),
            ],
        ),
        out_shape=[
            jax.ShapeDtypeStruct((width // 2, tok), BF),
            jax.ShapeDtypeStruct((width, tok), BF),
        ],
        compiler_params=params(),
        cost_estimate=cost(4 * tok * tok * width, 9 * tok * width),
        name="pair_intra",
    )(me, *after, q, k, v)


def pair_attended_kernel(head, me_ref, after_ref, q0_ref, q1_ref, i_ref, far_ref, s_ref, own_ref, oth_ref,
                         mine_ref, cross_ref, near_ref):
    core = (me_ref[0] % 2).astype(F32)
    south = (me_ref[0] // 2) % 2

    def fill(q_ref, side, o_ref):
        rows = lanes(side, head)
        state = s_ref[rows, :].astype(F32)
        near = (state + core * oth_ref[rows, :].astype(F32)).astype(BF)
        away = (state + (1.0 - core) * own_ref[rows, :].astype(F32)).astype(BF)
        here = dot(near, q_ref[...], 0, 1) + i_ref[rows, :].astype(F32)
        there = dot(away, far_ref[lanes(2 * side, head), :], 0, 0)
        there = there + far_ref[lanes(2 * side + 1, head), :].astype(F32)
        o_ref[0, 0] = here.astype(BF)
        o_ref[0, 1] = there.astype(BF)

    fill(q0_ref, south, mine_ref)
    crossing = pl.program_id(0) < pl.num_programs(0) // 2
    pl.when(crossing)(lambda: fill(q1_ref, 1 - south, cross_ref))
    pl.when(jnp.logical_not(crossing))(lambda: fill(q1_ref, 1 - south, near_ref))


def pair_attended(me, after, q, inner, far, state, own, oth, head):
    tok, width = q.shape
    places = width // (4 * head)
    half = places // 2

    def place(i, m):
        return (m[0] // 4) ^ i ^ half

    rows = pl.BlockSpec((2 * head, head), lambda i, m: (place(i, m), 0))

    def out(index):
        return pl.BlockSpec((1, 2, head, tok), lambda i, m: (index(i), 0, 0, 0))

    def shape(count):
        return jax.ShapeDtypeStruct((count, 2, head, tok), BF)

    return pl.pallas_call(
        functools.partial(pair_attended_kernel, head),
        grid_spec=pltpu.PrefetchScalarGridSpec(
            num_scalar_prefetch=1,
            grid=(places,),
            in_specs=[
                ANY,
                pl.BlockSpec((tok, head), lambda i, m: (0, 4 * place(i, m) + m[0] % 4)),
                pl.BlockSpec((tok, head), lambda i, m: (0, 4 * place(i, m) + (m[0] % 4 ^ 2))),
                pl.BlockSpec((2 * head, tok), lambda i, m: (place(i, m), 0)),
                pl.BlockSpec((4 * head, tok), lambda i, m: (place(i, m), 0)),
            ]
            + [rows] * 3,
            out_specs=[
                out(lambda i: i ^ half),
                out(lambda i: jnp.minimum(i, half - 1)),
                out(lambda i: jnp.maximum(i - half, 0)),
            ],
        ),
        out_shape=[shape(places), shape(half), shape(half)],
        compiler_params=params(),
        cost_estimate=cost(2 * tok * head * width, 10 * tok * width),
        name="pair_attended",
    )(me, after, q, q, inner, far, state, own, oth)


def quad_weight_kernel(waits, tp_ref, a_ref, b_ref, *refs):
    half, _, head, tok = a_ref.shape
    ins, outs = refs[:8], refs[8 + waits :]

    def product(part):
        total = None
        for k in range(4):
            block = (a_ref if k < 2 else b_ref)[:, k % 2].reshape(half * head, tok)
            term = dot(block, ins[2 * k + part][...], 1, 0)
            total = term if total is None else total + term
        for i, o_ref in enumerate(outs):
            o_ref[...] = total[i * head : (i + 1) * head].astype(BF)

    steps = pl.num_programs(0) // 2
    pl.when(pl.program_id(0) < steps)(lambda: product(0))
    pl.when(pl.program_id(0) >= steps)(lambda: product(1))


def quad_weight(tp, after, a, b, cots, far_side):
    places, _, head, tok = a.shape
    half = places // 2
    feat = cots[0].shape[1]
    step = min(512, feat)
    steps = feat // step
    whole = pl.BlockSpec((half,) + a.shape[1:], lambda i, t: (far_side, 0, 0, 0))
    own = pl.BlockSpec((tok, step), lambda i, t: (0, jnp.minimum(i, steps - 1)))
    other = pl.BlockSpec((tok, step), lambda i, t: (0, jnp.maximum(i - steps, 0)))
    return pl.pallas_call(
        functools.partial(quad_weight_kernel, len(after)),
        grid_spec=pltpu.PrefetchScalarGridSpec(
            num_scalar_prefetch=1,
            grid=(2 * steps,),
            in_specs=[whole, pl.BlockSpec(b.shape, lambda i, t: (0, 0, 0, 0))] + [own, other] * 4 + [ANY] * len(after),
            out_specs=[
                pl.BlockSpec((head, step), lambda i, t: (0, (i + t[0] * steps) % (2 * steps)))
            ]
            * half,
        ),
        out_shape=[jax.ShapeDtypeStruct((head, 2 * feat), BF)] * half,
        compiler_params=params(),
        cost_estimate=cost(2e10 if far_side else NEAR, 0),
        name="quad_weight",
    )(tp, a, b, *cots, *after)


def pair_query_kernel(head, me_ref, after_ref, g_ref, v_ref, k_ref, s_ref, kv_ref, t_ref, o_ref):
    core = me_ref[0] % 2
    half = g_ref.shape[0] // 2
    for j in range(g_ref.shape[1] // head):
        at, row = slice(j * head, (j + 1) * head), slice(j // 2 * head, (j // 2 + 1) * head)
        g = g_ref[:, at]
        near = s_ref[row, :].astype(F32) + core.astype(F32) * kv_ref[row, :].astype(F32)
        state = jnp.where(core == j % 2, near.astype(BF), t_ref[row, :])
        first_half, second_half = causal_apply(g, v_ref[:, at], k_ref[:, at], False)
        over = dot(g, state, 1, 1)
        o_ref[:half, at] = (first_half + over[:half]).astype(BF)
        o_ref[half:, at] = (second_half + over[half:]).astype(BF)


def pair_query_grad(me, after, g, v, k, state, kv, other, head):
    tok, width = g.shape
    step = min(4 * head, width)
    spec = pl.BlockSpec((tok, step), lambda i, m: (0, i))
    rows = pl.BlockSpec((step // 2, head), lambda i, m: (i, 0))
    return pl.pallas_call(
        functools.partial(pair_query_kernel, head),
        grid_spec=pltpu.PrefetchScalarGridSpec(
            num_scalar_prefetch=1,
            grid=(width // step,),
            in_specs=[ANY, spec, spec, spec, rows, rows, rows],
            out_specs=spec,
        ),
        out_shape=jax.ShapeDtypeStruct((tok, width), BF),
        compiler_params=params(),
        cost_estimate=cost(0, 0),
        name="query_grad",
    )(me, after, g, v, k, state, kv, other)


def pair_grad_kernel(head, waits, me_ref, tp_ref, own_ref, far_ref, w_ref, q_ref, *refs):
    g_ref, mine_ref, send_ref = refs[waits : waits + 3]
    cot_ref = refs[-1]
    feat = own_ref.shape[1]

    @pl.when(pl.program_id(0) == 0)
    def _():
        cot_ref[:, lanes(tp_ref[0], feat)] = own_ref[...]
        cot_ref[:, lanes(1 - tp_ref[0], feat)] = far_ref[...]

    core = me_ref[0] % 2
    g_ref[...] = dot(cot_ref[...], w_ref[...], 1, 1).astype(BF)
    for j in range(g_ref.shape[1] // (2 * head)):
        at = slice(j * head, (j + 1) * head)
        for o_ref, side in ((send_ref, 1 - core), (mine_ref, core)):
            pick = lanes(2 * j + side, head)
            o_ref[at, :] = dot(q_ref[:, pick], g_ref[:, pick], 0, 0).astype(BF)


def pair_grad(me, tp, after, own, far, w, q, head):
    tok, feat = own.shape
    width = q.shape[1]
    step = min(4 * head, width)
    whole = pl.BlockSpec((tok, feat), lambda i, m, t: (0, 0))
    rows = pl.BlockSpec((step // 2, head), lambda i, m, t: (i, 0))
    cols = pl.BlockSpec((tok, step), lambda i, m, t: (0, i))
    sums = jax.ShapeDtypeStruct((width // 2, head), BF)
    return pl.pallas_call(
        functools.partial(pair_grad_kernel, head, len(after)),
        grid_spec=pltpu.PrefetchScalarGridSpec(
            num_scalar_prefetch=2,
            grid=(width // step,),
            in_specs=[
                whole,
                whole,
                pl.BlockSpec((step, 2 * feat), lambda i, m, t: (i, 0)),
                cols,
            ]
            + [ANY] * len(after),
            out_specs=[cols, rows, rows],
            scratch_shapes=[pltpu.VMEM((tok, 2 * feat), BF)],
        ),
        out_shape=[jax.ShapeDtypeStruct((tok, width), BF), sums, sums],
        compiler_params=params(),
        cost_estimate=cost(4 * tok * feat * width, 4 * feat * width + 4 * tok * width),
        name="out_grad",
    )(me, tp, own, far, w, q, *after)


def pass_kernel(*refs):
    pass


def passed_after(x, after, flops):
    return pl.pallas_call(
        pass_kernel,
        in_specs=[ANY] * (1 + len(after)),
        out_specs=ANY,
        out_shape=jax.ShapeDtypeStruct(x.shape, x.dtype),
        input_output_aliases={0: 0},
        compiler_params=params(),
        cost_estimate=cost(flops, 0),
        name="passed_after",
    )(x, *after)


def add_kernel(after_ref, a_ref, b_ref, o_ref):
    o_ref[...] = (a_ref[...].astype(F32) + b_ref[...].astype(F32)).astype(BF)


def add_after(after, a, b):
    spec = pl.BlockSpec(a.shape, lambda: (0, 0))
    return pl.pallas_call(
        add_kernel,
        in_specs=[ANY, spec, spec],
        out_specs=spec,
        out_shape=jax.ShapeDtypeStruct(a.shape, BF),
        compiler_params=params(),
        cost_estimate=cost(0, 0),
        name="add_after",
    )(after, a, b)


def key_value_inner_kernel(head, after_ref, q_ref, k_ref, v_ref, g_ref, ko_ref, vo_ref):
    half = g_ref.shape[0] // 2
    for j in range(g_ref.shape[1] // head):
        at = slice(j * head, (j + 1) * head)
        q, k, v, g = q_ref[:, at], k_ref[:, at], v_ref[:, at], g_ref[:, at]
        first, second = causal_apply(v, g, q, True)
        ko_ref[:half, at] = first.astype(BF)
        ko_ref[half:, at] = second.astype(BF)
        first, second = causal_apply(k, q, g, True)
        vo_ref[:half, at] = first.astype(BF)
        vo_ref[half:, at] = second.astype(BF)


def key_value_inner(after, q, k, v, g, head):
    tok, width = g.shape
    step = min(4 * head, width)
    spec = pl.BlockSpec((tok, step), lambda i: (0, i))
    shape = jax.ShapeDtypeStruct((tok, width), BF)
    return pl.pallas_call(
        functools.partial(key_value_inner_kernel, head),
        grid=(width // step,),
        in_specs=[ANY, spec, spec, spec, spec],
        out_specs=[spec, spec],
        out_shape=[shape, shape],
        compiler_params=params(),
        cost_estimate=cost(0, 0),
        name="key_value_inner",
    )(after, q, k, v, g)


def key_value_outer_kernel(head, me_ref, k_ref, v_ref, ki_ref, vi_ref, s_ref, qd_ref, t_ref, ko_ref, vo_ref):
    core = me_ref[0] % 2
    for j in range(k_ref.shape[1] // head):
        at, row = slice(j * head, (j + 1) * head), slice(j // 2 * head, (j // 2 + 1) * head)
        near = s_ref[row, :].astype(F32) + (1 - core).astype(F32) * qd_ref[row, :].astype(F32)
        adj = jnp.where(core == j % 2, near.astype(BF), t_ref[row, :])
        ko_ref[:, at] = (dot(v_ref[:, at], adj, 1, 1) + ki_ref[:, at].astype(F32)).astype(BF)
        vo_ref[:, at] = (dot(k_ref[:, at], adj, 1, 0) + vi_ref[:, at].astype(F32)).astype(BF)


def key_value_outer(me, k, v, key_inner, value_inner, adjoint, qd, other, head):
    tok, width = k.shape
    step = min(4 * head, width)
    spec = pl.BlockSpec((tok, step), lambda i, m: (0, i))
    rows = pl.BlockSpec((step // 2, head), lambda i, m: (i, 0))
    shape = jax.ShapeDtypeStruct((tok, width), BF)
    return pl.pallas_call(
        functools.partial(key_value_outer_kernel, head),
        grid_spec=pltpu.PrefetchScalarGridSpec(
            num_scalar_prefetch=1,
            grid=(width // step,),
            in_specs=[spec, spec, spec, spec, rows, rows, rows],
            out_specs=[spec, spec],
        ),
        out_shape=[shape, shape],
        compiler_params=params(),
        cost_estimate=cost(0, 0),
        name="key_value_outer",
    )(me, k, v, key_inner, value_inner, adjoint, qd, other)


def local_paired(queries, keys, values, cotangent, out_weight, memory):
    head = memory.shape[2]
    n = lax.axis_size("ctx")
    me, tp = lax.axis_index("ctx"), lax.axis_index("tp")
    who, which = me.reshape(1), tp.reshape(1)
    core = (me % 2).astype(F32)
    groups = [[c for c in range(n) if c % 2 == side] for side in range(2)]

    def swap(x, bit):
        return lax.ppermute(x, "ctx", [(c, c ^ bit) for c in range(n)])

    def swap_tp(x):
        return lax.ppermute(x, "tp", [(0, 1), (1, 0)])

    def across(x):
        return lax.all_to_all(x, "ctx", 0, 0, axis_index_groups=groups, tiled=True)

    def added(x, factor, y):
        return (x.astype(F32) + factor * y.astype(F32)).astype(BF)

    kv_mine, kv_send = pair_sums(who, keys, values, head)
    kv_other = swap(kv_send, 1)
    far = swap_tp(cotangent)
    south = swap(cotangent, 2)
    chip = added(kv_mine, 1.0, kv_other)
    inner, sent = pair_intra(who, (chip,), queries, keys, values, head)
    start = lax.dynamic_index_in_dim(memory, me, 0, False)
    scanned, sent = scan_blocks(across(chip), start, n // 2, False, (inner, far, south), sent)
    state = across(scanned)

    far_south = swap_tp(south)
    grad, qd_mine, qd_send = pair_grad(
        who, which, (scanned, south), cotangent, far, out_weight, queries, head
    )
    mine, send, send_near = pair_attended(
        who, grad, queries, inner, swap(sent, 1), state, kv_mine, kv_other, head
    )
    received, received_near = swap(send, 2), swap(send_near, 2)
    state_other = swap(added(state, 1.0 - core, kv_mine), 1)

    qd_other = swap(qd_send, 1)
    chip = add_after(send, qd_mine, qd_other)
    query_g = pair_query_grad(who, chip, grad, values, keys, state, kv_other, state_other, head)
    cots = [cotangent, far, swap(cotangent, 1), swap(far, 1)]
    cots += [south, far_south, swap(south, 1), swap(far_south, 1)]

    received = passed_after(received, (query_g,), 2e10)
    crossing = quad_weight(which, (), mine, received, cots, 1)
    summed = added(crossing[0], 1.0, swap(crossing[1], 4))
    crossed = swap(summed, 8)
    scanned = scan_blocks(across(chip), jnp.zeros_like(start), n // 2, True, (crossing[0],))
    after_chip = across(scanned)
    same = quad_weight(which, (scanned,), mine, received_near, cots, 0)
    neighbour = swap(same[1], 4)
    inners = key_value_inner(same[0], queries, keys, values, grad, head)
    after_chip = passed_after(after_chip, (inners[0],), 0)
    adjoint_other = swap(added(after_chip, core, qd_mine), 1)
    key_g, value_g = key_value_outer(
        who, keys, values, *inners, after_chip, qd_other, adjoint_other, head
    )
    total = same[0].astype(F32) + neighbour.astype(F32) + crossed.astype(F32)
    return query_g, key_g, value_g, total


def local_any(queries, keys, values, cotangent, out_weight, memory):
    head = memory.shape[2]
    width = queries.shape[1]
    feat = cotangent.shape[1]
    n = lax.axis_size("ctx")
    rows = width // n
    me, tp = lax.axis_index("ctx"), lax.axis_index("tp")

    far = lax.ppermute(cotangent, "tp", [(0, 1), (1, 0)])
    kv = block_sums(keys, values, head)
    start = lax.dynamic_slice_in_dim(memory.reshape(width, head), me * rows, rows, 0)
    state = carried(kv, start, "ctx", False)
    inner = intra(queries, keys, values, head)
    grad, qd = out_grad_and_sums(tp.reshape(1), cotangent, far, out_weight, queries, head)
    adjoint = carried(qd, jnp.zeros_like(start), "ctx", True)
    attended = attended_of(queries, state, inner, head)
    term = weight_term(attended, cotangent, far)
    total = lax.psum_scatter(term, "ctx", scatter_dimension=0, tiled=True)
    query_g = query_grad_of(grad, values, keys, state, head)
    key_g, value_g = key_value_grad_of(queries, keys, values, grad, adjoint, head)
    total = total.astype(F32)
    total = jnp.where(tp == 0, total, jnp.concatenate([total[:, feat:], total[:, :feat]], 1))
    return query_g, key_g, value_g, total


def local(*args):
    heads = args[5].shape[0]
    n = lax.axis_size("ctx")
    if n == heads == 16 and lax.axis_size("tp") == 2:
        return local_paired(*args)
    return local_any(*args)


def solution(mesh):
    in_specs = (
        P("ctx", "tp"),
        P("ctx", "tp"),
        P("ctx", "tp"),
        P("ctx", "tp"),
        P("tp", None),
        P("tp", None, None),
    )
    out_specs = (P("ctx", "tp"), P("ctx", "tp"), P("ctx", "tp"), P(("tp", "ctx"), None))
    return jax.shard_map(local, mesh=mesh, in_specs=in_specs, out_specs=out_specs, check_vma=False)
```

```python
import functools

import jax
import jax.numpy as jnp
from jax import lax
from jax.experimental import pallas as pl
from jax.experimental.pallas import tpu as pltpu
from jax.sharding import PartitionSpec as P

BF = jnp.bfloat16
F32 = jnp.float32
NEAR = 0
SCAN = 2e10
VMEM_LIMIT = 56 * 1024 * 1024


def dot(a, b, ca, cb):
    return lax.dot_general(a, b, (((ca,), (cb,)), ((), ())), preferred_element_type=F32)


def lanes(index, head):
    return pl.ds(pl.multiple_of(index * head, head), head)


def params():
    return pltpu.CompilerParams(vmem_limit_bytes=VMEM_LIMIT)


def cost(flops, nbytes):
    return pl.CostEstimate(flops=int(flops), bytes_accessed=int(nbytes), transcendentals=0)


def kv_kernel(head, a_ref, b_ref, o_ref):
    for j in range(a_ref.shape[1] // head):
        at = slice(j * head, (j + 1) * head)
        o_ref[at, :] = dot(a_ref[:, at], b_ref[:, at], 0, 0).astype(o_ref.dtype)


def block_sums(a, b, head):
    tok, width = a.shape
    step = 2 * head
    return pl.pallas_call(
        functools.partial(kv_kernel, head),
        grid=(width // step,),
        in_specs=[pl.BlockSpec((tok, step), lambda i: (0, i))] * 2,
        out_specs=pl.BlockSpec((step, head), lambda i: (i, 0)),
        out_shape=jax.ShapeDtypeStruct((width, head), BF),
        compiler_params=params(),
        cost_estimate=cost(2 * tok * width * head, 4 * tok * width),
        name="block_sums",
    )(a, b)


def masked(tok, upper):
    row = lax.broadcasted_iota(jnp.int32, (tok, tok), 0)
    col = lax.broadcasted_iota(jnp.int32, (tok, tok), 1)
    return row <= col if upper else row >= col


def causal_apply(a, b, c, upper):
    tok = a.shape[0]
    half = tok // 2
    keep = masked(half, upper)

    def tile(x, y, diagonal):
        s = dot(x, y, 1, 1)
        if diagonal:
            s = jnp.where(keep, s, 0.0)
        return s.astype(BF)

    a0, a1, b0, b1, c0, c1 = a[:half], a[half:], b[:half], b[half:], c[:half], c[half:]
    first = dot(tile(a0, b0, True), c0, 1, 0)
    second = dot(tile(a1, b1, True), c1, 1, 0)
    if upper:
        first = first + dot(tile(a0, b1, False), c1, 1, 0)
    else:
        second = second + dot(tile(a1, b0, False), c0, 1, 0)
    return first, second


def intra_kernel(head, q_ref, k_ref, v_ref, o_ref):
    half = q_ref.shape[0] // 2
    for j in range(q_ref.shape[1] // head):
        at = slice(j * head, (j + 1) * head)
        first, second = causal_apply(q_ref[:, at], k_ref[:, at], v_ref[:, at], False)
        o_ref[:half, at] = first
        o_ref[half:, at] = second


def intra(q, k, v, head):
    tok, width = q.shape
    step = 2 * head
    spec = pl.BlockSpec((tok, step), lambda i: (0, i))
    return pl.pallas_call(
        functools.partial(intra_kernel, head),
        grid=(width // step,),
        in_specs=[spec] * 3,
        out_specs=spec,
        out_shape=jax.ShapeDtypeStruct((tok, width), F32),
        compiler_params=params(),
        cost_estimate=cost(4 * tok * tok * width, 10 * tok * width),
        name="intra",
    )(q, k, v)


def grad_kernel(head, tp_ref, own_ref, far_ref, wo_ref, wf_ref, q_ref, g_ref, s_ref):
    g = dot(own_ref[...], wo_ref[...], 1, 1) + dot(far_ref[...], wf_ref[...], 1, 1)
    g = g.astype(BF)
    g_ref[...] = g
    for j in range(g.shape[1] // head):
        at = slice(j * head, (j + 1) * head)
        s_ref[at, :] = dot(q_ref[:, at], g[:, at], 0, 0).astype(s_ref.dtype)


def out_grad_and_sums(tp, own, far, w, q, head):
    tok, feat = own.shape
    width = q.shape[1]
    step = 2 * head
    whole = pl.BlockSpec((tok, feat), lambda i, t: (0, 0))
    return pl.pallas_call(
        functools.partial(grad_kernel, head),
        grid_spec=pltpu.PrefetchScalarGridSpec(
            num_scalar_prefetch=1,
            grid=(width // step,),
            in_specs=[
                whole,
                whole,
                pl.BlockSpec((step, feat), lambda i, t: (i, t[0])),
                pl.BlockSpec((step, feat), lambda i, t: (i, 1 - t[0])),
                pl.BlockSpec((tok, step), lambda i, t: (0, i)),
            ],
            out_specs=[
                pl.BlockSpec((tok, step), lambda i, t: (0, i)),
                pl.BlockSpec((step, head), lambda i, t: (i, 0)),
            ],
        ),
        out_shape=[
            jax.ShapeDtypeStruct((tok, width), BF),
            jax.ShapeDtypeStruct((width, head), BF),
        ],
        compiler_params=params(),
        cost_estimate=cost(4 * tok * feat * width, 4 * feat * width + 4 * tok * width),
        name="out_grad",
    )(tp, own, far, w, w, q)


def attended_kernel(head, q_ref, s_ref, i_ref, o_ref):
    for j in range(q_ref.shape[1] // head):
        at = slice(j * head, (j + 1) * head)
        o_ref[:, at] = (dot(q_ref[:, at], s_ref[at, :], 1, 0) + i_ref[:, at]).astype(BF)


def attended_of(q, state, inner, head):
    tok, width = q.shape
    step = 2 * head
    spec = pl.BlockSpec((tok, step), lambda i: (0, i))
    return pl.pallas_call(
        functools.partial(attended_kernel, head),
        grid=(width // step,),
        in_specs=[spec, pl.BlockSpec((step, head), lambda i: (i, 0)), spec],
        out_specs=spec,
        out_shape=jax.ShapeDtypeStruct((tok, width), BF),
        compiler_params=params(),
        cost_estimate=cost(2 * tok * head * width, 8 * tok * width),
        name="attended",
    )(q, state, inner)


def weight_kernel(a_ref, own_ref, far_ref, o_ref):
    feat = own_ref.shape[1]
    a = a_ref[...]
    o_ref[:, :feat] = dot(a, own_ref[...], 0, 0).astype(o_ref.dtype)
    o_ref[:, feat:] = dot(a, far_ref[...], 0, 0).astype(o_ref.dtype)


def weight_term(a, own, far):
    tok, width = a.shape
    feat = own.shape[1]
    step = 256
    whole = pl.BlockSpec((tok, feat), lambda i: (0, 0))
    return pl.pallas_call(
        weight_kernel,
        grid=(width // step,),
        in_specs=[pl.BlockSpec((tok, step), lambda i: (0, i)), whole, whole],
        out_specs=pl.BlockSpec((step, 2 * feat), lambda i: (i, 0)),
        out_shape=jax.ShapeDtypeStruct((width, 2 * feat), BF),
        compiler_params=params(),
        cost_estimate=cost(4 * tok * feat * width, 4 * feat * width + 2 * tok * width),
        name="weight_term",
    )(a, own, far)


def query_kernel(head, g_ref, v_ref, k_ref, s_ref, o_ref):
    half = g_ref.shape[0] // 2
    for j in range(g_ref.shape[1] // head):
        at = slice(j * head, (j + 1) * head)
        g = g_ref[:, at]
        first, second = causal_apply(g, v_ref[:, at], k_ref[:, at], False)
        carried = dot(g, s_ref[at, :], 1, 1)
        o_ref[:half, at] = (first + carried[:half]).astype(BF)
        o_ref[half:, at] = (second + carried[half:]).astype(BF)


def query_grad_of(g, v, k, state, head):
    tok, width = g.shape
    step = 2 * head
    spec = pl.BlockSpec((tok, step), lambda i: (0, i))
    return pl.pallas_call(
        functools.partial(query_kernel, head),
        grid=(width // step,),
        in_specs=[spec, spec, spec, pl.BlockSpec((step, head), lambda i: (i, 0))],
        out_specs=spec,
        out_shape=jax.ShapeDtypeStruct((tok, width), BF),
        compiler_params=params(),
        cost_estimate=cost(4 * tok * tok * width, 8 * tok * width),
        name="query_grad",
    )(g, v, k, state)


def key_value_kernel(head, q_ref, k_ref, v_ref, g_ref, a_ref, ko_ref, vo_ref):
    half = g_ref.shape[0] // 2
    for j in range(g_ref.shape[1] // head):
        at = slice(j * head, (j + 1) * head)
        q, k, v, g, adj = q_ref[:, at], k_ref[:, at], v_ref[:, at], g_ref[:, at], a_ref[at, :]
        first, second = causal_apply(v, g, q, True)
        carried = dot(v, adj, 1, 1)
        ko_ref[:half, at] = (first + carried[:half]).astype(BF)
        ko_ref[half:, at] = (second + carried[half:]).astype(BF)
        first, second = causal_apply(k, q, g, True)
        carried = dot(k, adj, 1, 0)
        vo_ref[:half, at] = (first + carried[:half]).astype(BF)
        vo_ref[half:, at] = (second + carried[half:]).astype(BF)


def key_value_grad_of(q, k, v, g, adjoint, head):
    tok, width = g.shape
    step = 2 * head
    spec = pl.BlockSpec((tok, step), lambda i: (0, i))
    shape = jax.ShapeDtypeStruct((tok, width), BF)
    return pl.pallas_call(
        functools.partial(key_value_kernel, head),
        grid=(width // step,),
        in_specs=[spec, spec, spec, spec, pl.BlockSpec((step, head), lambda i: (i, 0))],
        out_specs=[spec, spec],
        out_shape=[shape, shape],
        compiler_params=params(),
        cost_estimate=cost(8 * tok * tok * width, 12 * tok * width),
        name="key_value_grad",
    )(q, k, v, g, adjoint)


ANY = pl.BlockSpec(memory_space=pl.ANY)


def scan_kernel(n, reverse, waits, x_ref, *refs):
    o_ref = refs[waits]
    rows = x_ref.shape[0] // n
    total = jnp.zeros((rows, x_ref.shape[1]), F32) if reverse else refs[0][...]
    for i in range(n):
        c = n - 1 - i if reverse else i
        at = slice(c * rows, (c + 1) * rows)
        o_ref[at, :] = total.astype(BF)
        total = total + x_ref[at, :].astype(F32)


def scan_blocks(x, start, n, reverse, after=(), passed=None):
    more = () if passed is None else (passed,)
    first = () if reverse else (start,)
    out = pl.pallas_call(
        functools.partial(scan_kernel, n, reverse, len(first) + len(after) + len(more)),
        in_specs=[pl.BlockSpec(y.shape, lambda: (0, 0)) for y in (x, *first)]
        + [ANY] * (len(after) + len(more)),
        out_specs=[pl.BlockSpec(x.shape, lambda: (0, 0))] + [ANY] * len(more),
        out_shape=[jax.ShapeDtypeStruct(x.shape, BF)]
        + [jax.ShapeDtypeStruct(p.shape, p.dtype) for p in more],
        input_output_aliases={1 + len(first) + len(after): 1} if more else {},
        compiler_params=params(),
        cost_estimate=cost(SCAN, 0),
        name="scan_blocks",
    )(x, *first, *after, *more)
    return out if more else out[0]


def carried(x, start, axis, reverse):
    n = lax.axis_size(axis)
    mine = lax.all_to_all(x, axis, 0, 0, tiled=True)
    return lax.all_to_all(scan_blocks(mine, start, n, reverse), axis, 0, 0, tiled=True)


def pair_sums_kernel(head, me_ref, a_ref, b_ref, mine_ref, send_ref):
    core = me_ref[0] % 2
    for j in range(a_ref.shape[1] // (2 * head)):
        at = slice(j * head, (j + 1) * head)
        for o_ref, side in ((send_ref, 1 - core), (mine_ref, core)):
            pick = lanes(2 * j + side, head)
            o_ref[at, :] = dot(a_ref[:, pick], b_ref[:, pick], 0, 0).astype(BF)


def pair_sums(me, a, b, head):
    tok, width = a.shape
    step = min(4 * head, width)
    spec = pl.BlockSpec((tok, step), lambda i, m: (0, i))
    out = pl.BlockSpec((step // 2, head), lambda i, m: (i, 0))
    shape = jax.ShapeDtypeStruct((width // 2, head), BF)
    return pl.pallas_call(
        functools.partial(pair_sums_kernel, head),
        grid_spec=pltpu.PrefetchScalarGridSpec(
            num_scalar_prefetch=1,
            grid=(width // step,),
            in_specs=[spec] * 2,
            out_specs=[out] * 2,
        ),
        out_shape=[shape] * 2,
        compiler_params=params(),
        cost_estimate=cost(2 * tok * width * head, 4 * tok * width),
        name="pair_sums",
    )(me, a, b)


def pair_intra_kernel(head, waits, me_ref, *refs):
    q_ref, k_ref, v_ref, mine_ref, send_ref = refs[waits:]
    core = me_ref[0] % 2
    half = q_ref.shape[0] // 2
    for j in range(q_ref.shape[1] // (2 * head)):
        for o_ref, side, base in ((send_ref, 1 - core, (2 * j + 1) * head), (mine_ref, core, j * head)):
            pick = lanes(2 * j + side, head)
            first, second = causal_apply(q_ref[:, pick], k_ref[:, pick], v_ref[:, pick], False)
            o_ref[base : base + head, :half] = first.astype(BF).T
            o_ref[base : base + head, half:] = second.astype(BF).T
        send_ref[2 * j * head : (2 * j + 1) * head, :] = q_ref[:, lanes(2 * j + 1 - core, head)].T


def pair_intra(me, after, q, k, v, head):
    tok, width = q.shape
    step = min(4 * head, width)
    spec = pl.BlockSpec((tok, step), lambda i, m: (0, i))
    return pl.pallas_call(
        functools.partial(pair_intra_kernel, head, len(after)),
        grid_spec=pltpu.PrefetchScalarGridSpec(
            num_scalar_prefetch=1,
            grid=(width // step,),
            in_specs=[ANY] * len(after) + [spec] * 3,
            out_specs=[
                pl.BlockSpec((step // 2, tok), lambda i, m: (i, 0)),
                pl.BlockSpec((step, tok), lambda i, m: (i, 0)),
            ],
        ),
        out_shape=[
            jax.ShapeDtypeStruct((width // 2, tok), BF),
            jax.ShapeDtypeStruct((width, tok), BF),
        ],
        compiler_params=params(),
        cost_estimate=cost(4 * tok * tok * width, 9 * tok * width),
        name="pair_intra",
    )(me, *after, q, k, v)


def pair_attended_kernel(head, me_ref, after_ref, q0_ref, q1_ref, i_ref, far_ref, s_ref, own_ref, oth_ref,
                         mine_ref, cross_ref, near_ref, away_ref):
    core = (me_ref[0] % 2).astype(F32)
    south = (me_ref[0] // 2) % 2

    def fill(q_ref, side, o_ref):
        rows = lanes(side, head)
        state = s_ref[rows, :].astype(F32)
        near = (state + core * oth_ref[rows, :].astype(F32)).astype(BF)
        away = (state + (1.0 - core) * own_ref[rows, :].astype(F32)).astype(BF)
        away_ref[rows, :] = away
        here = dot(near, q_ref[...], 0, 1) + i_ref[rows, :].astype(F32)
        there = dot(away, far_ref[lanes(2 * side, head), :], 0, 0)
        there = there + far_ref[lanes(2 * side + 1, head), :].astype(F32)
        o_ref[0, 0] = here.astype(BF)
        o_ref[0, 1] = there.astype(BF)

    fill(q0_ref, south, mine_ref)
    crossing = pl.program_id(0) < pl.num_programs(0) // 2
    pl.when(crossing)(lambda: fill(q1_ref, 1 - south, cross_ref))
    pl.when(jnp.logical_not(crossing))(lambda: fill(q1_ref, 1 - south, near_ref))


def pair_attended(me, after, q, inner, far, state, own, oth, head):
    tok, width = q.shape
    places = width // (4 * head)
    half = places // 2

    def place(i, m):
        return (m[0] // 4) ^ i ^ half

    rows = pl.BlockSpec((2 * head, head), lambda i, m: (place(i, m), 0))

    def out(index):
        return pl.BlockSpec((1, 2, head, tok), lambda i, m: (index(i), 0, 0, 0))

    def shape(count):
        return jax.ShapeDtypeStruct((count, 2, head, tok), BF)

    return pl.pallas_call(
        functools.partial(pair_attended_kernel, head),
        grid_spec=pltpu.PrefetchScalarGridSpec(
            num_scalar_prefetch=1,
            grid=(places,),
            in_specs=[
                ANY,
                pl.BlockSpec((tok, head), lambda i, m: (0, 4 * place(i, m) + m[0] % 4)),
                pl.BlockSpec((tok, head), lambda i, m: (0, 4 * place(i, m) + (m[0] % 4 ^ 2))),
                pl.BlockSpec((2 * head, tok), lambda i, m: (place(i, m), 0)),
                pl.BlockSpec((4 * head, tok), lambda i, m: (place(i, m), 0)),
            ]
            + [rows] * 3,
            out_specs=[
                out(lambda i: i ^ half),
                out(lambda i: jnp.minimum(i, half - 1)),
                out(lambda i: jnp.maximum(i - half, 0)),
                rows,
            ],
        ),
        out_shape=[
            shape(places),
            shape(half),
            shape(half),
            jax.ShapeDtypeStruct((width // 2, head), BF),
        ],
        compiler_params=params(),
        cost_estimate=cost(2 * tok * head * width, 10 * tok * width),
        name="pair_attended",
    )(me, after, q, q, inner, far, state, own, oth)


def quad_weight_kernel(waits, tp_ref, a_ref, b_ref, *refs):
    half, _, head, tok = a_ref.shape
    ins, outs = refs[:8], refs[8 + waits :]

    def product(part):
        total = None
        for k in range(4):
            block = (a_ref if k < 2 else b_ref)[:, k % 2].reshape(half * head, tok)
            term = dot(block, ins[2 * k + part][...], 1, 0)
            total = term if total is None else total + term
        for i, o_ref in enumerate(outs):
            o_ref[...] = total[i * head : (i + 1) * head].astype(BF)

    steps = pl.num_programs(0) // 2
    pl.when(pl.program_id(0) < steps)(lambda: product(0))
    pl.when(pl.program_id(0) >= steps)(lambda: product(1))


def quad_weight(tp, after, a, b, cots, far_side):
    places, _, head, tok = a.shape
    half = places // 2
    feat = cots[0].shape[1]
    step = min(512, feat)
    steps = feat // step
    whole = pl.BlockSpec((half,) + a.shape[1:], lambda i, t: (far_side, 0, 0, 0))
    own = pl.BlockSpec((tok, step), lambda i, t: (0, jnp.minimum(i, steps - 1)))
    other = pl.BlockSpec((tok, step), lambda i, t: (0, jnp.maximum(i - steps, 0)))
    return pl.pallas_call(
        functools.partial(quad_weight_kernel, len(after)),
        grid_spec=pltpu.PrefetchScalarGridSpec(
            num_scalar_prefetch=1,
            grid=(2 * steps,),
            in_specs=[whole, pl.BlockSpec(b.shape, lambda i, t: (0, 0, 0, 0))] + [own, other] * 4 + [ANY] * len(after),
            out_specs=[
                pl.BlockSpec((head, step), lambda i, t: (0, (i + t[0] * steps) % (2 * steps)))
            ]
            * half,
        ),
        out_shape=[jax.ShapeDtypeStruct((head, 2 * feat), BF)] * half,
        compiler_params=params(),
        cost_estimate=cost(2e10 if far_side else NEAR, 0),
        name="quad_weight",
    )(tp, a, b, *cots, *after)


def pair_query_kernel(head, me_ref, after_ref, g_ref, v_ref, k_ref, s_ref, kv_ref, t_ref, o_ref):
    core = me_ref[0] % 2
    half = g_ref.shape[0] // 2
    for j in range(g_ref.shape[1] // head):
        at, row = slice(j * head, (j + 1) * head), slice(j // 2 * head, (j // 2 + 1) * head)
        g = g_ref[:, at]
        near = s_ref[row, :].astype(F32) + core.astype(F32) * kv_ref[row, :].astype(F32)
        state = jnp.where(core == j % 2, near.astype(BF), t_ref[row, :])
        first_half, second_half = causal_apply(g, v_ref[:, at], k_ref[:, at], False)
        over = dot(g, state, 1, 1)
        o_ref[:half, at] = (first_half + over[:half]).astype(BF)
        o_ref[half:, at] = (second_half + over[half:]).astype(BF)


def pair_query_grad(me, after, g, v, k, state, kv, other, head):
    tok, width = g.shape
    step = min(4 * head, width)
    spec = pl.BlockSpec((tok, step), lambda i, m: (0, i))
    rows = pl.BlockSpec((step // 2, head), lambda i, m: (i, 0))
    return pl.pallas_call(
        functools.partial(pair_query_kernel, head),
        grid_spec=pltpu.PrefetchScalarGridSpec(
            num_scalar_prefetch=1,
            grid=(width // step,),
            in_specs=[ANY, spec, spec, spec, rows, rows, rows],
            out_specs=spec,
        ),
        out_shape=jax.ShapeDtypeStruct((tok, width), BF),
        compiler_params=params(),
        cost_estimate=cost(0, 0),
        name="query_grad",
    )(me, after, g, v, k, state, kv, other)


def pair_grad_kernel(head, waits, me_ref, tp_ref, own_ref, far_ref, w_ref, q_ref, *refs):
    g_ref, mine_ref, send_ref = refs[waits : waits + 3]
    cot_ref = refs[-1]
    feat = own_ref.shape[1]

    @pl.when(pl.program_id(0) == 0)
    def _():
        cot_ref[:, lanes(tp_ref[0], feat)] = own_ref[...]
        cot_ref[:, lanes(1 - tp_ref[0], feat)] = far_ref[...]

    core = me_ref[0] % 2
    g_ref[...] = dot(cot_ref[...], w_ref[...], 1, 1).astype(BF)
    for j in range(g_ref.shape[1] // (2 * head)):
        at = slice(j * head, (j + 1) * head)
        for o_ref, side in ((send_ref, 1 - core), (mine_ref, core)):
            pick = lanes(2 * j + side, head)
            o_ref[at, :] = dot(q_ref[:, pick], g_ref[:, pick], 0, 0).astype(BF)


def pair_grad(me, tp, after, own, far, w, q, head):
    tok, feat = own.shape
    width = q.shape[1]
    step = min(4 * head, width)
    whole = pl.BlockSpec((tok, feat), lambda i, m, t: (0, 0))
    rows = pl.BlockSpec((step // 2, head), lambda i, m, t: (i, 0))
    cols = pl.BlockSpec((tok, step), lambda i, m, t: (0, i))
    sums = jax.ShapeDtypeStruct((width // 2, head), BF)
    return pl.pallas_call(
        functools.partial(pair_grad_kernel, head, len(after)),
        grid_spec=pltpu.PrefetchScalarGridSpec(
            num_scalar_prefetch=2,
            grid=(width // step,),
            in_specs=[
                whole,
                whole,
                pl.BlockSpec((step, 2 * feat), lambda i, m, t: (i, 0)),
                cols,
            ]
            + [ANY] * len(after),
            out_specs=[cols, rows, rows],
            scratch_shapes=[pltpu.VMEM((tok, 2 * feat), BF)],
        ),
        out_shape=[jax.ShapeDtypeStruct((tok, width), BF), sums, sums],
        compiler_params=params(),
        cost_estimate=cost(4 * tok * feat * width, 4 * feat * width + 4 * tok * width),
        name="out_grad",
    )(me, tp, own, far, w, q, *after)


def pass_kernel(*refs):
    pass


def passed_after(x, after, flops):
    return pl.pallas_call(
        pass_kernel,
        in_specs=[ANY] * (1 + len(after)),
        out_specs=ANY,
        out_shape=jax.ShapeDtypeStruct(x.shape, x.dtype),
        input_output_aliases={0: 0},
        compiler_params=params(),
        cost_estimate=cost(flops, 0),
        name="passed_after",
    )(x, *after)


def add_kernel(after_ref, a_ref, b_ref, o_ref):
    o_ref[...] = (a_ref[...].astype(F32) + b_ref[...].astype(F32)).astype(BF)


def add_after(after, a, b):
    spec = pl.BlockSpec(a.shape, lambda: (0, 0))
    return pl.pallas_call(
        add_kernel,
        in_specs=[ANY, spec, spec],
        out_specs=spec,
        out_shape=jax.ShapeDtypeStruct(a.shape, BF),
        compiler_params=params(),
        cost_estimate=cost(0, 0),
        name="add_after",
    )(after, a, b)


def key_value_inner_kernel(head, after_ref, q_ref, k_ref, v_ref, g_ref, ko_ref, vo_ref):
    half = g_ref.shape[0] // 2
    for j in range(g_ref.shape[1] // head):
        at = slice(j * head, (j + 1) * head)
        q, k, v, g = q_ref[:, at], k_ref[:, at], v_ref[:, at], g_ref[:, at]
        first, second = causal_apply(v, g, q, True)
        ko_ref[:half, at] = first.astype(BF)
        ko_ref[half:, at] = second.astype(BF)
        first, second = causal_apply(k, q, g, True)
        vo_ref[:half, at] = first.astype(BF)
        vo_ref[half:, at] = second.astype(BF)


def key_value_inner(after, q, k, v, g, head):
    tok, width = g.shape
    step = min(4 * head, width)
    spec = pl.BlockSpec((tok, step), lambda i: (0, i))
    shape = jax.ShapeDtypeStruct((tok, width), BF)
    return pl.pallas_call(
        functools.partial(key_value_inner_kernel, head),
        grid=(width // step,),
        in_specs=[ANY, spec, spec, spec, spec],
        out_specs=[spec, spec],
        out_shape=[shape, shape],
        compiler_params=params(),
        cost_estimate=cost(0, 0),
        name="key_value_inner",
    )(after, q, k, v, g)


def key_value_outer_kernel(head, me_ref, k_ref, v_ref, ki_ref, vi_ref, s_ref, qd_ref, t_ref, ko_ref, vo_ref):
    core = me_ref[0] % 2
    for j in range(k_ref.shape[1] // head):
        at, row = slice(j * head, (j + 1) * head), slice(j // 2 * head, (j // 2 + 1) * head)
        near = s_ref[row, :].astype(F32) + (1 - core).astype(F32) * qd_ref[row, :].astype(F32)
        adj = jnp.where(core == j % 2, near.astype(BF), t_ref[row, :])
        ko_ref[:, at] = (dot(v_ref[:, at], adj, 1, 1) + ki_ref[:, at].astype(F32)).astype(BF)
        vo_ref[:, at] = (dot(k_ref[:, at], adj, 1, 0) + vi_ref[:, at].astype(F32)).astype(BF)


def key_value_outer(me, k, v, key_inner, value_inner, adjoint, qd, other, head):
    tok, width = k.shape
    step = min(4 * head, width)
    spec = pl.BlockSpec((tok, step), lambda i, m: (0, i))
    rows = pl.BlockSpec((step // 2, head), lambda i, m: (i, 0))
    shape = jax.ShapeDtypeStruct((tok, width), BF)
    return pl.pallas_call(
        functools.partial(key_value_outer_kernel, head),
        grid_spec=pltpu.PrefetchScalarGridSpec(
            num_scalar_prefetch=1,
            grid=(width // step,),
            in_specs=[spec, spec, spec, spec, rows, rows, rows],
            out_specs=[spec, spec],
        ),
        out_shape=[shape, shape],
        compiler_params=params(),
        cost_estimate=cost(0, 0),
        name="key_value_outer",
    )(me, k, v, key_inner, value_inner, adjoint, qd, other)


def local_paired(queries, keys, values, cotangent, out_weight, memory):
    head = memory.shape[2]
    n = lax.axis_size("ctx")
    me, tp = lax.axis_index("ctx"), lax.axis_index("tp")
    who, which = me.reshape(1), tp.reshape(1)
    core = (me % 2).astype(F32)
    groups = [[c for c in range(n) if c % 2 == side] for side in range(2)]

    def swap(x, bit):
        return lax.ppermute(x, "ctx", [(c, c ^ bit) for c in range(n)])

    def swap_tp(x):
        return lax.ppermute(x, "tp", [(0, 1), (1, 0)])

    def across(x):
        return lax.all_to_all(x, "ctx", 0, 0, axis_index_groups=groups, tiled=True)

    def added(x, factor, y):
        return (x.astype(F32) + factor * y.astype(F32)).astype(BF)

    kv_mine, kv_send = pair_sums(who, keys, values, head)
    kv_other = swap(kv_send, 1)
    far = swap_tp(cotangent)
    south = swap(cotangent, 2)
    chip = added(kv_mine, 1.0, kv_other)
    inner, sent = pair_intra(who, (chip,), queries, keys, values, head)
    start = lax.dynamic_index_in_dim(memory, me, 0, False)
    scanned, sent = scan_blocks(across(chip), start, n // 2, False, (inner, far, south), sent)
    state = across(scanned)

    far_south = swap_tp(south)
    grad, qd_mine, qd_send = pair_grad(
        who, which, (scanned, south), cotangent, far, out_weight, queries, head
    )
    mine, send, send_near, away = pair_attended(
        who, grad, queries, inner, swap(sent, 1), state, kv_mine, kv_other, head
    )
    received, received_near = swap(send, 2), swap(send_near, 2)
    state_other = swap(away, 1)

    qd_other = swap(qd_send, 1)
    chip = add_after(send, qd_mine, qd_other)
    cots = [cotangent, far, swap(cotangent, 1), swap(far, 1)]
    cots += [south, far_south, swap(south, 1), swap(far_south, 1)]

    received = passed_after(received, (chip, state_other), 2e10)
    crossing = quad_weight(which, (), mine, received, cots, 1)
    summed = added(crossing[0], 1.0, swap(crossing[1], 4))
    crossed = swap(summed, 8)
    scanned = scan_blocks(across(chip), None, n // 2, True, (crossing[0],))
    after_chip = across(scanned)
    same = quad_weight(which, (scanned,), mine, received_near, cots, 0)
    neighbour = swap(same[1], 4)
    query_g = pair_query_grad(who, summed, grad, values, keys, state, kv_other, state_other, head)
    inners = key_value_inner(query_g, queries, keys, values, grad, head)
    after_chip = passed_after(after_chip, (inners[0],), 0)
    adjoint_other = swap(added(after_chip, core, qd_mine), 1)
    key_g, value_g = key_value_outer(
        who, keys, values, *inners, after_chip, qd_other, adjoint_other, head
    )
    total = same[0].astype(F32) + neighbour.astype(F32) + crossed.astype(F32)
    return query_g, key_g, value_g, total


def local_any(queries, keys, values, cotangent, out_weight, memory):
    head = memory.shape[2]
    width = queries.shape[1]
    feat = cotangent.shape[1]
    n = lax.axis_size("ctx")
    rows = width // n
    me, tp = lax.axis_index("ctx"), lax.axis_index("tp")

    far = lax.ppermute(cotangent, "tp", [(0, 1), (1, 0)])
    kv = block_sums(keys, values, head)
    start = lax.dynamic_slice_in_dim(memory.reshape(width, head), me * rows, rows, 0)
    state = carried(kv, start, "ctx", False)
    inner = intra(queries, keys, values, head)
    grad, qd = out_grad_and_sums(tp.reshape(1), cotangent, far, out_weight, queries, head)
    adjoint = carried(qd, None, "ctx", True)
    attended = attended_of(queries, state, inner, head)
    term = weight_term(attended, cotangent, far)
    total = lax.psum_scatter(term, "ctx", scatter_dimension=0, tiled=True)
    query_g = query_grad_of(grad, values, keys, state, head)
    key_g, value_g = key_value_grad_of(queries, keys, values, grad, adjoint, head)
    total = total.astype(F32)
    total = jnp.where(tp == 0, total, jnp.concatenate([total[:, feat:], total[:, :feat]], 1))
    return query_g, key_g, value_g, total


def local(*args):
    heads = args[5].shape[0]
    n = lax.axis_size("ctx")
    if n == heads == 16 and lax.axis_size("tp") == 2:
        return local_paired(*args)
    return local_any(*args)


def solution(mesh):
    in_specs = (
        P("ctx", "tp"),
        P("ctx", "tp"),
        P("ctx", "tp"),
        P("ctx", "tp"),
        P("tp", None),
        P("tp", None, None),
    )
    out_specs = (P("ctx", "tp"), P("ctx", "tp"), P("ctx", "tp"), P(("tp", "ctx"), None))
    return jax.shard_map(local, mesh=mesh, in_specs=in_specs, out_specs=out_specs, check_vma=False)
```

```python
import functools

import jax
import jax.numpy as jnp
from jax import lax
from jax.experimental import pallas as pl
from jax.experimental.pallas import tpu as pltpu
from jax.sharding import PartitionSpec as P

BF = jnp.bfloat16
F32 = jnp.float32
NEAR = 0
SCAN = 2e10
VMEM_LIMIT = 56 * 1024 * 1024


def dot(a, b, ca, cb):
    return lax.dot_general(a, b, (((ca,), (cb,)), ((), ())), preferred_element_type=F32)


def lanes(index, head):
    return pl.ds(pl.multiple_of(index * head, head), head)


def params():
    return pltpu.CompilerParams(vmem_limit_bytes=VMEM_LIMIT)


def cost(flops, nbytes):
    return pl.CostEstimate(flops=int(flops), bytes_accessed=int(nbytes), transcendentals=0)


def kv_kernel(head, a_ref, b_ref, o_ref):
    for j in range(a_ref.shape[1] // head):
        at = slice(j * head, (j + 1) * head)
        o_ref[at, :] = dot(a_ref[:, at], b_ref[:, at], 0, 0).astype(o_ref.dtype)


def block_sums(a, b, head):
    tok, width = a.shape
    step = 2 * head
    return pl.pallas_call(
        functools.partial(kv_kernel, head),
        grid=(width // step,),
        in_specs=[pl.BlockSpec((tok, step), lambda i: (0, i))] * 2,
        out_specs=pl.BlockSpec((step, head), lambda i: (i, 0)),
        out_shape=jax.ShapeDtypeStruct((width, head), BF),
        compiler_params=params(),
        cost_estimate=cost(2 * tok * width * head, 4 * tok * width),
        name="block_sums",
    )(a, b)


def masked(tok, upper):
    row = lax.broadcasted_iota(jnp.int32, (tok, tok), 0)
    col = lax.broadcasted_iota(jnp.int32, (tok, tok), 1)
    return row <= col if upper else row >= col


def causal_apply(a, b, c, upper):
    tok = a.shape[0]
    half = tok // 2
    keep = masked(half, upper)

    def tile(x, y, diagonal):
        s = dot(x, y, 1, 1)
        if diagonal:
            s = jnp.where(keep, s, 0.0)
        return s.astype(BF)

    a0, a1, b0, b1, c0, c1 = a[:half], a[half:], b[:half], b[half:], c[:half], c[half:]
    first = dot(tile(a0, b0, True), c0, 1, 0)
    second = dot(tile(a1, b1, True), c1, 1, 0)
    if upper:
        first = first + dot(tile(a0, b1, False), c1, 1, 0)
    else:
        second = second + dot(tile(a1, b0, False), c0, 1, 0)
    return first, second


def intra_kernel(head, q_ref, k_ref, v_ref, o_ref):
    half = q_ref.shape[0] // 2
    for j in range(q_ref.shape[1] // head):
        at = slice(j * head, (j + 1) * head)
        first, second = causal_apply(q_ref[:, at], k_ref[:, at], v_ref[:, at], False)
        o_ref[:half, at] = first
        o_ref[half:, at] = second


def intra(q, k, v, head):
    tok, width = q.shape
    step = 2 * head
    spec = pl.BlockSpec((tok, step), lambda i: (0, i))
    return pl.pallas_call(
        functools.partial(intra_kernel, head),
        grid=(width // step,),
        in_specs=[spec] * 3,
        out_specs=spec,
        out_shape=jax.ShapeDtypeStruct((tok, width), F32),
        compiler_params=params(),
        cost_estimate=cost(4 * tok * tok * width, 10 * tok * width),
        name="intra",
    )(q, k, v)


def grad_kernel(head, tp_ref, own_ref, far_ref, wo_ref, wf_ref, q_ref, g_ref, s_ref):
    g = dot(own_ref[...], wo_ref[...], 1, 1) + dot(far_ref[...], wf_ref[...], 1, 1)
    g = g.astype(BF)
    g_ref[...] = g
    for j in range(g.shape[1] // head):
        at = slice(j * head, (j + 1) * head)
        s_ref[at, :] = dot(q_ref[:, at], g[:, at], 0, 0).astype(s_ref.dtype)


def out_grad_and_sums(tp, own, far, w, q, head):
    tok, feat = own.shape
    width = q.shape[1]
    step = 2 * head
    whole = pl.BlockSpec((tok, feat), lambda i, t: (0, 0))
    return pl.pallas_call(
        functools.partial(grad_kernel, head),
        grid_spec=pltpu.PrefetchScalarGridSpec(
            num_scalar_prefetch=1,
            grid=(width // step,),
            in_specs=[
                whole,
                whole,
                pl.BlockSpec((step, feat), lambda i, t: (i, t[0])),
                pl.BlockSpec((step, feat), lambda i, t: (i, 1 - t[0])),
                pl.BlockSpec((tok, step), lambda i, t: (0, i)),
            ],
            out_specs=[
                pl.BlockSpec((tok, step), lambda i, t: (0, i)),
                pl.BlockSpec((step, head), lambda i, t: (i, 0)),
            ],
        ),
        out_shape=[
            jax.ShapeDtypeStruct((tok, width), BF),
            jax.ShapeDtypeStruct((width, head), BF),
        ],
        compiler_params=params(),
        cost_estimate=cost(4 * tok * feat * width, 4 * feat * width + 4 * tok * width),
        name="out_grad",
    )(tp, own, far, w, w, q)


def attended_kernel(head, q_ref, s_ref, i_ref, o_ref):
    for j in range(q_ref.shape[1] // head):
        at = slice(j * head, (j + 1) * head)
        o_ref[:, at] = (dot(q_ref[:, at], s_ref[at, :], 1, 0) + i_ref[:, at]).astype(BF)


def attended_of(q, state, inner, head):
    tok, width = q.shape
    step = 2 * head
    spec = pl.BlockSpec((tok, step), lambda i: (0, i))
    return pl.pallas_call(
        functools.partial(attended_kernel, head),
        grid=(width // step,),
        in_specs=[spec, pl.BlockSpec((step, head), lambda i: (i, 0)), spec],
        out_specs=spec,
        out_shape=jax.ShapeDtypeStruct((tok, width), BF),
        compiler_params=params(),
        cost_estimate=cost(2 * tok * head * width, 8 * tok * width),
        name="attended",
    )(q, state, inner)


def weight_kernel(a_ref, own_ref, far_ref, o_ref):
    feat = own_ref.shape[1]
    a = a_ref[...]
    o_ref[:, :feat] = dot(a, own_ref[...], 0, 0).astype(o_ref.dtype)
    o_ref[:, feat:] = dot(a, far_ref[...], 0, 0).astype(o_ref.dtype)


def weight_term(a, own, far):
    tok, width = a.shape
    feat = own.shape[1]
    step = 256
    whole = pl.BlockSpec((tok, feat), lambda i: (0, 0))
    return pl.pallas_call(
        weight_kernel,
        grid=(width // step,),
        in_specs=[pl.BlockSpec((tok, step), lambda i: (0, i)), whole, whole],
        out_specs=pl.BlockSpec((step, 2 * feat), lambda i: (i, 0)),
        out_shape=jax.ShapeDtypeStruct((width, 2 * feat), BF),
        compiler_params=params(),
        cost_estimate=cost(4 * tok * feat * width, 4 * feat * width + 2 * tok * width),
        name="weight_term",
    )(a, own, far)


def query_kernel(head, g_ref, v_ref, k_ref, s_ref, o_ref):
    half = g_ref.shape[0] // 2
    for j in range(g_ref.shape[1] // head):
        at = slice(j * head, (j + 1) * head)
        g = g_ref[:, at]
        first, second = causal_apply(g, v_ref[:, at], k_ref[:, at], False)
        carried = dot(g, s_ref[at, :], 1, 1)
        o_ref[:half, at] = (first + carried[:half]).astype(BF)
        o_ref[half:, at] = (second + carried[half:]).astype(BF)


def query_grad_of(g, v, k, state, head):
    tok, width = g.shape
    step = 2 * head
    spec = pl.BlockSpec((tok, step), lambda i: (0, i))
    return pl.pallas_call(
        functools.partial(query_kernel, head),
        grid=(width // step,),
        in_specs=[spec, spec, spec, pl.BlockSpec((step, head), lambda i: (i, 0))],
        out_specs=spec,
        out_shape=jax.ShapeDtypeStruct((tok, width), BF),
        compiler_params=params(),
        cost_estimate=cost(4 * tok * tok * width, 8 * tok * width),
        name="query_grad",
    )(g, v, k, state)


def key_value_kernel(head, q_ref, k_ref, v_ref, g_ref, a_ref, ko_ref, vo_ref):
    half = g_ref.shape[0] // 2
    for j in range(g_ref.shape[1] // head):
        at = slice(j * head, (j + 1) * head)
        q, k, v, g, adj = q_ref[:, at], k_ref[:, at], v_ref[:, at], g_ref[:, at], a_ref[at, :]
        first, second = causal_apply(v, g, q, True)
        carried = dot(v, adj, 1, 1)
        ko_ref[:half, at] = (first + carried[:half]).astype(BF)
        ko_ref[half:, at] = (second + carried[half:]).astype(BF)
        first, second = causal_apply(k, q, g, True)
        carried = dot(k, adj, 1, 0)
        vo_ref[:half, at] = (first + carried[:half]).astype(BF)
        vo_ref[half:, at] = (second + carried[half:]).astype(BF)


def key_value_grad_of(q, k, v, g, adjoint, head):
    tok, width = g.shape
    step = 2 * head
    spec = pl.BlockSpec((tok, step), lambda i: (0, i))
    shape = jax.ShapeDtypeStruct((tok, width), BF)
    return pl.pallas_call(
        functools.partial(key_value_kernel, head),
        grid=(width // step,),
        in_specs=[spec, spec, spec, spec, pl.BlockSpec((step, head), lambda i: (i, 0))],
        out_specs=[spec, spec],
        out_shape=[shape, shape],
        compiler_params=params(),
        cost_estimate=cost(8 * tok * tok * width, 12 * tok * width),
        name="key_value_grad",
    )(q, k, v, g, adjoint)


ANY = pl.BlockSpec(memory_space=pl.ANY)


def scan_kernel(n, reverse, waits, x_ref, *refs):
    o_ref = refs[waits]
    rows = x_ref.shape[0] // n
    total = jnp.zeros((rows, x_ref.shape[1]), F32) if reverse else refs[0][...]
    for i in range(n):
        c = n - 1 - i if reverse else i
        at = slice(c * rows, (c + 1) * rows)
        o_ref[at, :] = total.astype(BF)
        total = total + x_ref[at, :].astype(F32)


def scan_blocks(x, start, n, reverse, after=(), passed=None):
    more = () if passed is None else (passed,)
    first = () if reverse else (start,)
    out = pl.pallas_call(
        functools.partial(scan_kernel, n, reverse, len(first) + len(after) + len(more)),
        in_specs=[pl.BlockSpec(y.shape, lambda: (0, 0)) for y in (x, *first)]
        + [ANY] * (len(after) + len(more)),
        out_specs=[pl.BlockSpec(x.shape, lambda: (0, 0))] + [ANY] * len(more),
        out_shape=[jax.ShapeDtypeStruct(x.shape, BF)]
        + [jax.ShapeDtypeStruct(p.shape, p.dtype) for p in more],
        input_output_aliases={1 + len(first) + len(after): 1} if more else {},
        compiler_params=params(),
        cost_estimate=cost(SCAN, 0),
        name="scan_blocks",
    )(x, *first, *after, *more)
    return out if more else out[0]


def carried(x, start, axis, reverse):
    n = lax.axis_size(axis)
    mine = lax.all_to_all(x, axis, 0, 0, tiled=True)
    return lax.all_to_all(scan_blocks(mine, start, n, reverse), axis, 0, 0, tiled=True)


def pair_sums_kernel(head, me_ref, a_ref, b_ref, mine_ref, send_ref):
    core = me_ref[0] % 2
    for j in range(a_ref.shape[1] // (2 * head)):
        at = slice(j * head, (j + 1) * head)
        for o_ref, side in ((send_ref, 1 - core), (mine_ref, core)):
            pick = lanes(2 * j + side, head)
            o_ref[at, :] = dot(a_ref[:, pick], b_ref[:, pick], 0, 0).astype(BF)


def pair_sums(me, a, b, head):
    tok, width = a.shape
    step = min(4 * head, width)
    spec = pl.BlockSpec((tok, step), lambda i, m: (0, i))
    out = pl.BlockSpec((step // 2, head), lambda i, m: (i, 0))
    shape = jax.ShapeDtypeStruct((width // 2, head), BF)
    return pl.pallas_call(
        functools.partial(pair_sums_kernel, head),
        grid_spec=pltpu.PrefetchScalarGridSpec(
            num_scalar_prefetch=1,
            grid=(width // step,),
            in_specs=[spec] * 2,
            out_specs=[out] * 2,
        ),
        out_shape=[shape] * 2,
        compiler_params=params(),
        cost_estimate=cost(2 * tok * width * head, 4 * tok * width),
        name="pair_sums",
    )(me, a, b)


def pair_intra_kernel(head, waits, me_ref, *refs):
    q_ref, k_ref, v_ref, mine_ref, send_ref = refs[waits:]
    core = me_ref[0] % 2
    half = q_ref.shape[0] // 2
    for j in range(q_ref.shape[1] // (2 * head)):
        for o_ref, side, base in ((send_ref, 1 - core, (2 * j + 1) * head), (mine_ref, core, j * head)):
            pick = lanes(2 * j + side, head)
            first, second = causal_apply(q_ref[:, pick], k_ref[:, pick], v_ref[:, pick], False)
            o_ref[base : base + head, :half] = first.astype(BF).T
            o_ref[base : base + head, half:] = second.astype(BF).T
        send_ref[2 * j * head : (2 * j + 1) * head, :] = q_ref[:, lanes(2 * j + 1 - core, head)].T


def pair_intra(me, after, q, k, v, head):
    tok, width = q.shape
    step = min(4 * head, width)
    spec = pl.BlockSpec((tok, step), lambda i, m: (0, i))
    return pl.pallas_call(
        functools.partial(pair_intra_kernel, head, len(after)),
        grid_spec=pltpu.PrefetchScalarGridSpec(
            num_scalar_prefetch=1,
            grid=(width // step,),
            in_specs=[ANY] * len(after) + [spec] * 3,
            out_specs=[
                pl.BlockSpec((step // 2, tok), lambda i, m: (i, 0)),
                pl.BlockSpec((step, tok), lambda i, m: (i, 0)),
            ],
        ),
        out_shape=[
            jax.ShapeDtypeStruct((width // 2, tok), BF),
            jax.ShapeDtypeStruct((width, tok), BF),
        ],
        compiler_params=params(),
        cost_estimate=cost(4 * tok * tok * width, 9 * tok * width),
        name="pair_intra",
    )(me, *after, q, k, v)


def pair_attended_kernel(head, me_ref, after_ref, q0_ref, q1_ref, i_ref, far_ref, s_ref, own_ref, oth_ref,
                         mine_ref, cross_ref, near_ref, away_ref):
    core = (me_ref[0] % 2).astype(F32)
    south = (me_ref[0] // 2) % 2

    def fill(q_ref, side, o_ref):
        rows = lanes(side, head)
        state = s_ref[rows, :].astype(F32)
        near = (state + core * oth_ref[rows, :].astype(F32)).astype(BF)
        away = (state + (1.0 - core) * own_ref[rows, :].astype(F32)).astype(BF)
        away_ref[rows, :] = away
        here = dot(near, q_ref[...], 0, 1) + i_ref[rows, :].astype(F32)
        there = dot(away, far_ref[lanes(2 * side, head), :], 0, 0)
        there = there + far_ref[lanes(2 * side + 1, head), :].astype(F32)
        o_ref[0, 0] = here.astype(BF)
        o_ref[0, 1] = there.astype(BF)

    fill(q0_ref, south, mine_ref)
    crossing = pl.program_id(0) < pl.num_programs(0) // 2
    pl.when(crossing)(lambda: fill(q1_ref, 1 - south, cross_ref))
    pl.when(jnp.logical_not(crossing))(lambda: fill(q1_ref, 1 - south, near_ref))


def pair_attended(me, after, q, inner, far, state, own, oth, head):
    tok, width = q.shape
    places = width // (4 * head)
    half = places // 2

    def place(i, m):
        return (m[0] // 4) ^ i ^ half

    rows = pl.BlockSpec((2 * head, head), lambda i, m: (place(i, m), 0))

    def out(index):
        return pl.BlockSpec((1, 2, head, tok), lambda i, m: (index(i), 0, 0, 0))

    def shape(count):
        return jax.ShapeDtypeStruct((count, 2, head, tok), BF)

    return pl.pallas_call(
        functools.partial(pair_attended_kernel, head),
        grid_spec=pltpu.PrefetchScalarGridSpec(
            num_scalar_prefetch=1,
            grid=(places,),
            in_specs=[
                ANY,
                pl.BlockSpec((tok, head), lambda i, m: (0, 4 * place(i, m) + m[0] % 4)),
                pl.BlockSpec((tok, head), lambda i, m: (0, 4 * place(i, m) + (m[0] % 4 ^ 2))),
                pl.BlockSpec((2 * head, tok), lambda i, m: (place(i, m), 0)),
                pl.BlockSpec((4 * head, tok), lambda i, m: (place(i, m), 0)),
            ]
            + [rows] * 3,
            out_specs=[
                out(lambda i: i ^ half),
                out(lambda i: jnp.minimum(i, half - 1)),
                out(lambda i: jnp.maximum(i - half, 0)),
                rows,
            ],
        ),
        out_shape=[
            shape(places),
            shape(half),
            shape(half),
            jax.ShapeDtypeStruct((width // 2, head), BF),
        ],
        compiler_params=params(),
        cost_estimate=cost(2 * tok * head * width, 10 * tok * width),
        name="pair_attended",
    )(me, after, q, q, inner, far, state, own, oth)


def quad_weight_kernel(waits, tp_ref, a_ref, b_ref, *refs):
    half, _, head, tok = a_ref.shape
    ins, outs, a_all, c_all = refs[:8], refs[8 + waits : -2], refs[-2], refs[-1]

    @pl.when(pl.program_id(0) == 0)
    def _():
        for k in range(4):
            block = (a_ref if k < 2 else b_ref)[:, k % 2]
            a_all[:, k * tok : (k + 1) * tok] = block.reshape(half * head, tok)

    def product(part):
        for k in range(4):
            c_all[k * tok : (k + 1) * tok, :] = ins[2 * k + part][...]
        total = dot(a_all[...], c_all[...], 1, 0)
        for i, o_ref in enumerate(outs):
            o_ref[...] = total[i * head : (i + 1) * head].astype(BF)

    steps = pl.num_programs(0) // 2
    pl.when(pl.program_id(0) < steps)(lambda: product(0))
    pl.when(pl.program_id(0) >= steps)(lambda: product(1))


def quad_weight(tp, after, a, b, cots, far_side):
    places, _, head, tok = a.shape
    half = places // 2
    feat = cots[0].shape[1]
    step = min(512, feat)
    steps = feat // step
    whole = pl.BlockSpec((half,) + a.shape[1:], lambda i, t: (far_side, 0, 0, 0))
    own = pl.BlockSpec((tok, step), lambda i, t: (0, jnp.minimum(i, steps - 1)))
    other = pl.BlockSpec((tok, step), lambda i, t: (0, jnp.maximum(i - steps, 0)))
    return pl.pallas_call(
        functools.partial(quad_weight_kernel, len(after)),
        grid_spec=pltpu.PrefetchScalarGridSpec(
            num_scalar_prefetch=1,
            grid=(2 * steps,),
            in_specs=[whole, pl.BlockSpec(b.shape, lambda i, t: (0, 0, 0, 0))] + [own, other] * 4 + [ANY] * len(after),
            out_specs=[
                pl.BlockSpec((head, step), lambda i, t: (0, (i + t[0] * steps) % (2 * steps)))
            ]
            * half,
            scratch_shapes=[
                pltpu.VMEM((half * head, 4 * tok), BF),
                pltpu.VMEM((4 * tok, step), BF),
            ],
        ),
        out_shape=[jax.ShapeDtypeStruct((head, 2 * feat), BF)] * half,
        compiler_params=params(),
        cost_estimate=cost(2e10 if far_side else NEAR, 0),
        name="quad_weight",
    )(tp, a, b, *cots, *after)


def pair_query_kernel(head, me_ref, after_ref, so_far_ref, g_ref, v_ref, k_ref, s_ref, kv_ref, t_ref, o_ref):
    core = me_ref[0] % 2
    half = g_ref.shape[0] // 2
    for j in range(g_ref.shape[1] // head):
        at, row = slice(j * head, (j + 1) * head), slice(j // 2 * head, (j // 2 + 1) * head)
        g = g_ref[:, at]
        near = s_ref[row, :].astype(F32) + core.astype(F32) * kv_ref[row, :].astype(F32)
        state = jnp.where(core == j % 2, near.astype(BF), t_ref[row, :])
        first_half, second_half = causal_apply(g, v_ref[:, at], k_ref[:, at], False)
        over = dot(g, state, 1, 1)
        o_ref[:half, at] = (first_half + over[:half]).astype(BF)
        o_ref[half:, at] = (second_half + over[half:]).astype(BF)


def pair_query_grad(me, part, after, so_far, g, v, k, state, kv, other, head):
    tok, width = g.shape
    step = min(4 * head, width // 2)
    steps = width // 2 // step
    spec = pl.BlockSpec((tok, step), lambda i, m: (0, i + part * steps))
    rows = pl.BlockSpec((step // 2, head), lambda i, m: (i + part * steps, 0))
    return pl.pallas_call(
        functools.partial(pair_query_kernel, head),
        grid_spec=pltpu.PrefetchScalarGridSpec(
            num_scalar_prefetch=1,
            grid=(steps,),
            in_specs=[ANY, ANY, spec, spec, spec, rows, rows, rows],
            out_specs=spec,
        ),
        out_shape=jax.ShapeDtypeStruct((tok, width), BF),
        input_output_aliases={2: 0} if part else {},
        compiler_params=params(),
        cost_estimate=cost(0, 0),
        name="query_grad",
    )(me, after, so_far, g, v, k, state, kv, other)


def pair_grad_kernel(head, waits, me_ref, tp_ref, own_ref, far_ref, w_ref, q_ref, *refs):
    g_ref, mine_ref, send_ref = refs[waits : waits + 3]
    cot_ref = refs[-1]
    feat = own_ref.shape[1]

    @pl.when(pl.program_id(0) == 0)
    def _():
        cot_ref[:, lanes(tp_ref[0], feat)] = own_ref[...]
        cot_ref[:, lanes(1 - tp_ref[0], feat)] = far_ref[...]

    core = me_ref[0] % 2
    g_ref[...] = dot(cot_ref[...], w_ref[...], 1, 1).astype(BF)
    for j in range(g_ref.shape[1] // (2 * head)):
        at = slice(j * head, (j + 1) * head)
        for o_ref, side in ((send_ref, 1 - core), (mine_ref, core)):
            pick = lanes(2 * j + side, head)
            o_ref[at, :] = dot(q_ref[:, pick], g_ref[:, pick], 0, 0).astype(BF)


def pair_grad(me, tp, after, own, far, w, q, head):
    tok, feat = own.shape
    width = q.shape[1]
    step = min(4 * head, width)
    whole = pl.BlockSpec((tok, feat), lambda i, m, t: (0, 0))
    rows = pl.BlockSpec((step // 2, head), lambda i, m, t: (i, 0))
    cols = pl.BlockSpec((tok, step), lambda i, m, t: (0, i))
    sums = jax.ShapeDtypeStruct((width // 2, head), BF)
    return pl.pallas_call(
        functools.partial(pair_grad_kernel, head, len(after)),
        grid_spec=pltpu.PrefetchScalarGridSpec(
            num_scalar_prefetch=2,
            grid=(width // step,),
            in_specs=[
                whole,
                whole,
                pl.BlockSpec((step, 2 * feat), lambda i, m, t: (i, 0)),
                cols,
            ]
            + [ANY] * len(after),
            out_specs=[cols, rows, rows],
            scratch_shapes=[pltpu.VMEM((tok, 2 * feat), BF)],
        ),
        out_shape=[jax.ShapeDtypeStruct((tok, width), BF), sums, sums],
        compiler_params=params(),
        cost_estimate=cost(4 * tok * feat * width, 4 * feat * width + 4 * tok * width),
        name="out_grad",
    )(me, tp, own, far, w, q, *after)


def pass_kernel(*refs):
    pass


def passed_after(x, after, flops):
    return pl.pallas_call(
        pass_kernel,
        in_specs=[ANY] * (1 + len(after)),
        out_specs=ANY,
        out_shape=jax.ShapeDtypeStruct(x.shape, x.dtype),
        input_output_aliases={0: 0},
        compiler_params=params(),
        cost_estimate=cost(flops, 0),
        name="passed_after",
    )(x, *after)


def add_kernel(after_ref, a_ref, b_ref, o_ref):
    o_ref[...] = (a_ref[...].astype(F32) + b_ref[...].astype(F32)).astype(BF)


def add_after(after, a, b):
    spec = pl.BlockSpec(a.shape, lambda: (0, 0))
    return pl.pallas_call(
        add_kernel,
        in_specs=[ANY, spec, spec],
        out_specs=spec,
        out_shape=jax.ShapeDtypeStruct(a.shape, BF),
        compiler_params=params(),
        cost_estimate=cost(0, 0),
        name="add_after",
    )(after, a, b)


def key_value_inner_kernel(head, after_ref, q_ref, k_ref, v_ref, g_ref, ko_ref, vo_ref):
    half = g_ref.shape[0] // 2
    for j in range(g_ref.shape[1] // head):
        at = slice(j * head, (j + 1) * head)
        q, k, v, g = q_ref[:, at], k_ref[:, at], v_ref[:, at], g_ref[:, at]
        first, second = causal_apply(v, g, q, True)
        ko_ref[:half, at] = first.astype(BF)
        ko_ref[half:, at] = second.astype(BF)
        first, second = causal_apply(k, q, g, True)
        vo_ref[:half, at] = first.astype(BF)
        vo_ref[half:, at] = second.astype(BF)


def key_value_inner(after, q, k, v, g, head):
    tok, width = g.shape
    step = min(4 * head, width)
    spec = pl.BlockSpec((tok, step), lambda i: (0, i))
    shape = jax.ShapeDtypeStruct((tok, width), BF)
    return pl.pallas_call(
        functools.partial(key_value_inner_kernel, head),
        grid=(width // step,),
        in_specs=[ANY, spec, spec, spec, spec],
        out_specs=[spec, spec],
        out_shape=[shape, shape],
        compiler_params=params(),
        cost_estimate=cost(0, 0),
        name="key_value_inner",
    )(after, q, k, v, g)


def key_value_outer_kernel(head, me_ref, k_ref, v_ref, ki_ref, vi_ref, s_ref, qd_ref, t_ref, ko_ref, vo_ref):
    core = me_ref[0] % 2
    for j in range(k_ref.shape[1] // head):
        at, row = slice(j * head, (j + 1) * head), slice(j // 2 * head, (j // 2 + 1) * head)
        near = s_ref[row, :].astype(F32) + (1 - core).astype(F32) * qd_ref[row, :].astype(F32)
        adj = jnp.where(core == j % 2, near.astype(BF), t_ref[row, :])
        ko_ref[:, at] = (dot(v_ref[:, at], adj, 1, 1) + ki_ref[:, at].astype(F32)).astype(BF)
        vo_ref[:, at] = (dot(k_ref[:, at], adj, 1, 0) + vi_ref[:, at].astype(F32)).astype(BF)


def key_value_outer(me, k, v, key_inner, value_inner, adjoint, qd, other, head):
    tok, width = k.shape
    step = min(4 * head, width)
    spec = pl.BlockSpec((tok, step), lambda i, m: (0, i))
    rows = pl.BlockSpec((step // 2, head), lambda i, m: (i, 0))
    shape = jax.ShapeDtypeStruct((tok, width), BF)
    return pl.pallas_call(
        functools.partial(key_value_outer_kernel, head),
        grid_spec=pltpu.PrefetchScalarGridSpec(
            num_scalar_prefetch=1,
            grid=(width // step,),
            in_specs=[spec, spec, spec, spec, rows, rows, rows],
            out_specs=[spec, spec],
        ),
        out_shape=[shape, shape],
        compiler_params=params(),
        cost_estimate=cost(0, 0),
        name="key_value_outer",
    )(me, k, v, key_inner, value_inner, adjoint, qd, other)


def local_paired(queries, keys, values, cotangent, out_weight, memory):
    head = memory.shape[2]
    n = lax.axis_size("ctx")
    me, tp = lax.axis_index("ctx"), lax.axis_index("tp")
    who, which = me.reshape(1), tp.reshape(1)
    core = (me % 2).astype(F32)
    groups = [[c for c in range(n) if c % 2 == side] for side in range(2)]

    def swap(x, bit):
        return lax.ppermute(x, "ctx", [(c, c ^ bit) for c in range(n)])

    def swap_tp(x):
        return lax.ppermute(x, "tp", [(0, 1), (1, 0)])

    def across(x):
        return lax.all_to_all(x, "ctx", 0, 0, axis_index_groups=groups, tiled=True)

    def added(x, factor, y):
        return (x.astype(F32) + factor * y.astype(F32)).astype(BF)

    kv_mine, kv_send = pair_sums(who, keys, values, head)
    kv_other = swap(kv_send, 1)
    far = swap_tp(cotangent)
    south = swap(cotangent, 2)
    chip = added(kv_mine, 1.0, kv_other)
    inner, sent = pair_intra(who, (chip,), queries, keys, values, head)
    start = lax.dynamic_index_in_dim(memory, me, 0, False)
    scanned, sent = scan_blocks(across(chip), start, n // 2, False, (inner, far, south), sent)
    state = across(scanned)

    far_south = swap_tp(south)
    grad, qd_mine, qd_send = pair_grad(
        who, which, (scanned, south), cotangent, far, out_weight, queries, head
    )
    mine, send, send_near, away = pair_attended(
        who, grad, queries, inner, swap(sent, 1), state, kv_mine, kv_other, head
    )
    received, received_near = swap(send, 2), swap(send_near, 2)
    state_other = swap(away, 1)

    qd_other = swap(qd_send, 1)
    chip = add_after(send, qd_mine, qd_other)
    cots = [cotangent, far, swap(cotangent, 1), swap(far, 1)]
    cots += [south, far_south, swap(south, 1), swap(far_south, 1)]

    query_args = (grad, values, keys, state, kv_other, state_other, head)
    query_g = pair_query_grad(who, 0, chip, grad, *query_args)
    received = passed_after(received, (query_g,), 2e10)
    crossing = quad_weight(which, (), mine, received, cots, 1)
    summed = added(crossing[0], 1.0, swap(crossing[1], 4))
    crossed = swap(summed, 8)
    scanned = scan_blocks(across(chip), None, n // 2, True, (crossing[0],))
    after_chip = across(scanned)
    same = quad_weight(which, (scanned,), mine, received_near, cots, 0)
    neighbour = swap(same[1], 4)
    query_g = pair_query_grad(who, 1, summed, query_g, *query_args)
    inners = key_value_inner(query_g, queries, keys, values, grad, head)
    after_chip = passed_after(after_chip, (inners[0],), 0)
    adjoint_other = swap(added(after_chip, core, qd_mine), 1)
    key_g, value_g = key_value_outer(
        who, keys, values, *inners, after_chip, qd_other, adjoint_other, head
    )
    total = same[0].astype(F32) + neighbour.astype(F32) + crossed.astype(F32)
    return query_g, key_g, value_g, total


def local_any(queries, keys, values, cotangent, out_weight, memory):
    head = memory.shape[2]
    width = queries.shape[1]
    feat = cotangent.shape[1]
    n = lax.axis_size("ctx")
    rows = width // n
    me, tp = lax.axis_index("ctx"), lax.axis_index("tp")

    far = lax.ppermute(cotangent, "tp", [(0, 1), (1, 0)])
    kv = block_sums(keys, values, head)
    start = lax.dynamic_slice_in_dim(memory.reshape(width, head), me * rows, rows, 0)
    state = carried(kv, start, "ctx", False)
    inner = intra(queries, keys, values, head)
    grad, qd = out_grad_and_sums(tp.reshape(1), cotangent, far, out_weight, queries, head)
    adjoint = carried(qd, None, "ctx", True)
    attended = attended_of(queries, state, inner, head)
    term = weight_term(attended, cotangent, far)
    total = lax.psum_scatter(term, "ctx", scatter_dimension=0, tiled=True)
    query_g = query_grad_of(grad, values, keys, state, head)
    key_g, value_g = key_value_grad_of(queries, keys, values, grad, adjoint, head)
    total = total.astype(F32)
    total = jnp.where(tp == 0, total, jnp.concatenate([total[:, feat:], total[:, :feat]], 1))
    return query_g, key_g, value_g, total


def local(*args):
    heads = args[5].shape[0]
    n = lax.axis_size("ctx")
    if n == heads == 16 and lax.axis_size("tp") == 2:
        return local_paired(*args)
    return local_any(*args)


def solution(mesh):
    in_specs = (
        P("ctx", "tp"),
        P("ctx", "tp"),
        P("ctx", "tp"),
        P("ctx", "tp"),
        P("tp", None),
        P("tp", None, None),
    )
    out_specs = (P("ctx", "tp"), P("ctx", "tp"), P("ctx", "tp"), P(("tp", "ctx"), None))
    return jax.shard_map(local, mesh=mesh, in_specs=in_specs, out_specs=out_specs, check_vma=False)
```

```python
import functools

import jax
import jax.numpy as jnp
from jax import lax
from jax.experimental import pallas as pl
from jax.experimental.pallas import tpu as pltpu
from jax.sharding import PartitionSpec as P

BF = jnp.bfloat16
F32 = jnp.float32
NEAR = 0
SCAN = 2e10
VMEM_LIMIT = 56 * 1024 * 1024


def dot(a, b, ca, cb):
    return lax.dot_general(a, b, (((ca,), (cb,)), ((), ())), preferred_element_type=F32)


def lanes(index, head):
    return pl.ds(pl.multiple_of(index * head, head), head)


def params():
    return pltpu.CompilerParams(vmem_limit_bytes=VMEM_LIMIT)


def cost(flops, nbytes):
    return pl.CostEstimate(flops=int(flops), bytes_accessed=int(nbytes), transcendentals=0)


def kv_kernel(head, a_ref, b_ref, o_ref):
    for j in range(a_ref.shape[1] // head):
        at = slice(j * head, (j + 1) * head)
        o_ref[at, :] = dot(a_ref[:, at], b_ref[:, at], 0, 0).astype(o_ref.dtype)


def block_sums(a, b, head):
    tok, width = a.shape
    step = 2 * head
    return pl.pallas_call(
        functools.partial(kv_kernel, head),
        grid=(width // step,),
        in_specs=[pl.BlockSpec((tok, step), lambda i: (0, i))] * 2,
        out_specs=pl.BlockSpec((step, head), lambda i: (i, 0)),
        out_shape=jax.ShapeDtypeStruct((width, head), BF),
        compiler_params=params(),
        cost_estimate=cost(2 * tok * width * head, 4 * tok * width),
        name="block_sums",
    )(a, b)


def masked(tok, upper):
    row = lax.broadcasted_iota(jnp.int32, (tok, tok), 0)
    col = lax.broadcasted_iota(jnp.int32, (tok, tok), 1)
    return row <= col if upper else row >= col


def causal_apply(a, b, c, upper):
    tok = a.shape[0]
    half = tok // 2
    keep = masked(half, upper)

    def tile(x, y, diagonal):
        s = dot(x, y, 1, 1)
        if diagonal:
            s = jnp.where(keep, s, 0.0)
        return s.astype(BF)

    a0, a1, b0, b1, c0, c1 = a[:half], a[half:], b[:half], b[half:], c[:half], c[half:]
    first = dot(tile(a0, b0, True), c0, 1, 0)
    second = dot(tile(a1, b1, True), c1, 1, 0)
    if upper:
        first = first + dot(tile(a0, b1, False), c1, 1, 0)
    else:
        second = second + dot(tile(a1, b0, False), c0, 1, 0)
    return first, second


def intra_kernel(head, q_ref, k_ref, v_ref, o_ref):
    half = q_ref.shape[0] // 2
    for j in range(q_ref.shape[1] // head):
        at = slice(j * head, (j + 1) * head)
        first, second = causal_apply(q_ref[:, at], k_ref[:, at], v_ref[:, at], False)
        o_ref[:half, at] = first
        o_ref[half:, at] = second


def intra(q, k, v, head):
    tok, width = q.shape
    step = 2 * head
    spec = pl.BlockSpec((tok, step), lambda i: (0, i))
    return pl.pallas_call(
        functools.partial(intra_kernel, head),
        grid=(width // step,),
        in_specs=[spec] * 3,
        out_specs=spec,
        out_shape=jax.ShapeDtypeStruct((tok, width), F32),
        compiler_params=params(),
        cost_estimate=cost(4 * tok * tok * width, 10 * tok * width),
        name="intra",
    )(q, k, v)


def grad_kernel(head, tp_ref, own_ref, far_ref, wo_ref, wf_ref, q_ref, g_ref, s_ref):
    g = dot(own_ref[...], wo_ref[...], 1, 1) + dot(far_ref[...], wf_ref[...], 1, 1)
    g = g.astype(BF)
    g_ref[...] = g
    for j in range(g.shape[1] // head):
        at = slice(j * head, (j + 1) * head)
        s_ref[at, :] = dot(q_ref[:, at], g[:, at], 0, 0).astype(s_ref.dtype)


def out_grad_and_sums(tp, own, far, w, q, head):
    tok, feat = own.shape
    width = q.shape[1]
    step = 2 * head
    whole = pl.BlockSpec((tok, feat), lambda i, t: (0, 0))
    return pl.pallas_call(
        functools.partial(grad_kernel, head),
        grid_spec=pltpu.PrefetchScalarGridSpec(
            num_scalar_prefetch=1,
            grid=(width // step,),
            in_specs=[
                whole,
                whole,
                pl.BlockSpec((step, feat), lambda i, t: (i, t[0])),
                pl.BlockSpec((step, feat), lambda i, t: (i, 1 - t[0])),
                pl.BlockSpec((tok, step), lambda i, t: (0, i)),
            ],
            out_specs=[
                pl.BlockSpec((tok, step), lambda i, t: (0, i)),
                pl.BlockSpec((step, head), lambda i, t: (i, 0)),
            ],
        ),
        out_shape=[
            jax.ShapeDtypeStruct((tok, width), BF),
            jax.ShapeDtypeStruct((width, head), BF),
        ],
        compiler_params=params(),
        cost_estimate=cost(4 * tok * feat * width, 4 * feat * width + 4 * tok * width),
        name="out_grad",
    )(tp, own, far, w, w, q)


def attended_kernel(head, q_ref, s_ref, i_ref, o_ref):
    for j in range(q_ref.shape[1] // head):
        at = slice(j * head, (j + 1) * head)
        o_ref[:, at] = (dot(q_ref[:, at], s_ref[at, :], 1, 0) + i_ref[:, at]).astype(BF)


def attended_of(q, state, inner, head):
    tok, width = q.shape
    step = 2 * head
    spec = pl.BlockSpec((tok, step), lambda i: (0, i))
    return pl.pallas_call(
        functools.partial(attended_kernel, head),
        grid=(width // step,),
        in_specs=[spec, pl.BlockSpec((step, head), lambda i: (i, 0)), spec],
        out_specs=spec,
        out_shape=jax.ShapeDtypeStruct((tok, width), BF),
        compiler_params=params(),
        cost_estimate=cost(2 * tok * head * width, 8 * tok * width),
        name="attended",
    )(q, state, inner)


def weight_kernel(a_ref, own_ref, far_ref, o_ref):
    feat = own_ref.shape[1]
    a = a_ref[...]
    o_ref[:, :feat] = dot(a, own_ref[...], 0, 0).astype(o_ref.dtype)
    o_ref[:, feat:] = dot(a, far_ref[...], 0, 0).astype(o_ref.dtype)


def weight_term(a, own, far):
    tok, width = a.shape
    feat = own.shape[1]
    step = 256
    whole = pl.BlockSpec((tok, feat), lambda i: (0, 0))
    return pl.pallas_call(
        weight_kernel,
        grid=(width // step,),
        in_specs=[pl.BlockSpec((tok, step), lambda i: (0, i)), whole, whole],
        out_specs=pl.BlockSpec((step, 2 * feat), lambda i: (i, 0)),
        out_shape=jax.ShapeDtypeStruct((width, 2 * feat), BF),
        compiler_params=params(),
        cost_estimate=cost(4 * tok * feat * width, 4 * feat * width + 2 * tok * width),
        name="weight_term",
    )(a, own, far)


def query_kernel(head, g_ref, v_ref, k_ref, s_ref, o_ref):
    half = g_ref.shape[0] // 2
    for j in range(g_ref.shape[1] // head):
        at = slice(j * head, (j + 1) * head)
        g = g_ref[:, at]
        first, second = causal_apply(g, v_ref[:, at], k_ref[:, at], False)
        carried = dot(g, s_ref[at, :], 1, 1)
        o_ref[:half, at] = (first + carried[:half]).astype(BF)
        o_ref[half:, at] = (second + carried[half:]).astype(BF)


def query_grad_of(g, v, k, state, head):
    tok, width = g.shape
    step = 2 * head
    spec = pl.BlockSpec((tok, step), lambda i: (0, i))
    return pl.pallas_call(
        functools.partial(query_kernel, head),
        grid=(width // step,),
        in_specs=[spec, spec, spec, pl.BlockSpec((step, head), lambda i: (i, 0))],
        out_specs=spec,
        out_shape=jax.ShapeDtypeStruct((tok, width), BF),
        compiler_params=params(),
        cost_estimate=cost(4 * tok * tok * width, 8 * tok * width),
        name="query_grad",
    )(g, v, k, state)


def key_value_kernel(head, q_ref, k_ref, v_ref, g_ref, a_ref, ko_ref, vo_ref):
    half = g_ref.shape[0] // 2
    for j in range(g_ref.shape[1] // head):
        at = slice(j * head, (j + 1) * head)
        q, k, v, g, adj = q_ref[:, at], k_ref[:, at], v_ref[:, at], g_ref[:, at], a_ref[at, :]
        first, second = causal_apply(v, g, q, True)
        carried = dot(v, adj, 1, 1)
        ko_ref[:half, at] = (first + carried[:half]).astype(BF)
        ko_ref[half:, at] = (second + carried[half:]).astype(BF)
        first, second = causal_apply(k, q, g, True)
        carried = dot(k, adj, 1, 0)
        vo_ref[:half, at] = (first + carried[:half]).astype(BF)
        vo_ref[half:, at] = (second + carried[half:]).astype(BF)


def key_value_grad_of(q, k, v, g, adjoint, head):
    tok, width = g.shape
    step = 2 * head
    spec = pl.BlockSpec((tok, step), lambda i: (0, i))
    shape = jax.ShapeDtypeStruct((tok, width), BF)
    return pl.pallas_call(
        functools.partial(key_value_kernel, head),
        grid=(width // step,),
        in_specs=[spec, spec, spec, spec, pl.BlockSpec((step, head), lambda i: (i, 0))],
        out_specs=[spec, spec],
        out_shape=[shape, shape],
        compiler_params=params(),
        cost_estimate=cost(8 * tok * tok * width, 12 * tok * width),
        name="key_value_grad",
    )(q, k, v, g, adjoint)


ANY = pl.BlockSpec(memory_space=pl.ANY)


def scan_kernel(n, reverse, waits, x_ref, *refs):
    o_ref = refs[waits]
    rows = x_ref.shape[0] // n
    total = jnp.zeros((rows, x_ref.shape[1]), F32) if reverse else refs[0][...]
    for i in range(n):
        c = n - 1 - i if reverse else i
        at = slice(c * rows, (c + 1) * rows)
        o_ref[at, :] = total.astype(BF)
        total = total + x_ref[at, :].astype(F32)


def scan_blocks(x, start, n, reverse, after=(), passed=None):
    more = () if passed is None else (passed,)
    first = () if reverse else (start,)
    out = pl.pallas_call(
        functools.partial(scan_kernel, n, reverse, len(first) + len(after) + len(more)),
        in_specs=[pl.BlockSpec(y.shape, lambda: (0, 0)) for y in (x, *first)]
        + [ANY] * (len(after) + len(more)),
        out_specs=[pl.BlockSpec(x.shape, lambda: (0, 0))] + [ANY] * len(more),
        out_shape=[jax.ShapeDtypeStruct(x.shape, BF)]
        + [jax.ShapeDtypeStruct(p.shape, p.dtype) for p in more],
        input_output_aliases={1 + len(first) + len(after): 1} if more else {},
        compiler_params=params(),
        cost_estimate=cost(SCAN, 0),
        name="scan_blocks",
    )(x, *first, *after, *more)
    return out if more else out[0]


def carried(x, start, axis, reverse):
    n = lax.axis_size(axis)
    mine = lax.all_to_all(x, axis, 0, 0, tiled=True)
    return lax.all_to_all(scan_blocks(mine, start, n, reverse), axis, 0, 0, tiled=True)


def pair_sums_kernel(head, me_ref, a_ref, b_ref, mine_ref, send_ref):
    core = me_ref[0] % 2
    for j in range(a_ref.shape[1] // (2 * head)):
        at = slice(j * head, (j + 1) * head)
        for o_ref, side in ((send_ref, 1 - core), (mine_ref, core)):
            pick = lanes(2 * j + side, head)
            o_ref[at, :] = dot(a_ref[:, pick], b_ref[:, pick], 0, 0).astype(BF)


def pair_sums(me, a, b, head):
    tok, width = a.shape
    step = min(4 * head, width)
    spec = pl.BlockSpec((tok, step), lambda i, m: (0, i))
    out = pl.BlockSpec((step // 2, head), lambda i, m: (i, 0))
    shape = jax.ShapeDtypeStruct((width // 2, head), BF)
    return pl.pallas_call(
        functools.partial(pair_sums_kernel, head),
        grid_spec=pltpu.PrefetchScalarGridSpec(
            num_scalar_prefetch=1,
            grid=(width // step,),
            in_specs=[spec] * 2,
            out_specs=[out] * 2,
        ),
        out_shape=[shape] * 2,
        compiler_params=params(),
        cost_estimate=cost(2 * tok * width * head, 4 * tok * width),
        name="pair_sums",
    )(me, a, b)


def pair_intra_kernel(head, waits, me_ref, *refs):
    q_ref, k_ref, v_ref, mine_ref, send_ref = refs[waits:]
    core = me_ref[0] % 2
    half = q_ref.shape[0] // 2
    for j in range(q_ref.shape[1] // (2 * head)):
        for o_ref, side, base in ((send_ref, 1 - core, (2 * j + 1) * head), (mine_ref, core, j * head)):
            pick = lanes(2 * j + side, head)
            first, second = causal_apply(q_ref[:, pick], k_ref[:, pick], v_ref[:, pick], False)
            o_ref[base : base + head, :half] = first.astype(BF).T
            o_ref[base : base + head, half:] = second.astype(BF).T
        send_ref[2 * j * head : (2 * j + 1) * head, :] = q_ref[:, lanes(2 * j + 1 - core, head)].T


def pair_intra(me, after, q, k, v, head):
    tok, width = q.shape
    step = min(4 * head, width)
    spec = pl.BlockSpec((tok, step), lambda i, m: (0, i))
    return pl.pallas_call(
        functools.partial(pair_intra_kernel, head, len(after)),
        grid_spec=pltpu.PrefetchScalarGridSpec(
            num_scalar_prefetch=1,
            grid=(width // step,),
            in_specs=[ANY] * len(after) + [spec] * 3,
            out_specs=[
                pl.BlockSpec((step // 2, tok), lambda i, m: (i, 0)),
                pl.BlockSpec((step, tok), lambda i, m: (i, 0)),
            ],
        ),
        out_shape=[
            jax.ShapeDtypeStruct((width // 2, tok), BF),
            jax.ShapeDtypeStruct((width, tok), BF),
        ],
        compiler_params=params(),
        cost_estimate=cost(4 * tok * tok * width, 9 * tok * width),
        name="pair_intra",
    )(me, *after, q, k, v)


def pair_attended_kernel(head, me_ref, after_ref, q0_ref, q1_ref, i_ref, far_ref, s_ref, own_ref, oth_ref,
                         mine_ref, cross_ref, near_ref, away_ref):
    core = (me_ref[0] % 2).astype(F32)
    south = (me_ref[0] // 2) % 2

    def fill(q_ref, side, o_ref):
        rows = lanes(side, head)
        state = s_ref[rows, :].astype(F32)
        near = (state + core * oth_ref[rows, :].astype(F32)).astype(BF)
        away = (state + (1.0 - core) * own_ref[rows, :].astype(F32)).astype(BF)
        away_ref[rows, :] = away
        here = dot(near, q_ref[...], 0, 1) + i_ref[rows, :].astype(F32)
        there = dot(away, far_ref[lanes(2 * side, head), :], 0, 0)
        there = there + far_ref[lanes(2 * side + 1, head), :].astype(F32)
        o_ref[0, 0] = here.astype(BF)
        o_ref[0, 1] = there.astype(BF)

    fill(q0_ref, south, mine_ref)
    crossing = pl.program_id(0) < pl.num_programs(0) // 2
    pl.when(crossing)(lambda: fill(q1_ref, 1 - south, cross_ref))
    pl.when(jnp.logical_not(crossing))(lambda: fill(q1_ref, 1 - south, near_ref))


def pair_attended(me, after, q, inner, far, state, own, oth, head):
    tok, width = q.shape
    places = width // (4 * head)
    half = places // 2

    def place(i, m):
        return (m[0] // 4) ^ i ^ half

    rows = pl.BlockSpec((2 * head, head), lambda i, m: (place(i, m), 0))

    def out(index):
        return pl.BlockSpec((1, 2, head, tok), lambda i, m: (index(i), 0, 0, 0))

    def shape(count):
        return jax.ShapeDtypeStruct((count, 2, head, tok), BF)

    return pl.pallas_call(
        functools.partial(pair_attended_kernel, head),
        grid_spec=pltpu.PrefetchScalarGridSpec(
            num_scalar_prefetch=1,
            grid=(places,),
            in_specs=[
                ANY,
                pl.BlockSpec((tok, head), lambda i, m: (0, 4 * place(i, m) + m[0] % 4)),
                pl.BlockSpec((tok, head), lambda i, m: (0, 4 * place(i, m) + (m[0] % 4 ^ 2))),
                pl.BlockSpec((2 * head, tok), lambda i, m: (place(i, m), 0)),
                pl.BlockSpec((4 * head, tok), lambda i, m: (place(i, m), 0)),
            ]
            + [rows] * 3,
            out_specs=[
                out(lambda i: i ^ half),
                out(lambda i: jnp.minimum(i, half - 1)),
                out(lambda i: jnp.maximum(i - half, 0)),
                rows,
            ],
        ),
        out_shape=[
            shape(places),
            shape(half),
            shape(half),
            jax.ShapeDtypeStruct((width // 2, head), BF),
        ],
        compiler_params=params(),
        cost_estimate=cost(2 * tok * head * width, 10 * tok * width),
        name="pair_attended",
    )(me, after, q, q, inner, far, state, own, oth)


def quad_weight_kernel(waits, tp_ref, a_ref, b_ref, *refs):
    half, _, head, tok = a_ref.shape
    ins, outs, a_all, c_all = refs[:8], refs[8 + waits : -2], refs[-2], refs[-1]

    @pl.when(pl.program_id(0) == 0)
    def _():
        for k in range(4):
            block = (a_ref if k < 2 else b_ref)[:, k % 2]
            a_all[:, k * tok : (k + 1) * tok] = block.reshape(half * head, tok)

    def product(part):
        for k in range(4):
            c_all[k * tok : (k + 1) * tok, :] = ins[2 * k + part][...]
        total = dot(a_all[...], c_all[...], 1, 0)
        for i, o_ref in enumerate(outs):
            o_ref[...] = total[i * head : (i + 1) * head].astype(BF)

    steps = pl.num_programs(0) // 2
    pl.when(pl.program_id(0) < steps)(lambda: product(0))
    pl.when(pl.program_id(0) >= steps)(lambda: product(1))


def quad_weight(tp, after, a, b, cots, far_side):
    places, _, head, tok = a.shape
    half = places // 2
    feat = cots[0].shape[1]
    step = min(512, feat)
    steps = feat // step
    whole = pl.BlockSpec((half,) + a.shape[1:], lambda i, t: (far_side, 0, 0, 0))
    own = pl.BlockSpec((tok, step), lambda i, t: (0, jnp.minimum(i, steps - 1)))
    other = pl.BlockSpec((tok, step), lambda i, t: (0, jnp.maximum(i - steps, 0)))
    return pl.pallas_call(
        functools.partial(quad_weight_kernel, len(after)),
        grid_spec=pltpu.PrefetchScalarGridSpec(
            num_scalar_prefetch=1,
            grid=(2 * steps,),
            in_specs=[whole, pl.BlockSpec(b.shape, lambda i, t: (0, 0, 0, 0))] + [own, other] * 4 + [ANY] * len(after),
            out_specs=[
                pl.BlockSpec((head, step), lambda i, t: (0, (i + t[0] * steps) % (2 * steps)))
            ]
            * half,
            scratch_shapes=[
                pltpu.VMEM((half * head, 4 * tok), BF),
                pltpu.VMEM((4 * tok, step), BF),
            ],
        ),
        out_shape=[jax.ShapeDtypeStruct((head, 2 * feat), BF)] * half,
        compiler_params=params(),
        cost_estimate=cost(2e10 if far_side else NEAR, 0),
        name="quad_weight",
    )(tp, a, b, *cots, *after)


def pair_query_kernel(head, me_ref, after_ref, so_far_ref, g_ref, v_ref, k_ref, s_ref, kv_ref, t_ref, o_ref):
    core = me_ref[0] % 2
    half = g_ref.shape[0] // 2
    for j in range(g_ref.shape[1] // head):
        at, row = slice(j * head, (j + 1) * head), slice(j // 2 * head, (j // 2 + 1) * head)
        g = g_ref[:, at]
        near = s_ref[row, :].astype(F32) + core.astype(F32) * kv_ref[row, :].astype(F32)
        state = jnp.where(core == j % 2, near.astype(BF), t_ref[row, :])
        first_half, second_half = causal_apply(g, v_ref[:, at], k_ref[:, at], False)
        over = dot(g, state, 1, 1)
        o_ref[:half, at] = (first_half + over[:half]).astype(BF)
        o_ref[half:, at] = (second_half + over[half:]).astype(BF)


def pair_query_grad(me, part, after, so_far, g, v, k, state, kv, other, head):
    tok, width = g.shape
    step = min(4 * head, width // 2)
    steps = width // 2 // step
    spec = pl.BlockSpec((tok, step), lambda i, m: (0, i + part * steps))
    rows = pl.BlockSpec((step // 2, head), lambda i, m: (i + part * steps, 0))
    return pl.pallas_call(
        functools.partial(pair_query_kernel, head),
        grid_spec=pltpu.PrefetchScalarGridSpec(
            num_scalar_prefetch=1,
            grid=(steps,),
            in_specs=[ANY, ANY, spec, spec, spec, rows, rows, rows],
            out_specs=spec,
        ),
        out_shape=jax.ShapeDtypeStruct((tok, width), BF),
        input_output_aliases={2: 0} if part else {},
        compiler_params=params(),
        cost_estimate=cost(0, 0),
        name="query_grad",
    )(me, after, so_far, g, v, k, state, kv, other)


def pair_grad_kernel(head, waits, me_ref, tp_ref, own_ref, far_ref, w_ref, q_ref, *refs):
    g_ref, mine_ref, send_ref = refs[waits : waits + 3]
    cot_ref = refs[-1]
    feat = own_ref.shape[1]

    @pl.when(pl.program_id(0) == 0)
    def _():
        cot_ref[:, lanes(tp_ref[0], feat)] = own_ref[...]
        cot_ref[:, lanes(1 - tp_ref[0], feat)] = far_ref[...]

    core = me_ref[0] % 2
    g_ref[...] = dot(cot_ref[...], w_ref[...], 1, 1).astype(BF)
    for j in range(g_ref.shape[1] // (2 * head)):
        at = slice(j * head, (j + 1) * head)
        for o_ref, side in ((send_ref, 1 - core), (mine_ref, core)):
            pick = lanes(2 * j + side, head)
            o_ref[at, :] = dot(q_ref[:, pick], g_ref[:, pick], 0, 0).astype(BF)


def pair_grad(me, tp, after, own, far, w, q, head):
    tok, feat = own.shape
    width = q.shape[1]
    step = min(4 * head, width)
    whole = pl.BlockSpec((tok, feat), lambda i, m, t: (0, 0))
    rows = pl.BlockSpec((step // 2, head), lambda i, m, t: (i, 0))
    cols = pl.BlockSpec((tok, step), lambda i, m, t: (0, i))
    sums = jax.ShapeDtypeStruct((width // 2, head), BF)
    return pl.pallas_call(
        functools.partial(pair_grad_kernel, head, len(after)),
        grid_spec=pltpu.PrefetchScalarGridSpec(
            num_scalar_prefetch=2,
            grid=(width // step,),
            in_specs=[
                whole,
                whole,
                pl.BlockSpec((step, 2 * feat), lambda i, m, t: (i, 0)),
                cols,
            ]
            + [ANY] * len(after),
            out_specs=[cols, rows, rows],
            scratch_shapes=[pltpu.VMEM((tok, 2 * feat), BF)],
        ),
        out_shape=[jax.ShapeDtypeStruct((tok, width), BF), sums, sums],
        compiler_params=params(),
        cost_estimate=cost(4 * tok * feat * width, 4 * feat * width + 4 * tok * width),
        name="out_grad",
    )(me, tp, own, far, w, q, *after)


def pass_kernel(*refs):
    pass


def passed_after(x, after, flops):
    return pl.pallas_call(
        pass_kernel,
        in_specs=[ANY] * (1 + len(after)),
        out_specs=ANY,
        out_shape=jax.ShapeDtypeStruct(x.shape, x.dtype),
        input_output_aliases={0: 0},
        compiler_params=params(),
        cost_estimate=cost(flops, 0),
        name="passed_after",
    )(x, *after)


def add_kernel(after_ref, a_ref, b_ref, o_ref):
    o_ref[...] = (a_ref[...].astype(F32) + b_ref[...].astype(F32)).astype(BF)


def add_after(after, a, b):
    spec = pl.BlockSpec(a.shape, lambda: (0, 0))
    return pl.pallas_call(
        add_kernel,
        in_specs=[ANY, spec, spec],
        out_specs=spec,
        out_shape=jax.ShapeDtypeStruct(a.shape, BF),
        compiler_params=params(),
        cost_estimate=cost(0, 0),
        name="add_after",
    )(after, a, b)


def pair_key_value_kernel(head, me_ref, after_ref, q_ref, k_ref, v_ref, g_ref, s_ref, qd_ref, t_ref, ko_ref, vo_ref):
    core = me_ref[0] % 2
    half = g_ref.shape[0] // 2
    for j in range(g_ref.shape[1] // head):
        at, row = slice(j * head, (j + 1) * head), slice(j // 2 * head, (j // 2 + 1) * head)
        near = s_ref[row, :].astype(F32) + (1 - core).astype(F32) * qd_ref[row, :].astype(F32)
        q, k, v, g = q_ref[:, at], k_ref[:, at], v_ref[:, at], g_ref[:, at]
        adj = jnp.where(core == j % 2, near.astype(BF), t_ref[row, :])
        first, second = causal_apply(v, g, q, True)
        over = dot(v, adj, 1, 1)
        ko_ref[:half, at] = (first + over[:half]).astype(BF)
        ko_ref[half:, at] = (second + over[half:]).astype(BF)
        first, second = causal_apply(k, q, g, True)
        over = dot(k, adj, 1, 0)
        vo_ref[:half, at] = (first + over[:half]).astype(BF)
        vo_ref[half:, at] = (second + over[half:]).astype(BF)


def pair_key_value_grad(me, after, q, k, v, g, adjoint, qd, other, head):
    tok, width = g.shape
    step = min(4 * head, width)
    spec = pl.BlockSpec((tok, step), lambda i, m: (0, i))
    rows = pl.BlockSpec((step // 2, head), lambda i, m: (i, 0))
    shape = jax.ShapeDtypeStruct((tok, width), BF)
    return pl.pallas_call(
        functools.partial(pair_key_value_kernel, head),
        grid_spec=pltpu.PrefetchScalarGridSpec(
            num_scalar_prefetch=1,
            grid=(width // step,),
            in_specs=[ANY, spec, spec, spec, spec, rows, rows, rows],
            out_specs=[spec, spec],
        ),
        out_shape=[shape, shape],
        compiler_params=params(),
        cost_estimate=cost(0, 0),
        name="key_value_grad",
    )(me, after, q, k, v, g, adjoint, qd, other)


def local_paired(queries, keys, values, cotangent, out_weight, memory):
    head = memory.shape[2]
    n = lax.axis_size("ctx")
    me, tp = lax.axis_index("ctx"), lax.axis_index("tp")
    who, which = me.reshape(1), tp.reshape(1)
    core = (me % 2).astype(F32)
    groups = [[c for c in range(n) if c % 2 == side] for side in range(2)]

    def swap(x, bit):
        return lax.ppermute(x, "ctx", [(c, c ^ bit) for c in range(n)])

    def swap_tp(x):
        return lax.ppermute(x, "tp", [(0, 1), (1, 0)])

    def across(x):
        return lax.all_to_all(x, "ctx", 0, 0, axis_index_groups=groups, tiled=True)

    def added(x, factor, y):
        return (x.astype(F32) + factor * y.astype(F32)).astype(BF)

    kv_mine, kv_send = pair_sums(who, keys, values, head)
    kv_other = swap(kv_send, 1)
    far = swap_tp(cotangent)
    south = swap(cotangent, 2)
    chip = added(kv_mine, 1.0, kv_other)
    inner, sent = pair_intra(who, (chip,), queries, keys, values, head)
    start = lax.dynamic_index_in_dim(memory, me, 0, False)
    scanned, sent = scan_blocks(across(chip), start, n // 2, False, (inner, far, south), sent)
    state = across(scanned)

    far_south = swap_tp(south)
    grad, qd_mine, qd_send = pair_grad(
        who, which, (scanned, south), cotangent, far, out_weight, queries, head
    )
    mine, send, send_near, away = pair_attended(
        who, grad, queries, inner, swap(sent, 1), state, kv_mine, kv_other, head
    )
    received, received_near = swap(send, 2), swap(send_near, 2)
    state_other = swap(away, 1)

    qd_other = swap(qd_send, 1)
    chip = add_after(send, qd_mine, qd_other)
    cots = [cotangent, far, swap(cotangent, 1), swap(far, 1)]
    cots += [south, far_south, swap(south, 1), swap(far_south, 1)]

    query_args = (grad, values, keys, state, kv_other, state_other, head)
    query_g = pair_query_grad(who, 0, chip, grad, *query_args)
    received = passed_after(received, (query_g,), 2e10)
    crossing = quad_weight(which, (), mine, received, cots, 1)
    summed = added(crossing[0], 1.0, swap(crossing[1], 4))
    crossed = swap(summed, 8)
    scanned = scan_blocks(across(chip), None, n // 2, True, (crossing[0],))
    after_chip = across(scanned)
    same = quad_weight(which, (scanned,), mine, received_near, cots, 0)
    neighbour = swap(same[1], 4)
    query_g = pair_query_grad(who, 1, summed, query_g, *query_args)
    after_chip = passed_after(after_chip, (query_g,), 0)
    adjoint_other = swap(added(after_chip, core, qd_mine), 1)
    key_g, value_g = pair_key_value_grad(
        who, query_g, queries, keys, values, grad, after_chip, qd_other, adjoint_other, head
    )
    total = same[0].astype(F32) + neighbour.astype(F32) + crossed.astype(F32)
    return query_g, key_g, value_g, total


def local_any(queries, keys, values, cotangent, out_weight, memory):
    head = memory.shape[2]
    width = queries.shape[1]
    feat = cotangent.shape[1]
    n = lax.axis_size("ctx")
    rows = width // n
    me, tp = lax.axis_index("ctx"), lax.axis_index("tp")

    far = lax.ppermute(cotangent, "tp", [(0, 1), (1, 0)])
    kv = block_sums(keys, values, head)
    start = lax.dynamic_slice_in_dim(memory.reshape(width, head), me * rows, rows, 0)
    state = carried(kv, start, "ctx", False)
    inner = intra(queries, keys, values, head)
    grad, qd = out_grad_and_sums(tp.reshape(1), cotangent, far, out_weight, queries, head)
    adjoint = carried(qd, None, "ctx", True)
    attended = attended_of(queries, state, inner, head)
    term = weight_term(attended, cotangent, far)
    total = lax.psum_scatter(term, "ctx", scatter_dimension=0, tiled=True)
    query_g = query_grad_of(grad, values, keys, state, head)
    key_g, value_g = key_value_grad_of(queries, keys, values, grad, adjoint, head)
    total = total.astype(F32)
    total = jnp.where(tp == 0, total, jnp.concatenate([total[:, feat:], total[:, :feat]], 1))
    return query_g, key_g, value_g, total


def local(*args):
    heads = args[5].shape[0]
    n = lax.axis_size("ctx")
    if n == heads == 16 and lax.axis_size("tp") == 2:
        return local_paired(*args)
    return local_any(*args)


def solution(mesh):
    in_specs = (
        P("ctx", "tp"),
        P("ctx", "tp"),
        P("ctx", "tp"),
        P("ctx", "tp"),
        P("tp", None),
        P("tp", None, None),
    )
    out_specs = (P("ctx", "tp"), P("ctx", "tp"), P("ctx", "tp"), P(("tp", "ctx"), None))
    return jax.shard_map(local, mesh=mesh, in_specs=in_specs, out_specs=out_specs, check_vma=False)
```

```python
import functools

import jax
import jax.numpy as jnp
from jax import lax
from jax.experimental import pallas as pl
from jax.experimental.pallas import tpu as pltpu
from jax.sharding import PartitionSpec as P

BF = jnp.bfloat16
F32 = jnp.float32
NEAR = 0
SCAN = 2e10
VMEM_LIMIT = 56 * 1024 * 1024


def dot(a, b, ca, cb):
    return lax.dot_general(a, b, (((ca,), (cb,)), ((), ())), preferred_element_type=F32)


def lanes(index, head):
    return pl.ds(pl.multiple_of(index * head, head), head)


def params():
    return pltpu.CompilerParams(vmem_limit_bytes=VMEM_LIMIT)


def cost(flops, nbytes):
    return pl.CostEstimate(flops=int(flops), bytes_accessed=int(nbytes), transcendentals=0)


def kv_kernel(head, a_ref, b_ref, o_ref):
    for j in range(a_ref.shape[1] // head):
        at = slice(j * head, (j + 1) * head)
        o_ref[at, :] = dot(a_ref[:, at], b_ref[:, at], 0, 0).astype(o_ref.dtype)


def block_sums(a, b, head):
    tok, width = a.shape
    step = 2 * head
    return pl.pallas_call(
        functools.partial(kv_kernel, head),
        grid=(width // step,),
        in_specs=[pl.BlockSpec((tok, step), lambda i: (0, i))] * 2,
        out_specs=pl.BlockSpec((step, head), lambda i: (i, 0)),
        out_shape=jax.ShapeDtypeStruct((width, head), BF),
        compiler_params=params(),
        cost_estimate=cost(2 * tok * width * head, 4 * tok * width),
        name="block_sums",
    )(a, b)


def masked(tok, upper):
    row = lax.broadcasted_iota(jnp.int32, (tok, tok), 0)
    col = lax.broadcasted_iota(jnp.int32, (tok, tok), 1)
    return row <= col if upper else row >= col


def causal_apply(a, b, c, upper):
    tok = a.shape[0]
    half = tok // 2
    keep = masked(half, upper)

    def tile(x, y, diagonal):
        s = dot(x, y, 1, 1)
        if diagonal:
            s = jnp.where(keep, s, 0.0)
        return s.astype(BF)

    a0, a1, b0, b1, c0, c1 = a[:half], a[half:], b[:half], b[half:], c[:half], c[half:]
    first = dot(tile(a0, b0, True), c0, 1, 0)
    second = dot(tile(a1, b1, True), c1, 1, 0)
    if upper:
        first = first + dot(tile(a0, b1, False), c1, 1, 0)
    else:
        second = second + dot(tile(a1, b0, False), c0, 1, 0)
    return first, second


def intra_kernel(head, q_ref, k_ref, v_ref, o_ref):
    half = q_ref.shape[0] // 2
    for j in range(q_ref.shape[1] // head):
        at = slice(j * head, (j + 1) * head)
        first, second = causal_apply(q_ref[:, at], k_ref[:, at], v_ref[:, at], False)
        o_ref[:half, at] = first
        o_ref[half:, at] = second


def intra(q, k, v, head):
    tok, width = q.shape
    step = 2 * head
    spec = pl.BlockSpec((tok, step), lambda i: (0, i))
    return pl.pallas_call(
        functools.partial(intra_kernel, head),
        grid=(width // step,),
        in_specs=[spec] * 3,
        out_specs=spec,
        out_shape=jax.ShapeDtypeStruct((tok, width), F32),
        compiler_params=params(),
        cost_estimate=cost(4 * tok * tok * width, 10 * tok * width),
        name="intra",
    )(q, k, v)


def grad_kernel(head, tp_ref, own_ref, far_ref, wo_ref, wf_ref, q_ref, g_ref, s_ref):
    g = dot(own_ref[...], wo_ref[...], 1, 1) + dot(far_ref[...], wf_ref[...], 1, 1)
    g = g.astype(BF)
    g_ref[...] = g
    for j in range(g.shape[1] // head):
        at = slice(j * head, (j + 1) * head)
        s_ref[at, :] = dot(q_ref[:, at], g[:, at], 0, 0).astype(s_ref.dtype)


def out_grad_and_sums(tp, own, far, w, q, head):
    tok, feat = own.shape
    width = q.shape[1]
    step = 2 * head
    whole = pl.BlockSpec((tok, feat), lambda i, t: (0, 0))
    return pl.pallas_call(
        functools.partial(grad_kernel, head),
        grid_spec=pltpu.PrefetchScalarGridSpec(
            num_scalar_prefetch=1,
            grid=(width // step,),
            in_specs=[
                whole,
                whole,
                pl.BlockSpec((step, feat), lambda i, t: (i, t[0])),
                pl.BlockSpec((step, feat), lambda i, t: (i, 1 - t[0])),
                pl.BlockSpec((tok, step), lambda i, t: (0, i)),
            ],
            out_specs=[
                pl.BlockSpec((tok, step), lambda i, t: (0, i)),
                pl.BlockSpec((step, head), lambda i, t: (i, 0)),
            ],
        ),
        out_shape=[
            jax.ShapeDtypeStruct((tok, width), BF),
            jax.ShapeDtypeStruct((width, head), BF),
        ],
        compiler_params=params(),
        cost_estimate=cost(4 * tok * feat * width, 4 * feat * width + 4 * tok * width),
        name="out_grad",
    )(tp, own, far, w, w, q)


def attended_kernel(head, q_ref, s_ref, i_ref, o_ref):
    for j in range(q_ref.shape[1] // head):
        at = slice(j * head, (j + 1) * head)
        o_ref[:, at] = (dot(q_ref[:, at], s_ref[at, :], 1, 0) + i_ref[:, at]).astype(BF)


def attended_of(q, state, inner, head):
    tok, width = q.shape
    step = 2 * head
    spec = pl.BlockSpec((tok, step), lambda i: (0, i))
    return pl.pallas_call(
        functools.partial(attended_kernel, head),
        grid=(width // step,),
        in_specs=[spec, pl.BlockSpec((step, head), lambda i: (i, 0)), spec],
        out_specs=spec,
        out_shape=jax.ShapeDtypeStruct((tok, width), BF),
        compiler_params=params(),
        cost_estimate=cost(2 * tok * head * width, 8 * tok * width),
        name="attended",
    )(q, state, inner)


def weight_kernel(a_ref, own_ref, far_ref, o_ref):
    feat = own_ref.shape[1]
    a = a_ref[...]
    o_ref[:, :feat] = dot(a, own_ref[...], 0, 0).astype(o_ref.dtype)
    o_ref[:, feat:] = dot(a, far_ref[...], 0, 0).astype(o_ref.dtype)


def weight_term(a, own, far):
    tok, width = a.shape
    feat = own.shape[1]
    step = 256
    whole = pl.BlockSpec((tok, feat), lambda i: (0, 0))
    return pl.pallas_call(
        weight_kernel,
        grid=(width // step,),
        in_specs=[pl.BlockSpec((tok, step), lambda i: (0, i)), whole, whole],
        out_specs=pl.BlockSpec((step, 2 * feat), lambda i: (i, 0)),
        out_shape=jax.ShapeDtypeStruct((width, 2 * feat), BF),
        compiler_params=params(),
        cost_estimate=cost(4 * tok * feat * width, 4 * feat * width + 2 * tok * width),
        name="weight_term",
    )(a, own, far)


def query_kernel(head, g_ref, v_ref, k_ref, s_ref, o_ref):
    half = g_ref.shape[0] // 2
    for j in range(g_ref.shape[1] // head):
        at = slice(j * head, (j + 1) * head)
        g = g_ref[:, at]
        first, second = causal_apply(g, v_ref[:, at], k_ref[:, at], False)
        carried = dot(g, s_ref[at, :], 1, 1)
        o_ref[:half, at] = (first + carried[:half]).astype(BF)
        o_ref[half:, at] = (second + carried[half:]).astype(BF)


def query_grad_of(g, v, k, state, head):
    tok, width = g.shape
    step = 2 * head
    spec = pl.BlockSpec((tok, step), lambda i: (0, i))
    return pl.pallas_call(
        functools.partial(query_kernel, head),
        grid=(width // step,),
        in_specs=[spec, spec, spec, pl.BlockSpec((step, head), lambda i: (i, 0))],
        out_specs=spec,
        out_shape=jax.ShapeDtypeStruct((tok, width), BF),
        compiler_params=params(),
        cost_estimate=cost(4 * tok * tok * width, 8 * tok * width),
        name="query_grad",
    )(g, v, k, state)


def key_value_kernel(head, q_ref, k_ref, v_ref, g_ref, a_ref, ko_ref, vo_ref):
    half = g_ref.shape[0] // 2
    for j in range(g_ref.shape[1] // head):
        at = slice(j * head, (j + 1) * head)
        q, k, v, g, adj = q_ref[:, at], k_ref[:, at], v_ref[:, at], g_ref[:, at], a_ref[at, :]
        first, second = causal_apply(v, g, q, True)
        carried = dot(v, adj, 1, 1)
        ko_ref[:half, at] = (first + carried[:half]).astype(BF)
        ko_ref[half:, at] = (second + carried[half:]).astype(BF)
        first, second = causal_apply(k, q, g, True)
        carried = dot(k, adj, 1, 0)
        vo_ref[:half, at] = (first + carried[:half]).astype(BF)
        vo_ref[half:, at] = (second + carried[half:]).astype(BF)


def key_value_grad_of(q, k, v, g, adjoint, head):
    tok, width = g.shape
    step = 2 * head
    spec = pl.BlockSpec((tok, step), lambda i: (0, i))
    shape = jax.ShapeDtypeStruct((tok, width), BF)
    return pl.pallas_call(
        functools.partial(key_value_kernel, head),
        grid=(width // step,),
        in_specs=[spec, spec, spec, spec, pl.BlockSpec((step, head), lambda i: (i, 0))],
        out_specs=[spec, spec],
        out_shape=[shape, shape],
        compiler_params=params(),
        cost_estimate=cost(8 * tok * tok * width, 12 * tok * width),
        name="key_value_grad",
    )(q, k, v, g, adjoint)


ANY = pl.BlockSpec(memory_space=pl.ANY)


def scan_kernel(n, reverse, waits, x_ref, *refs):
    o_ref = refs[waits]
    rows = x_ref.shape[0] // n
    total = jnp.zeros((rows, x_ref.shape[1]), F32) if reverse else refs[0][...]
    for i in range(n):
        c = n - 1 - i if reverse else i
        at = slice(c * rows, (c + 1) * rows)
        o_ref[at, :] = total.astype(BF)
        total = total + x_ref[at, :].astype(F32)


def scan_blocks(x, start, n, reverse, after=(), passed=None):
    more = () if passed is None else (passed,)
    first = () if reverse else (start,)
    out = pl.pallas_call(
        functools.partial(scan_kernel, n, reverse, len(first) + len(after) + len(more)),
        in_specs=[pl.BlockSpec(y.shape, lambda: (0, 0)) for y in (x, *first)]
        + [ANY] * (len(after) + len(more)),
        out_specs=[pl.BlockSpec(x.shape, lambda: (0, 0))] + [ANY] * len(more),
        out_shape=[jax.ShapeDtypeStruct(x.shape, BF)]
        + [jax.ShapeDtypeStruct(p.shape, p.dtype) for p in more],
        input_output_aliases={1 + len(first) + len(after): 1} if more else {},
        compiler_params=params(),
        cost_estimate=cost(SCAN, 0),
        name="scan_blocks",
    )(x, *first, *after, *more)
    return out if more else out[0]


def carried(x, start, axis, reverse):
    n = lax.axis_size(axis)
    mine = lax.all_to_all(x, axis, 0, 0, tiled=True)
    return lax.all_to_all(scan_blocks(mine, start, n, reverse), axis, 0, 0, tiled=True)


def pair_sums_kernel(head, me_ref, a_ref, b_ref, mine_ref, send_ref):
    core = me_ref[0] % 2
    for j in range(a_ref.shape[1] // (2 * head)):
        at = slice(j * head, (j + 1) * head)
        for o_ref, side in ((send_ref, 1 - core), (mine_ref, core)):
            pick = lanes(2 * j + side, head)
            o_ref[at, :] = dot(a_ref[:, pick], b_ref[:, pick], 0, 0).astype(BF)


def pair_sums(me, a, b, head):
    tok, width = a.shape
    step = min(4 * head, width)
    spec = pl.BlockSpec((tok, step), lambda i, m: (0, i))
    out = pl.BlockSpec((step // 2, head), lambda i, m: (i, 0))
    shape = jax.ShapeDtypeStruct((width // 2, head), BF)
    return pl.pallas_call(
        functools.partial(pair_sums_kernel, head),
        grid_spec=pltpu.PrefetchScalarGridSpec(
            num_scalar_prefetch=1,
            grid=(width // step,),
            in_specs=[spec] * 2,
            out_specs=[out] * 2,
        ),
        out_shape=[shape] * 2,
        compiler_params=params(),
        cost_estimate=cost(2 * tok * width * head, 4 * tok * width),
        name="pair_sums",
    )(me, a, b)


def pair_intra_kernel(head, waits, me_ref, *refs):
    q_ref, k_ref, v_ref, mine_ref, send_ref = refs[waits:]
    core = me_ref[0] % 2
    half = q_ref.shape[0] // 2
    for j in range(q_ref.shape[1] // (2 * head)):
        for o_ref, side, base in ((send_ref, 1 - core, (2 * j + 1) * head), (mine_ref, core, j * head)):
            pick = lanes(2 * j + side, head)
            first, second = causal_apply(q_ref[:, pick], k_ref[:, pick], v_ref[:, pick], False)
            o_ref[base : base + head, :half] = first.astype(BF).T
            o_ref[base : base + head, half:] = second.astype(BF).T
        send_ref[2 * j * head : (2 * j + 1) * head, :] = q_ref[:, lanes(2 * j + 1 - core, head)].T


def pair_intra(me, after, q, k, v, head):
    tok, width = q.shape
    step = min(4 * head, width)
    spec = pl.BlockSpec((tok, step), lambda i, m: (0, i))
    return pl.pallas_call(
        functools.partial(pair_intra_kernel, head, len(after)),
        grid_spec=pltpu.PrefetchScalarGridSpec(
            num_scalar_prefetch=1,
            grid=(width // step,),
            in_specs=[ANY] * len(after) + [spec] * 3,
            out_specs=[
                pl.BlockSpec((step // 2, tok), lambda i, m: (i, 0)),
                pl.BlockSpec((step, tok), lambda i, m: (i, 0)),
            ],
        ),
        out_shape=[
            jax.ShapeDtypeStruct((width // 2, tok), BF),
            jax.ShapeDtypeStruct((width, tok), BF),
        ],
        compiler_params=params(),
        cost_estimate=cost(4 * tok * tok * width, 9 * tok * width),
        name="pair_intra",
    )(me, *after, q, k, v)


def pair_attended_kernel(head, me_ref, after_ref, q0_ref, q1_ref, i_ref, far_ref, s_ref, own_ref, oth_ref,
                         mine_ref, cross_ref, near_ref, away_ref):
    core = (me_ref[0] % 2).astype(F32)
    south = (me_ref[0] // 2) % 2

    def fill(q_ref, side, o_ref):
        rows = lanes(side, head)
        state = s_ref[rows, :].astype(F32)
        near = (state + core * oth_ref[rows, :].astype(F32)).astype(BF)
        away = (state + (1.0 - core) * own_ref[rows, :].astype(F32)).astype(BF)
        away_ref[rows, :] = away
        here = dot(near, q_ref[...], 0, 1) + i_ref[rows, :].astype(F32)
        there = dot(away, far_ref[lanes(2 * side, head), :], 0, 0)
        there = there + far_ref[lanes(2 * side + 1, head), :].astype(F32)
        o_ref[0, 0] = here.astype(BF)
        o_ref[0, 1] = there.astype(BF)

    fill(q0_ref, south, mine_ref)
    crossing = pl.program_id(0) < pl.num_programs(0) // 2
    pl.when(crossing)(lambda: fill(q1_ref, 1 - south, cross_ref))
    pl.when(jnp.logical_not(crossing))(lambda: fill(q1_ref, 1 - south, near_ref))


def pair_attended(me, after, q, inner, far, state, own, oth, head):
    tok, width = q.shape
    places = width // (4 * head)
    half = places // 2

    def place(i, m):
        return (m[0] // 4) ^ i ^ half

    rows = pl.BlockSpec((2 * head, head), lambda i, m: (place(i, m), 0))

    def out(index):
        return pl.BlockSpec((1, 2, head, tok), lambda i, m: (index(i), 0, 0, 0))

    def shape(count):
        return jax.ShapeDtypeStruct((count, 2, head, tok), BF)

    return pl.pallas_call(
        functools.partial(pair_attended_kernel, head),
        grid_spec=pltpu.PrefetchScalarGridSpec(
            num_scalar_prefetch=1,
            grid=(places,),
            in_specs=[
                ANY,
                pl.BlockSpec((tok, head), lambda i, m: (0, 4 * place(i, m) + m[0] % 4)),
                pl.BlockSpec((tok, head), lambda i, m: (0, 4 * place(i, m) + (m[0] % 4 ^ 2))),
                pl.BlockSpec((2 * head, tok), lambda i, m: (place(i, m), 0)),
                pl.BlockSpec((4 * head, tok), lambda i, m: (place(i, m), 0)),
            ]
            + [rows] * 3,
            out_specs=[
                out(lambda i: i ^ half),
                out(lambda i: jnp.minimum(i, half - 1)),
                out(lambda i: jnp.maximum(i - half, 0)),
                rows,
            ],
        ),
        out_shape=[
            shape(places),
            shape(half),
            shape(half),
            jax.ShapeDtypeStruct((width // 2, head), BF),
        ],
        compiler_params=params(),
        cost_estimate=cost(2 * tok * head * width, 10 * tok * width),
        name="pair_attended",
    )(me, after, q, q, inner, far, state, own, oth)


def quad_weight_kernel(waits, tp_ref, a_ref, b_ref, *refs):
    half, _, head, tok = a_ref.shape
    ins, outs, a_all, c_all = refs[:8], refs[8 + waits : -2], refs[-2], refs[-1]

    @pl.when(pl.program_id(0) == 0)
    def _():
        for k in range(4):
            block = (a_ref if k < 2 else b_ref)[:, k % 2]
            a_all[:, k * tok : (k + 1) * tok] = block.reshape(half * head, tok)

    def product(part):
        for k in range(4):
            c_all[k * tok : (k + 1) * tok, :] = ins[2 * k + part][...]
        total = dot(a_all[...], c_all[...], 1, 0)
        for i, o_ref in enumerate(outs):
            o_ref[...] = total[i * head : (i + 1) * head].astype(BF)

    steps = pl.num_programs(0) // 2
    pl.when(pl.program_id(0) < steps)(lambda: product(0))
    pl.when(pl.program_id(0) >= steps)(lambda: product(1))


def quad_weight(tp, after, a, b, cots, far_side):
    places, _, head, tok = a.shape
    half = places // 2
    feat = cots[0].shape[1]
    step = min(512, feat)
    steps = feat // step
    whole = pl.BlockSpec((half,) + a.shape[1:], lambda i, t: (far_side, 0, 0, 0))
    own = pl.BlockSpec((tok, step), lambda i, t: (0, jnp.minimum(i, steps - 1)))
    other = pl.BlockSpec((tok, step), lambda i, t: (0, jnp.maximum(i - steps, 0)))
    return pl.pallas_call(
        functools.partial(quad_weight_kernel, len(after)),
        grid_spec=pltpu.PrefetchScalarGridSpec(
            num_scalar_prefetch=1,
            grid=(2 * steps,),
            in_specs=[whole, pl.BlockSpec(b.shape, lambda i, t: (0, 0, 0, 0))] + [own, other] * 4 + [ANY] * len(after),
            out_specs=[
                pl.BlockSpec((head, step), lambda i, t: (0, (i + t[0] * steps) % (2 * steps)))
            ]
            * half,
            scratch_shapes=[
                pltpu.VMEM((half * head, 4 * tok), BF),
                pltpu.VMEM((4 * tok, step), BF),
            ],
        ),
        out_shape=[jax.ShapeDtypeStruct((head, 2 * feat), BF)] * half,
        compiler_params=params(),
        cost_estimate=cost(2e10 if far_side else NEAR, 0),
        name="quad_weight",
    )(tp, a, b, *cots, *after)


def pair_query_kernel(head, me_ref, after_ref, so_far_ref, g_ref, v_ref, k_ref, s_ref, kv_ref, t_ref, o_ref):
    core = me_ref[0] % 2
    half = g_ref.shape[0] // 2
    for j in range(g_ref.shape[1] // head):
        at, row = slice(j * head, (j + 1) * head), slice(j // 2 * head, (j // 2 + 1) * head)
        g = g_ref[:, at]
        near = s_ref[row, :].astype(F32) + core.astype(F32) * kv_ref[row, :].astype(F32)
        state = jnp.where(core == j % 2, near.astype(BF), t_ref[row, :])
        first_half, second_half = causal_apply(g, v_ref[:, at], k_ref[:, at], False)
        over = dot(g, state, 1, 1)
        o_ref[:half, at] = (first_half + over[:half]).astype(BF)
        o_ref[half:, at] = (second_half + over[half:]).astype(BF)


def pair_query_grad(me, part, after, so_far, g, v, k, state, kv, other, head):
    tok, width = g.shape
    step = min(4 * head, width // 2)
    first = max(1, width // step // 4)
    steps = width // step - first if part else first
    spec = pl.BlockSpec((tok, step), lambda i, m: (0, i + part * first))
    rows = pl.BlockSpec((step // 2, head), lambda i, m: (i + part * first, 0))
    return pl.pallas_call(
        functools.partial(pair_query_kernel, head),
        grid_spec=pltpu.PrefetchScalarGridSpec(
            num_scalar_prefetch=1,
            grid=(steps,),
            in_specs=[ANY, ANY, spec, spec, spec, rows, rows, rows],
            out_specs=spec,
        ),
        out_shape=jax.ShapeDtypeStruct((tok, width), BF),
        input_output_aliases={2: 0} if part else {},
        compiler_params=params(),
        cost_estimate=cost(0, 0),
        name="query_grad",
    )(me, after, so_far, g, v, k, state, kv, other)


def pair_grad_kernel(head, waits, me_ref, tp_ref, own_ref, far_ref, w_ref, q_ref, *refs):
    g_ref, mine_ref, send_ref = refs[waits : waits + 3]
    cot_ref = refs[-1]
    feat = own_ref.shape[1]

    @pl.when(pl.program_id(0) == 0)
    def _():
        cot_ref[:, lanes(tp_ref[0], feat)] = own_ref[...]
        cot_ref[:, lanes(1 - tp_ref[0], feat)] = far_ref[...]

    core = me_ref[0] % 2
    g_ref[...] = dot(cot_ref[...], w_ref[...], 1, 1).astype(BF)
    for j in range(g_ref.shape[1] // (2 * head)):
        at = slice(j * head, (j + 1) * head)
        for o_ref, side in ((send_ref, 1 - core), (mine_ref, core)):
            pick = lanes(2 * j + side, head)
            o_ref[at, :] = dot(q_ref[:, pick], g_ref[:, pick], 0, 0).astype(BF)


def pair_grad(me, tp, after, own, far, w, q, head):
    tok, feat = own.shape
    width = q.shape[1]
    step = min(4 * head, width)
    whole = pl.BlockSpec((tok, feat), lambda i, m, t: (0, 0))
    rows = pl.BlockSpec((step // 2, head), lambda i, m, t: (i, 0))
    cols = pl.BlockSpec((tok, step), lambda i, m, t: (0, i))
    sums = jax.ShapeDtypeStruct((width // 2, head), BF)
    return pl.pallas_call(
        functools.partial(pair_grad_kernel, head, len(after)),
        grid_spec=pltpu.PrefetchScalarGridSpec(
            num_scalar_prefetch=2,
            grid=(width // step,),
            in_specs=[
                whole,
                whole,
                pl.BlockSpec((step, 2 * feat), lambda i, m, t: (i, 0)),
                cols,
            ]
            + [ANY] * len(after),
            out_specs=[cols, rows, rows],
            scratch_shapes=[pltpu.VMEM((tok, 2 * feat), BF)],
        ),
        out_shape=[jax.ShapeDtypeStruct((tok, width), BF), sums, sums],
        compiler_params=params(),
        cost_estimate=cost(4 * tok * feat * width, 4 * feat * width + 4 * tok * width),
        name="out_grad",
    )(me, tp, own, far, w, q, *after)


def pass_kernel(*refs):
    pass


def passed_after(x, after, flops):
    return pl.pallas_call(
        pass_kernel,
        in_specs=[ANY] * (1 + len(after)),
        out_specs=ANY,
        out_shape=jax.ShapeDtypeStruct(x.shape, x.dtype),
        input_output_aliases={0: 0},
        compiler_params=params(),
        cost_estimate=cost(flops, 0),
        name="passed_after",
    )(x, *after)


def add_kernel(after_ref, a_ref, b_ref, o_ref):
    o_ref[...] = (a_ref[...].astype(F32) + b_ref[...].astype(F32)).astype(BF)


def add_after(after, a, b):
    spec = pl.BlockSpec(a.shape, lambda: (0, 0))
    return pl.pallas_call(
        add_kernel,
        in_specs=[ANY, spec, spec],
        out_specs=spec,
        out_shape=jax.ShapeDtypeStruct(a.shape, BF),
        compiler_params=params(),
        cost_estimate=cost(0, 0),
        name="add_after",
    )(after, a, b)


def pair_key_value_kernel(head, me_ref, after_ref, q_ref, k_ref, v_ref, g_ref, s_ref, qd_ref, t_ref, ko_ref, vo_ref):
    core = me_ref[0] % 2
    half = g_ref.shape[0] // 2
    for j in range(g_ref.shape[1] // head):
        at, row = slice(j * head, (j + 1) * head), slice(j // 2 * head, (j // 2 + 1) * head)
        near = s_ref[row, :].astype(F32) + (1 - core).astype(F32) * qd_ref[row, :].astype(F32)
        q, k, v, g = q_ref[:, at], k_ref[:, at], v_ref[:, at], g_ref[:, at]
        adj = jnp.where(core == j % 2, near.astype(BF), t_ref[row, :])
        first, second = causal_apply(v, g, q, True)
        over = dot(v, adj, 1, 1)
        ko_ref[:half, at] = (first + over[:half]).astype(BF)
        ko_ref[half:, at] = (second + over[half:]).astype(BF)
        first, second = causal_apply(k, q, g, True)
        over = dot(k, adj, 1, 0)
        vo_ref[:half, at] = (first + over[:half]).astype(BF)
        vo_ref[half:, at] = (second + over[half:]).astype(BF)


def pair_key_value_grad(me, after, q, k, v, g, adjoint, qd, other, head):
    tok, width = g.shape
    step = min(4 * head, width)
    spec = pl.BlockSpec((tok, step), lambda i, m: (0, i))
    rows = pl.BlockSpec((step // 2, head), lambda i, m: (i, 0))
    shape = jax.ShapeDtypeStruct((tok, width), BF)
    return pl.pallas_call(
        functools.partial(pair_key_value_kernel, head),
        grid_spec=pltpu.PrefetchScalarGridSpec(
            num_scalar_prefetch=1,
            grid=(width // step,),
            in_specs=[ANY, spec, spec, spec, spec, rows, rows, rows],
            out_specs=[spec, spec],
        ),
        out_shape=[shape, shape],
        compiler_params=params(),
        cost_estimate=cost(0, 0),
        name="key_value_grad",
    )(me, after, q, k, v, g, adjoint, qd, other)


def local_paired(queries, keys, values, cotangent, out_weight, memory):
    head = memory.shape[2]
    n = lax.axis_size("ctx")
    me, tp = lax.axis_index("ctx"), lax.axis_index("tp")
    who, which = me.reshape(1), tp.reshape(1)
    core = (me % 2).astype(F32)
    groups = [[c for c in range(n) if c % 2 == side] for side in range(2)]

    def swap(x, bit):
        return lax.ppermute(x, "ctx", [(c, c ^ bit) for c in range(n)])

    def swap_tp(x):
        return lax.ppermute(x, "tp", [(0, 1), (1, 0)])

    def across(x):
        return lax.all_to_all(x, "ctx", 0, 0, axis_index_groups=groups, tiled=True)

    def added(x, factor, y):
        return (x.astype(F32) + factor * y.astype(F32)).astype(BF)

    kv_mine, kv_send = pair_sums(who, keys, values, head)
    kv_other = swap(kv_send, 1)
    far = swap_tp(cotangent)
    south = swap(cotangent, 2)
    chip = added(kv_mine, 1.0, kv_other)
    inner, sent = pair_intra(who, (chip,), queries, keys, values, head)
    start = lax.dynamic_index_in_dim(memory, me, 0, False)
    scanned, sent = scan_blocks(across(chip), start, n // 2, False, (inner, far, south), sent)
    state = across(scanned)

    far_south = swap_tp(south)
    grad, qd_mine, qd_send = pair_grad(
        who, which, (scanned, south), cotangent, far, out_weight, queries, head
    )
    mine, send, send_near, away = pair_attended(
        who, grad, queries, inner, swap(sent, 1), state, kv_mine, kv_other, head
    )
    received, received_near = swap(send, 2), swap(send_near, 2)
    state_other = swap(away, 1)

    qd_other = swap(qd_send, 1)
    chip = add_after(send, qd_mine, qd_other)
    cots = [cotangent, far, swap(cotangent, 1), swap(far, 1)]
    cots += [south, far_south, swap(south, 1), swap(far_south, 1)]

    query_args = (grad, values, keys, state, kv_other, state_other, head)
    query_g = pair_query_grad(who, 0, chip, grad, *query_args)
    received = passed_after(received, (query_g,), 2e10)
    crossing = quad_weight(which, (), mine, received, cots, 1)
    summed = added(crossing[0], 1.0, swap(crossing[1], 4))
    crossed = swap(summed, 8)
    scanned = scan_blocks(across(chip), None, n // 2, True, (crossing[0],))
    after_chip = across(scanned)
    same = quad_weight(which, (scanned,), mine, received_near, cots, 0)
    neighbour = swap(same[1], 4)
    query_g = pair_query_grad(who, 1, summed, query_g, *query_args)
    after_chip = passed_after(after_chip, (query_g,), 0)
    adjoint_other = swap(added(after_chip, core, qd_mine), 1)
    key_g, value_g = pair_key_value_grad(
        who, query_g, queries, keys, values, grad, after_chip, qd_other, adjoint_other, head
    )
    total = same[0].astype(F32) + neighbour.astype(F32) + crossed.astype(F32)
    return query_g, key_g, value_g, total


def local_any(queries, keys, values, cotangent, out_weight, memory):
    head = memory.shape[2]
    width = queries.shape[1]
    feat = cotangent.shape[1]
    n = lax.axis_size("ctx")
    rows = width // n
    me, tp = lax.axis_index("ctx"), lax.axis_index("tp")

    far = lax.ppermute(cotangent, "tp", [(0, 1), (1, 0)])
    kv = block_sums(keys, values, head)
    start = lax.dynamic_slice_in_dim(memory.reshape(width, head), me * rows, rows, 0)
    state = carried(kv, start, "ctx", False)
    inner = intra(queries, keys, values, head)
    grad, qd = out_grad_and_sums(tp.reshape(1), cotangent, far, out_weight, queries, head)
    adjoint = carried(qd, None, "ctx", True)
    attended = attended_of(queries, state, inner, head)
    term = weight_term(attended, cotangent, far)
    total = lax.psum_scatter(term, "ctx", scatter_dimension=0, tiled=True)
    query_g = query_grad_of(grad, values, keys, state, head)
    key_g, value_g = key_value_grad_of(queries, keys, values, grad, adjoint, head)
    total = total.astype(F32)
    total = jnp.where(tp == 0, total, jnp.concatenate([total[:, feat:], total[:, :feat]], 1))
    return query_g, key_g, value_g, total


def local(*args):
    heads = args[5].shape[0]
    n = lax.axis_size("ctx")
    if n == heads == 16 and lax.axis_size("tp") == 2:
        return local_paired(*args)
    return local_any(*args)


def solution(mesh):
    in_specs = (
        P("ctx", "tp"),
        P("ctx", "tp"),
        P("ctx", "tp"),
        P("ctx", "tp"),
        P("tp", None),
        P("tp", None, None),
    )
    out_specs = (P("ctx", "tp"), P("ctx", "tp"), P("ctx", "tp"), P(("tp", "ctx"), None))
    return jax.shard_map(local, mesh=mesh, in_specs=in_specs, out_specs=out_specs, check_vma=False)
```
